32 devices in a mesh: ens: 2 (over y), tile: 4 (over z), chan: 2 (over x), sec: 2 (over core).
Axes of the slice: x: 2, y: 2, z: 4, core: 2. Of those that a mesh axis runs over, the one named last changes fastest.
Arguments:
- ocean_state: bfloat16 [256, 128, 4, 128], P(('chan', 'sec'), ('ens', 'tile')), parts along dimension 1, may hold values from -6 to 6
- atmos: bfloat16 [16384, 384], P(('ens', 'tile')), parts along dimension 0, may hold values from -6 to 6
- flux_weight: bfloat16 [384, 256], P(None, ('chan', 'sec')), may hold values from -0.3125 to 0.3125
- conv_weight: bfloat16 [9, 256, 256], P(None, None, ('chan', 'sec')), may hold values from -0.125 to 0.125
- conv_bias: bfloat16 [256], P(('chan', 'sec')), may hold values from -3 to 3
- norm_gain: bfloat16 [256], P(('chan', 'sec')), may hold values from 0.5 to 2
- in_weight: bfloat16 [256, 1024], P(None, ('chan', 'sec')), may hold values from -0.375 to 0.375
- in_bias: bfloat16 [1024], P(('chan', 'sec')), may hold values from -3 to 3
- out_weight: bfloat16 [1024, 256], P(('chan', 'sec')), may hold values from -0.25 to 0.25
- layer_scale: bfloat16 [256], P(('chan', 'sec')), may hold values from 0.5 to 2
- cell_mask: int32 [64, 4, 128], P('tile'), may hold values from 0 to 1, as said below
- neighbours: int32 [64, 8], P('tile'), may hold values from -1 to 63, as said below
- remap: int32 [64, 4, 128], P('tile'), may hold values from 0 to 8191
Outputs:
- ocean_next: bfloat16 [256, 128, 4, 128], P(('chan', 'sec'), ('ens', 'tile')), parts along dimension 1
The draws below stay inside these ranges and needn't reach their ends.
There are 2 independent parts, one for each index of `ens`. The reference program is written for one: setup_inputs(seed, part) draws one part's arguments, and reference() takes and returns one part's arrays. A program takes and returns all parts, laid end to end along the dimension named above; an argument that names none is the same for every part. Nothing has to cross between parts.
Inputs may be any that keep to these rules, and one draw needn't show every extreme that they name: `cell_mask`: land cells and every cell of a land block are 0. `neighbours`: for a slot among those of tile index t, each entry is -1 or a slot among those of tile indices t - 1, t and t + 1, i.e. in [(t - 1) * 16, (t + 2) * 16); entries that name land blocks are -1.
All inputs are finite; a program needn't handle non-finite values.
Results may differ from the reference program's by a relative error of at most 0.01.
Values may be sent and summed in bfloat16 or wider, within the bound.
No kernel may reach another device: no remote copies, remote signals or barrier semaphores. Data moves between devices by JAX's collectives and lax.ppermute only.
A program may use at most 64 MiB of HBM per device.

```python
import math
import jax
import jax.numpy as jnp
from jax import lax

C = 256
HID = 1024
FA = 384
NB = 16
BH = 4
BW = 128
SLOTS = 64
ATM_ROWS = 8192
N_CHAN = 2
N_SEC = 2


def geography(key):
    device_count = SLOTS // NB
    key_order, key_land = jax.random.split(jax.random.fold_in(key, 7))
    scores = jax.random.randint(key_order, (device_count, NB), 0, 1 << 20) * NB + jnp.arange(NB, dtype=jnp.int32)[None, :]
    order = jnp.argsort(scores, axis=1).astype(jnp.int32)
    slot_of = jnp.argsort(order, axis=1).astype(jnp.int32)
    land = jax.random.randint(key_land, (device_count, NB), 0, 4) == 0
    return (order, slot_of, land)


def draw_neighbours(key, part):
    order, slot_of, land = geography(key)
    device_count = SLOTS // NB
    device_ids = jnp.zeros((device_count, NB), jnp.int32) + jnp.arange(device_count, dtype=jnp.int32)[:, None]
    block_row = device_ids
    block_col = order
    moves = [(0, -1), (0, 1), (-1, 0), (1, 0), (-1, -1), (-1, 1), (1, -1), (1, 1)]
    listed = []
    for move_row, move_col in moves:
        row_to = block_row + move_row
        col_to = block_col + move_col
        inside = (row_to >= 0) & (row_to < device_count) & (col_to >= 0) & (col_to < NB)
        col_safe = jnp.clip(col_to, 0, NB - 1)
        row_safe = jnp.clip(row_to, 0, device_count - 1)
        owner = row_safe
        local_block = col_safe
        target = owner * NB + slot_of[owner, local_block]
        live = inside & jnp.logical_not(land[owner, local_block])
        listed.append(jnp.where(live, target, -1))
    return jnp.stack(listed, axis=-1).reshape(SLOTS, 8).astype(jnp.int32)


def draw_cell_mask(key, part):
    order, slot_of, land = geography(key)
    land_slot = jnp.take_along_axis(land, order, axis=1).reshape(SLOTS)
    wet = jax.random.randint(jax.random.fold_in(key, 11), (SLOTS, BH, BW), 0, 8) != 0
    return (wet & jnp.logical_not(land_slot)[:, None, None]).astype(jnp.int32)


def set_ends(array, rng, smallest, top_value):
    longest = array.shape.index(max(array.shape))
    spots = []
    for shift in (0, 1):
        where = [jax.random.randint(jax.random.fold_in(rng, axis), (), 0, length) for axis, length in enumerate(array.shape)]
        where[longest] = (where[longest] + shift) % array.shape[longest]
        spots.append(tuple(where))
    return array.at[spots[0]].set(smallest).at[spots[1]].set(top_value)


def with_spikes(result, key, source, target, parts, factor):
    def block_of(dim):
        return (jnp.arange(result.shape[dim]) // (result.shape[dim] // parts)).reshape((-1,) + (1,) * (result.ndim - 1 - dim))

    first = jax.random.permutation(key, parts)[block_of(target)]
    far = (block_of(target) + parts // 2) % parts
    return jnp.where((block_of(source) == first) | (block_of(source) == far), factor * result, result)


def shard_levels(stream_key, shape, pieces, smallest, top_value):
    def one(position, blocks):
        draws = jax.random.uniform(jax.random.fold_in(jax.random.fold_in(stream_key, 6), position), (blocks,), jnp.float32, smallest / len(pieces), top_value / len(pieces))
        return jnp.repeat(jnp.exp(draws), shape[position] // blocks).reshape((-1,) + (1,) * (len(shape) - position - 1))

    loudness = one(*pieces[0])
    for cut in pieces[1:]:
        loudness = loudness * one(*cut)
    return loudness


def noise(rng, extent, deviation, bound, shards=(), held_as=jnp.bfloat16):
    entries = deviation * jax.random.normal(rng, extent, jnp.float32)
    if shards:
        entries = entries * shard_levels(rng, extent, shards, -0.22, 0.18)
    return jnp.clip(entries, -bound, bound).astype(held_as)


def gaussian_with(key, shape, deviation, most, pieces, heavy, held_as=jnp.bfloat16):
    drawn = deviation * jax.random.normal(key, shape, jnp.float32)
    if pieces:
        drawn = drawn * shard_levels(key, shape, pieces, -0.22, 0.18)
    return jnp.clip(with_spikes(drawn, jax.random.fold_in(key, 3), *heavy), -most, most).astype(held_as)


def setup_inputs(seed: int = 0, part: int = 0) -> dict:
    key_list = jax.random.split(jax.random.key(seed), 14)
    part_keys = jax.random.split(jax.random.fold_in(key_list[13], part), 14)
    return {
        "ocean_state": noise(part_keys[0], (C, SLOTS, BH, BW), 1.0, 6.0, ((0, 4), (1, 4))),
        "atmos": noise(part_keys[1], (ATM_ROWS, FA), 1.0, 6.0, ((0, 4),)),
        "flux_weight": noise(key_list[2], (FA, C), FA ** -0.5, 0.3125, ((1, 4),)),
        "conv_weight": noise(key_list[3], (9, C, C), (9 * C) ** -0.5, 0.125, ((2, 4),)),
        "conv_bias": noise(key_list[4], (C,), 0.5, 3.0, ((0, 4),)),
        "norm_gain": jnp.clip(jnp.exp(math.log(2.0) - 1.3862944 * jax.random.uniform(key_list[5], (C,), jnp.float32) ** shard_levels(key_list[5], (C,), ((0, 4),), -0.2, 0.2)), 0.5, 2.0).astype(jnp.bfloat16),
        "in_weight": noise(key_list[6], (C, HID), C ** -0.5, 0.375, ((1, 4),)),
        "in_bias": noise(key_list[7], (HID,), 0.5, 3.0, ((0, 4),)),
        "out_weight": gaussian_with(key_list[8], (HID, C), HID ** -0.5, 0.25, ((0, 4),), (0, 1, 4, 2.0)),
        "layer_scale": jnp.clip(jnp.exp(math.log(2.0) - 1.3862944 * jax.random.uniform(key_list[9], (C,), jnp.float32) ** shard_levels(key_list[9], (C,), ((0, 4),), -0.2, 0.2)), 0.5, 2.0).astype(jnp.bfloat16),
        "cell_mask": draw_cell_mask(jax.random.fold_in(key_list[13], 71), part),
        "neighbours": draw_neighbours(jax.random.fold_in(key_list[13], 71), part),
        "remap": set_ends(jax.random.randint(key_list[12], (SLOTS, BH, BW), 0, ATM_ROWS), jax.random.fold_in(key_list[12], 1), 0, ATM_ROWS - 1).astype(jnp.int32),
    }


norm_eps = 1e-06

def strips_of(state):
    return jnp.concatenate([state[:, :, 0, :], state[:, :, -1, :], state[:, :, :, 0], state[:, :, :, -1], state[:, :, 0, 0:1], state[:, :, 0, -1:], state[:, :, -1, 0:1], state[:, :, -1, -1:]], axis=2)

def pad_blocks(state, strips, slot_index, valid):
    channels, slot_count, block_rows, block_cols = state.shape
    width = strips.shape[2]
    picked = jnp.take(strips, slot_index.reshape(-1), axis=1).reshape(channels, slot_count, 8, width)
    picked = jnp.where(valid[None, :, :, None], picked, jnp.zeros_like(picked))
    offset_base = 2 * block_cols + 2 * block_rows
    west_col = picked[:, :, 0, 2 * block_cols + block_rows:offset_base]
    east_col = picked[:, :, 1, 2 * block_cols:2 * block_cols + block_rows]
    prev_row = picked[:, :, 2, block_cols:2 * block_cols]
    next_row = picked[:, :, 3, 0:block_cols]
    top_row = jnp.concatenate([picked[:, :, 4, offset_base + 3:offset_base + 4], prev_row, picked[:, :, 5, offset_base + 2:offset_base + 3]], axis=2)
    bottom_row = jnp.concatenate([picked[:, :, 6, offset_base + 1:offset_base + 2], next_row, picked[:, :, 7, offset_base:offset_base + 1]], axis=2)
    middle = jnp.concatenate([west_col[:, :, :, None], state, east_col[:, :, :, None]], axis=3)
    return jnp.concatenate([top_row[:, :, None, :], middle, bottom_row[:, :, None, :]], axis=2)

def conv_taps(padded, kernel, block_rows, block_cols):
    padded = padded.astype(jnp.float32)
    kernel = kernel.astype(jnp.float32)
    total = jnp.zeros((kernel.shape[2], padded.shape[1], block_rows, block_cols), jnp.float32)
    for tap in range(9):
        tap_row = tap // 3
        tap_col = tap % 3
        window = padded[:, :, tap_row:tap_row + block_rows, tap_col:tap_col + block_cols]
        total = total + jnp.einsum('cskl,co->oskl', window, kernel[tap])
    return total

def reference(ocean_state, atmos, flux_weight, conv_weight, conv_bias, norm_gain, in_weight, in_bias, out_weight, layer_scale, cell_mask, neighbours, remap):
    valid = neighbours >= 0
    slot_index = jnp.clip(neighbours, 0, SLOTS - 1).astype(jnp.int32)
    padded = pad_blocks(ocean_state, strips_of(ocean_state), slot_index, valid)
    conv_out = conv_taps(padded, conv_weight, BH, BW) + conv_bias.astype(jnp.float32)[:, None, None, None]
    squares = lax.optimization_barrier(jnp.sum(conv_out * conv_out, axis=0))
    normed = (conv_out * lax.rsqrt(squares / C + norm_eps) * norm_gain.astype(jnp.float32)[:, None, None, None]).astype(jnp.bfloat16)
    pre = jnp.einsum('csij,ch->hsij', normed.astype(jnp.float32), in_weight.astype(jnp.float32))
    hidden = jax.nn.gelu(pre + in_bias.astype(jnp.float32)[:, None, None, None], approximate=False).astype(jnp.bfloat16)
    groups = N_CHAN * N_SEC
    hid_groups = hidden.reshape(groups, HID // groups, SLOTS, BH, BW)
    out_groups = out_weight.reshape(groups, HID // groups, C)

    def add_group(total, pair):
        term = jnp.einsum('hsij,hc->csij', pair[0].astype(jnp.float32), pair[1].astype(jnp.float32)).astype(jnp.bfloat16)
        term = lax.optimization_barrier(term)
        return (total + term.astype(jnp.float32), None)
    update, _ = lax.scan(add_group, jnp.zeros((C, SLOTS, BH, BW), jnp.float32), (hid_groups, out_groups))
    fluxes = jnp.dot(atmos, flux_weight, preferred_element_type=jnp.float32).astype(jnp.bfloat16)
    forcing = jnp.take(fluxes, remap.reshape(-1).astype(jnp.int32), axis=0).T.reshape(C, SLOTS, BH, BW)
    total = ocean_state.astype(jnp.float32) + layer_scale.astype(jnp.float32)[:, None, None, None] * update + forcing.astype(jnp.float32)
    return (cell_mask.astype(jnp.float32)[None] * total).astype(jnp.bfloat16)
```

```python
import functools

import jax
import jax.numpy as jnp
from jax import lax
from jax.experimental import pallas as pl
from jax.experimental.pallas import tpu as pltpu
from jax.sharding import PartitionSpec as P

norm_eps = 1e-06
bf16 = jnp.bfloat16
f32 = jnp.float32
GROUP = ("chan", "sec")
BIAS_ROWS = 32
VMEM = pl.BlockSpec(memory_space=pltpu.VMEM)
SMEM = pl.BlockSpec(memory_space=pltpu.SMEM)


def shape(dims, dtype=bf16):
    return jax.ShapeDtypeStruct(dims, dtype)


def params(mib=48):
    return pltpu.CompilerParams(vmem_limit_bytes=mib * 1024 * 1024)


def ein(a, b, dims):
    return lax.dot_general(a, b, (dims, ((), ())), preferred_element_type=f32)


def prep_kernel(state_ref, xt_ref, strips_ref):
    chan_local, slot_count, block_rows, block_cols = state_ref.shape
    lane = lax.broadcasted_iota(jnp.int32, (chan_local, block_cols), 1)
    cols = jnp.zeros((chan_local, block_cols), f32)
    for s in range(slot_count):
        rows = jnp.swapaxes(state_ref[:, s].astype(f32), 0, 1)
        packed = rows.astype(bf16)
        xt_ref[s] = packed
        strips_ref[2 * s] = packed[0]
        strips_ref[2 * s + 1] = packed[block_rows - 1]
        for r in range(block_rows):
            at = 2 * (block_rows * s + r)
            turned = pltpu.roll(rows[r], at + 1, 1)
            cols = jnp.where((lane == at) | (lane == at + 1), turned, cols)
    strips_ref[2 * slot_count] = cols.astype(bf16)


def prep(state):
    chan_local, slot_count, block_rows, block_cols = state.shape
    return pl.pallas_call(
        prep_kernel,
        out_shape=(
            shape((slot_count, block_rows, chan_local, block_cols)),
            shape((2 * slot_count + 1, chan_local, block_cols)),
        ),
        in_specs=[VMEM],
        out_specs=(VMEM, VMEM),
        compiler_params=params(),
        name="prep_state",
    )(state)


def pack_kernel(conv_ref, bias_ref, gain_ref, in_ref, in_bias_ref, out_ref, pack_ref):
    taps, chan_local, channels = conv_ref.shape
    hid_local = out_ref.shape[0]
    for t in range(taps):
        pack_ref[pl.ds(t * chan_local, chan_local), :] = conv_ref[t]
    at = taps * chan_local
    pack_ref[pl.ds(at, hid_local), :] = in_ref[...].astype(f32).T.astype(bf16)
    pack_ref[pl.ds(at + hid_local, hid_local), :] = out_ref[...]

    def widen(row):
        row = row.astype(f32)
        if row.shape[1] == channels:
            return row
        return jnp.concatenate([row, jnp.zeros((1, channels - row.shape[1]), f32)], axis=1)

    rest = jnp.zeros((BIAS_ROWS - 3, channels), f32)
    biases = jnp.concatenate(
        [widen(bias_ref[...]), widen(gain_ref[...]), widen(in_bias_ref[...]), rest], axis=0
    )
    pack_ref[pl.ds(at + 2 * hid_local, BIAS_ROWS), :] = biases.astype(bf16)


def pack_weights(conv_weight, conv_bias, norm_gain, in_weight, in_bias, out_weight):
    taps, channels, chan_local = conv_weight.shape
    hid_local = out_weight.shape[0]
    return pl.pallas_call(
        pack_kernel,
        out_shape=shape((taps * chan_local + 2 * hid_local + BIAS_ROWS, channels)),
        in_specs=[VMEM] * 6,
        out_specs=VMEM,
        compiler_params=params(),
        name="pack_weights",
    )(
        conv_weight.transpose(0, 2, 1),
        conv_bias[None],
        norm_gain[None],
        in_weight,
        in_bias[None],
        out_weight,
    )


def unpack_kernel(chan_local, hid_local, all_ref, conv_ref, in_ref, out_ref, col_ref, hid_col_ref):
    groups, _, channels = all_ref.shape
    at = 9 * chan_local
    rows = []
    for j in range(groups):
        for t in range(9):
            conv_ref[pl.ds(j * chan_local, chan_local), pl.ds(t * channels, channels)] = all_ref[
                j, pl.ds(t * chan_local, chan_local), :
            ]
        in_ref[pl.ds(j * hid_local, hid_local), :] = all_ref[j, pl.ds(at, hid_local), :]
        biases = all_ref[j, pl.ds(at + 2 * hid_local, BIAS_ROWS), :].astype(f32)
        across = biases.T
        col_ref[pl.ds(j * chan_local, chan_local), :] = across[:chan_local]
        hid_col_ref[pl.ds(j * hid_local, hid_local), :] = across[:hid_local]
    outs = jnp.concatenate(
        [all_ref[j, pl.ds(at + hid_local, hid_local), :] for j in range(groups)], axis=0
    )
    out_ref[...] = outs.astype(f32).T.astype(bf16)


def unpack_weights(gathered, chan_local, hid_local):
    groups, _, channels = gathered.shape
    hidden = groups * hid_local
    return pl.pallas_call(
        functools.partial(unpack_kernel, chan_local, hid_local),
        out_shape=(
            shape((channels, 9 * channels)),
            shape((hidden, channels)),
            shape((channels, hidden)),
            shape((channels, BIAS_ROWS), f32),
            shape((hidden, BIAS_ROWS), f32),
        ),
        in_specs=[VMEM],
        out_specs=(VMEM,) * 5,
        compiler_params=params(),
        name="unpack_weights",
    )(gathered)


def flux_kernel(atmos_ref, weight_ref, out_ref):
    rows, lanes = out_ref.shape
    chan_local, features = weight_ref.shape
    weight = weight_ref[...]
    total = jnp.zeros((rows, lanes), f32)
    for k in range(lanes // chan_local):
        parts = [weight if j == k else jnp.zeros_like(weight) for j in range(lanes // chan_local)]
        wide = jnp.concatenate(parts, axis=0)
        total = total + ein(atmos_ref[pl.ds(k * rows, rows), :], wide, ((1,), (1,)))
    out_ref[...] = total.astype(bf16)


def fluxes_of(atmos, flux_weight):
    side = 128 // flux_weight.shape[1]
    return pl.pallas_call(
        flux_kernel,
        out_shape=shape((atmos.shape[0] // side, 128)),
        in_specs=[VMEM, VMEM],
        out_specs=VMEM,
        compiler_params=params(),
        name="fluxes",
    )(atmos, flux_weight.T)


def rim_kernel(entry_ref, at_ref, prev_ref, own_ref, next_ref, rim_ref, held):
    tiles, chan_local, block_cols = own_ref.shape
    groups = rim_ref.shape[0]
    slot_count = (tiles - 1) // 2
    per = slot_count // groups
    held[pl.ds(0, tiles)] = prev_ref[...]
    held[pl.ds(tiles, tiles)] = own_ref[...]
    held[pl.ds(2 * tiles, tiles)] = next_ref[...]
    held[3 * tiles] = jnp.zeros((chan_local, block_cols), bf16)
    ends = jnp.concatenate(
        [prev_ref[tiles - 1], own_ref[tiles - 1], next_ref[tiles - 1]], axis=1
    )
    spot = lax.broadcasted_iota(jnp.int32, (3 * block_cols, block_cols), 0)
    for d in range(groups):
        for s in range(per):
            rim_ref[d, 2 * s] = held[entry_ref[0, d * per + s]]
            rim_ref[d, 2 * s + 1] = held[entry_ref[1, d * per + s]]
        chosen = (spot == at_ref[pl.ds(d, 1), :]).astype(f32).astype(bf16)
        rim_ref[d, 2 * per] = ein(ends, chosen, ((1,), (0,))).astype(bf16)


def rims_of(strips_prev, strips, strips_next, neighbours, first_slot, groups):
    tiles, chan_local, block_cols = strips.shape
    slot_count = (tiles - 1) // 2
    per = slot_count // groups
    block_rows = block_cols // (2 * slot_count)
    valid = neighbours >= 0
    slot = jnp.clip(neighbours - first_slot, 0, 3 * slot_count - 1)
    tile_of = slot // slot_count
    place = tile_of * tiles + 2 * (slot - tile_of * slot_count)
    entries = jnp.stack(
        [
            jnp.where(valid[:, 2], place[:, 2] + 1, 3 * tiles),
            jnp.where(valid[:, 3], place[:, 3], 3 * tiles),
        ]
    )
    base = jnp.where(valid, 2 * block_rows * slot, -2 * block_rows * 2)
    last = 2 * (block_rows - 1)
    west = [base[:, 4] + last] + [base[:, 0] + 2 * r for r in range(block_rows)] + [base[:, 6]]
    east = [base[:, 5] + last] + [base[:, 1] + 2 * r for r in range(block_rows)] + [base[:, 7]]
    none = [jnp.full((slot_count,), -1, jnp.int32)] * (8 - block_rows - 2)
    at = jnp.stack(west + none + [e + 1 for e in east] + none, axis=1)
    at = at.reshape(groups, per * 16)
    at = jnp.pad(at, ((0, 0), (0, block_cols - per * 16)), constant_values=-1)
    return pl.pallas_call(
        rim_kernel,
        out_shape=shape((groups, 2 * per + 1, chan_local, block_cols)),
        in_specs=[SMEM, VMEM, VMEM, VMEM, VMEM],
        out_specs=VMEM,
        scratch_shapes=[pltpu.VMEM((3 * tiles + 1, chan_local, block_cols), bf16)],
        compiler_params=params(),
        name="rims",
    )(entries, at, strips_prev, strips, strips_next)


def block_kernel(
    body_ref, rim_ref, conv_ref, in_ref, out_ref, col_ref, hid_col_ref, upd_ref, taken, hid
):
    groups, per, block_rows, chan_local, block_cols = body_ref.shape
    channels = groups * chan_local
    hidden = in_ref.shape[0]
    lane = lax.broadcasted_iota(jnp.int32, (chan_local, block_cols), 1)
    bias = col_ref[:, 0:1]
    gain = col_ref[:, 1:2]
    for s in range(per):
        for j in range(groups):
            ends = rim_ref[j, 2 * per].astype(f32)
            for p in range(block_rows + 2):
                if p == 0:
                    mid = rim_ref[j, 2 * s]
                elif p == block_rows + 1:
                    mid = rim_ref[j, 2 * s + 1]
                else:
                    mid = body_ref[j, s, p - 1]
                wide = mid.astype(f32)
                spot = 16 * s + p
                left = jnp.where(
                    lane == 0,
                    pltpu.roll(ends, (block_cols - spot) % block_cols, 1),
                    pltpu.roll(wide, 1, 1),
                ).astype(bf16)
                right = jnp.where(
                    lane == block_cols - 1,
                    pltpu.roll(ends, (2 * block_cols - 1 - spot - 8) % block_cols, 1),
                    pltpu.roll(wide, block_cols - 1, 1),
                ).astype(bf16)
                for a in range(3):
                    i = p - a
                    if 0 <= i < block_rows:
                        for b, piece in enumerate((left, mid, right)):
                            taken[
                                s % 2,
                                pl.ds((3 * a + b) * channels + j * chan_local, chan_local),
                                pl.ds(i * block_cols, block_cols),
                            ] = piece
        conv = ein(conv_ref[...], taken[s % 2], ((1,), (0,))) + bias
        squares = jnp.sum(conv * conv, axis=0, keepdims=True)
        normed = (conv * lax.rsqrt(squares / channels + norm_eps) * gain).astype(bf16)
        step = min(hidden, 256)
        for h in range(0, hidden, step):
            pre = ein(in_ref[pl.ds(h, step), :], normed, ((1,), (0,)))
            pre = pre + hid_col_ref[pl.ds(h, step), 2:3]
            act = pre * (0.5 * lax.erf(pre * (0.5**0.5)) + 0.5)
            hid[s % 2, pl.ds(h, step), :] = act.astype(bf16)
        upd = ein(out_ref[...], hid[s % 2], ((1,), (0,))).astype(bf16)
        for j in range(groups):
            for i in range(block_rows):
                upd_ref[j, s, i] = upd[
                    j * chan_local : (j + 1) * chan_local, i * block_cols : (i + 1) * block_cols
                ]


def block_step(body, rims, weights):
    groups, per, block_rows, chan_local, block_cols = body.shape
    channels = groups * chan_local
    hidden = weights[1].shape[0]
    cells = per * block_rows * block_cols
    return pl.pallas_call(
        block_kernel,
        out_shape=shape(body.shape),
        in_specs=[VMEM] * 7,
        out_specs=VMEM,
        scratch_shapes=[
            pltpu.VMEM((2, 9 * channels, block_rows * block_cols), bf16),
            pltpu.VMEM((2, hidden, block_rows * block_cols), bf16),
        ],
        compiler_params=params(),
        cost_estimate=pl.CostEstimate(
            flops=2 * cells * (9 * channels * channels + 2 * channels * hidden),
            bytes_accessed=8 * 1024 * 1024,
            transcendentals=0,
        ),
        name="block_step",
    )(body, rims, *weights)


def forcing_kernel(row_ref, side_ref, table_ref, out_ref, wide, got):
    slot_count, block_rows, chan_local, block_cols = out_ref.shape
    lanes = table_ref.shape[1]
    wide[...] = table_ref[...].astype(f32)

    def one(q, _):
        for k in range(block_cols):
            got[pl.ds(k, 1), :] = wide[pl.ds(row_ref[q, k], 1), :]
        across = got[...].T
        side = side_ref[pl.ds(q, 1), :]
        total = across[:chan_local]
        for k in range(1, lanes // chan_local):
            total = jnp.where(side == k, across[k * chan_local : (k + 1) * chan_local], total)
        out_ref[q // block_rows, q % block_rows] = total.astype(bf16)
        return 0

    lax.fori_loop(0, slot_count * block_rows, one, 0)


def forcing_of(table, remap, rows_local, chan_local):
    slot_count, block_rows, block_cols = remap.shape
    side_by = 128 // chan_local
    part = rows_local // side_by
    target = jnp.clip(remap, 0, table.shape[0] * side_by - 1).reshape(-1, block_cols)
    tile_of = target // rows_local
    within = target - tile_of * rows_local
    side = within // part
    row = tile_of * part + within - side * part
    return pl.pallas_call(
        forcing_kernel,
        out_shape=shape((slot_count, block_rows, chan_local, block_cols)),
        in_specs=[SMEM, VMEM, VMEM],
        out_specs=VMEM,
        scratch_shapes=[
            pltpu.VMEM(table.shape, f32),
            pltpu.VMEM((block_cols, table.shape[1]), f32),
        ],
        compiler_params=params(),
        cost_estimate=pl.CostEstimate(
            flops=0, bytes_accessed=32 * 1024 * 1024, transcendentals=0
        ),
        name="forcing",
    )(row, side, table)


def final_kernel(xt_ref, upd_ref, forcing_ref, mask_ref, scale_ref, out_ref):
    slot_count, block_rows, chan_local, block_cols = xt_ref.shape
    scale = scale_ref[...].astype(f32)
    for s in range(slot_count):
        total = xt_ref[s].astype(f32) + scale[None] * upd_ref[s].astype(f32)
        total = total + forcing_ref[s].astype(f32)
        total = mask_ref[s].astype(f32)[:, None, :] * total
        out_ref[:, s] = jnp.swapaxes(total, 0, 1).astype(bf16)


def final_step(xt, update, forcing, cell_mask, layer_scale):
    slot_count, block_rows, chan_local, block_cols = xt.shape
    return pl.pallas_call(
        final_kernel,
        out_shape=shape((chan_local, slot_count, block_rows, block_cols)),
        in_specs=[VMEM] * 5,
        out_specs=VMEM,
        compiler_params=params(),
        name="final_step",
    )(xt, update, forcing, cell_mask, layer_scale[:, None])


def on_device(
    ocean_state,
    atmos,
    flux_weight,
    conv_weight,
    conv_bias,
    norm_gain,
    in_weight,
    in_bias,
    out_weight,
    layer_scale,
    cell_mask,
    neighbours,
    remap,
):
    chan_local, slot_count, block_rows, block_cols = ocean_state.shape
    groups = lax.axis_size(GROUP)
    tile_count = lax.axis_size("tile")
    per = slot_count // groups
    hid_local = in_weight.shape[1]

    xt, strips = prep(ocean_state)
    up = [(i, i + 1) for i in range(tile_count - 1)]
    strips_prev = lax.ppermute(strips, "tile", up)
    strips_next = lax.ppermute(strips, "tile", [(b, a) for a, b in up])
    body = lax.all_to_all(
        xt.reshape(groups, per, block_rows, chan_local, block_cols), GROUP, 0, 0, tiled=True
    )
    packed = pack_weights(conv_weight, conv_bias, norm_gain, in_weight, in_bias, out_weight)
    gathered = lax.all_gather(packed, GROUP, axis=0)
    flux = fluxes_of(atmos, flux_weight)
    table = lax.all_gather(flux, "tile", axis=0, tiled=True)

    first_slot = (lax.axis_index("tile") - 1) * slot_count
    rims = rims_of(strips_prev, strips, strips_next, neighbours, first_slot, groups)
    rims = lax.all_to_all(rims, GROUP, 0, 0, tiled=True)
    weights = unpack_weights(gathered, chan_local, hid_local)
    update = block_step(body, rims, weights)
    update, table = lax.optimization_barrier((update, table))
    update = lax.all_to_all(update, GROUP, 0, 0, tiled=True)
    update = update.reshape(xt.shape)
    forcing = forcing_of(table, remap, atmos.shape[0], chan_local)
    return final_step(xt, update, forcing, cell_mask, layer_scale)


def solution(mesh):
    placed = (
        P(("chan", "sec"), ("ens", "tile"), None, None),
        P(("ens", "tile"), None),
        P(None, ("chan", "sec")),
        P(None, None, ("chan", "sec")),
        P(("chan", "sec")),
        P(("chan", "sec")),
        P(None, ("chan", "sec")),
        P(("chan", "sec")),
        P(("chan", "sec"), None),
        P(("chan", "sec")),
        P("tile", None, None),
        P("tile", None),
        P("tile", None, None),
    )
    return jax.shard_map(
        on_device,
        mesh=mesh,
        in_specs=placed,
        out_specs=P(("chan", "sec"), ("ens", "tile"), None, None),
        check_vma=False,
    )
```

```python
import functools

import jax
import jax.numpy as jnp
from jax import lax
from jax.experimental import pallas as pl
from jax.experimental.pallas import tpu as pltpu
from jax.sharding import PartitionSpec as P

norm_eps = 1e-06
bf16 = jnp.bfloat16
f32 = jnp.float32
GROUP = ("chan", "sec")
BIAS_ROWS = 32
VMEM = pl.BlockSpec(memory_space=pltpu.VMEM)
SMEM = pl.BlockSpec(memory_space=pltpu.SMEM)


def shape(dims, dtype=bf16):
    return jax.ShapeDtypeStruct(dims, dtype)


def params(mib=48):
    return pltpu.CompilerParams(vmem_limit_bytes=mib * 1024 * 1024)


def ein(a, b, dims):
    return lax.dot_general(a, b, (dims, ((), ())), preferred_element_type=f32)


def prep_kernel(state_ref, xt_ref, strips_ref):
    chan_local, slot_count, block_rows, block_cols = state_ref.shape
    lane = lax.broadcasted_iota(jnp.int32, (chan_local, block_cols), 1)
    cols = jnp.zeros((chan_local, block_cols), f32)
    for s in range(slot_count):
        rows = jnp.swapaxes(state_ref[:, s].astype(f32), 0, 1)
        packed = rows.astype(bf16)
        xt_ref[s] = packed
        strips_ref[2 * s] = packed[0]
        strips_ref[2 * s + 1] = packed[block_rows - 1]
        for r in range(block_rows):
            at = 2 * (block_rows * s + r)
            turned = pltpu.roll(rows[r], at + 1, 1)
            cols = jnp.where((lane == at) | (lane == at + 1), turned, cols)
    strips_ref[2 * slot_count] = cols.astype(bf16)


def prep(state):
    chan_local, slot_count, block_rows, block_cols = state.shape
    return pl.pallas_call(
        prep_kernel,
        out_shape=(
            shape((slot_count, block_rows, chan_local, block_cols)),
            shape((2 * slot_count + 1, chan_local, block_cols)),
        ),
        in_specs=[VMEM],
        out_specs=(VMEM, VMEM),
        compiler_params=params(),
        name="prep_state",
    )(state)


def pack_kernel(
    half_ref, conv_ref, bias_ref, gain_ref, in_ref, in_bias_ref, out_ref, pack_ref, part_ref
):
    taps, chan_local, channels = conv_ref.shape
    hid_local = out_ref.shape[0]
    for t in range(taps):
        pack_ref[pl.ds(t * chan_local, chan_local), :] = conv_ref[t]
    at = taps * chan_local
    pack_ref[pl.ds(at, hid_local), :] = in_ref[...].astype(f32).T.astype(bf16)
    pack_ref[pl.ds(at + hid_local, hid_local), :] = out_ref[...]

    def widen(row):
        row = row.astype(f32)
        if row.shape[1] == channels:
            return row
        return jnp.concatenate([row, jnp.zeros((1, channels - row.shape[1]), f32)], axis=1)

    rest = jnp.zeros((BIAS_ROWS - 3, channels), f32)
    biases = jnp.concatenate(
        [widen(bias_ref[...]), widen(gain_ref[...]), widen(in_bias_ref[...]), rest], axis=0
    )
    pack_ref[pl.ds(at + 2 * hid_local, BIAS_ROWS), :] = biases.astype(bf16)
    part = part_ref.shape[0]
    part_ref[...] = pack_ref[pl.ds(pl.multiple_of(half_ref[0] * part, 16), part), :]


def pack_weights(half, conv_weight, conv_bias, norm_gain, in_weight, in_bias, out_weight):
    taps, channels, chan_local = conv_weight.shape
    hid_local = out_weight.shape[0]
    rows = taps * chan_local + 2 * hid_local + BIAS_ROWS
    return pl.pallas_call(
        pack_kernel,
        out_shape=(shape((rows, channels)), shape((rows // 2, channels))),
        in_specs=[SMEM] + [VMEM] * 6,
        out_specs=(VMEM, VMEM),
        compiler_params=params(60),
        name="pack_weights",
    )(
        half[None],
        conv_weight.transpose(0, 2, 1),
        conv_bias[None],
        norm_gain[None],
        in_weight,
        in_bias[None],
        out_weight,
    )


def unpack_kernel(chan_local, hid_local, starts_ref, *refs):
    *pieces, conv_ref, in_ref, out_ref, col_ref, hid_col_ref, all_ref = refs
    groups, rows, channels = all_ref.shape
    unit = min(rows, *(piece.shape[0] for piece in pieces))
    for n, piece in enumerate(pieces):
        for k in range(piece.shape[0] // unit):
            at = starts_ref[n] + k
            parts = rows // unit
            start = pl.multiple_of((at % parts) * unit, 16)
            all_ref[at // parts, pl.ds(start, unit), :] = piece[pl.ds(k * unit, unit), :]
    at = 9 * chan_local
    for j in range(groups):
        for t in range(9):
            conv_ref[pl.ds(j * chan_local, chan_local), pl.ds(t * channels, channels)] = all_ref[
                j, pl.ds(t * chan_local, chan_local), :
            ]
        in_ref[pl.ds(j * hid_local, hid_local), :] = all_ref[j, pl.ds(at, hid_local), :]
        biases = all_ref[j, pl.ds(at + 2 * hid_local, BIAS_ROWS), :].astype(f32)
        across = biases.T
        col_ref[pl.ds(j * chan_local, chan_local), :] = across[:chan_local]
        hid_col_ref[pl.ds(j * hid_local, hid_local), :] = across[:hid_local]
    outs = jnp.concatenate(
        [all_ref[j, pl.ds(at + hid_local, hid_local), :] for j in range(groups)], axis=0
    )
    out_ref[...] = outs.astype(f32).T.astype(bf16)


def unpack_weights(pieces, starts, groups, chan_local, hid_local):
    rows = sum(piece.shape[0] for piece in pieces) // groups
    channels = groups * chan_local
    hidden = groups * hid_local
    return pl.pallas_call(
        functools.partial(unpack_kernel, chan_local, hid_local),
        out_shape=(
            shape((channels, 9 * channels)),
            shape((hidden, channels)),
            shape((channels, hidden)),
            shape((channels, BIAS_ROWS), f32),
            shape((hidden, BIAS_ROWS), f32),
        ),
        in_specs=[SMEM] + [VMEM] * len(pieces),
        out_specs=(VMEM,) * 5,
        scratch_shapes=[pltpu.VMEM((groups, rows, channels), bf16)],
        compiler_params=params(),
        name="unpack_weights",
    )(starts, *pieces)


def swap(value, axis):
    return lax.ppermute(value, axis, [(0, 1), (1, 0)])


def exchange_weights(packed, part):
    if lax.axis_size("ens") != 2 or lax.axis_size("chan") != 2 or lax.axis_size("sec") != 2:
        whole = lax.all_gather(packed, GROUP, axis=0, tiled=True)
        return [whole], jnp.zeros((1,), jnp.int32)
    ens, chan, sec = (lax.axis_index(name) for name in ("ens", "chan", "sec"))
    other = swap(packed, "sec")
    near = swap(part, "chan")
    far = swap(near, "ens")
    near_other = swap(near, "sec")
    far_other = swap(far, "sec")
    own = 2 * (2 * chan + sec)
    beside = 2 * (2 * chan + 1 - sec)
    across = 2 * (2 * (1 - chan) + sec)
    corner = 2 * (2 * (1 - chan) + 1 - sec)
    starts = [own, beside, across + ens, across + 1 - ens, corner + ens, corner + 1 - ens]
    return [packed, other, near, far, near_other, far_other], jnp.stack(starts)


def flux_kernel(atmos_ref, weight_ref, out_ref):
    rows, lanes = out_ref.shape
    chan_local, features = weight_ref.shape
    weight = weight_ref[...]
    total = jnp.zeros((rows, lanes), f32)
    for k in range(lanes // chan_local):
        parts = [weight if j == k else jnp.zeros_like(weight) for j in range(lanes // chan_local)]
        wide = jnp.concatenate(parts, axis=0)
        total = total + ein(atmos_ref[pl.ds(k * rows, rows), :], wide, ((1,), (1,)))
    out_ref[...] = total.astype(bf16)


def fluxes_of(atmos, flux_weight):
    side = 128 // flux_weight.shape[1]
    return pl.pallas_call(
        flux_kernel,
        out_shape=shape((atmos.shape[0] // side, 128)),
        in_specs=[VMEM, VMEM],
        out_specs=VMEM,
        compiler_params=params(),
        name="fluxes",
    )(atmos, flux_weight.T)


def rim_kernel(entry_ref, at_ref, prev_ref, own_ref, next_ref, rim_ref, held):
    tiles, chan_local, block_cols = own_ref.shape
    groups = rim_ref.shape[0]
    slot_count = (tiles - 1) // 2
    per = slot_count // groups
    held[pl.ds(0, tiles)] = prev_ref[...]
    held[pl.ds(tiles, tiles)] = own_ref[...]
    held[pl.ds(2 * tiles, tiles)] = next_ref[...]
    held[3 * tiles] = jnp.zeros((chan_local, block_cols), bf16)
    ends = jnp.concatenate(
        [prev_ref[tiles - 1], own_ref[tiles - 1], next_ref[tiles - 1]], axis=1
    )
    spot = lax.broadcasted_iota(jnp.int32, (3 * block_cols, block_cols), 0)
    for d in range(groups):
        for s in range(per):
            rim_ref[d, 2 * s] = held[entry_ref[0, d * per + s]]
            rim_ref[d, 2 * s + 1] = held[entry_ref[1, d * per + s]]
        chosen = (spot == at_ref[pl.ds(d, 1), :]).astype(f32).astype(bf16)
        rim_ref[d, 2 * per] = ein(ends, chosen, ((1,), (0,))).astype(bf16)


def rims_of(strips_prev, strips, strips_next, neighbours, first_slot, groups):
    tiles, chan_local, block_cols = strips.shape
    slot_count = (tiles - 1) // 2
    per = slot_count // groups
    block_rows = block_cols // (2 * slot_count)
    valid = neighbours >= 0
    slot = jnp.clip(neighbours - first_slot, 0, 3 * slot_count - 1)
    tile_of = slot // slot_count
    place = tile_of * tiles + 2 * (slot - tile_of * slot_count)
    entries = jnp.stack(
        [
            jnp.where(valid[:, 2], place[:, 2] + 1, 3 * tiles),
            jnp.where(valid[:, 3], place[:, 3], 3 * tiles),
        ]
    )
    base = jnp.where(valid, 2 * block_rows * slot, -2 * block_rows * 2)
    last = 2 * (block_rows - 1)
    west = [base[:, 4] + last] + [base[:, 0] + 2 * r for r in range(block_rows)] + [base[:, 6]]
    east = [base[:, 5] + last] + [base[:, 1] + 2 * r for r in range(block_rows)] + [base[:, 7]]
    none = [jnp.full((slot_count,), -1, jnp.int32)] * (8 - block_rows - 2)
    at = jnp.stack(west + none + [e + 1 for e in east] + none, axis=1)
    at = at.reshape(groups, per * 16)
    at = jnp.pad(at, ((0, 0), (0, block_cols - per * 16)), constant_values=-1)
    return pl.pallas_call(
        rim_kernel,
        out_shape=shape((groups, 2 * per + 1, chan_local, block_cols)),
        in_specs=[SMEM, VMEM, VMEM, VMEM, VMEM],
        out_specs=VMEM,
        scratch_shapes=[pltpu.VMEM((3 * tiles + 1, chan_local, block_cols), bf16)],
        compiler_params=params(),
        name="rims",
    )(entries, at, strips_prev, strips, strips_next)


def block_kernel(
    body_ref, rim_ref, conv_ref, in_ref, out_ref, col_ref, hid_col_ref, upd_ref, taken, hid
):
    groups, per, block_rows, chan_local, block_cols = body_ref.shape
    channels = groups * chan_local
    hidden = in_ref.shape[0]
    lane = lax.broadcasted_iota(jnp.int32, (chan_local, block_cols), 1)
    bias = col_ref[:, 0:1]
    gain = col_ref[:, 1:2]
    for s in range(per):
        for j in range(groups):
            ends = rim_ref[j, 2 * per].astype(f32)
            for p in range(block_rows + 2):
                if p == 0:
                    mid = rim_ref[j, 2 * s]
                elif p == block_rows + 1:
                    mid = rim_ref[j, 2 * s + 1]
                else:
                    mid = body_ref[j, s, p - 1]
                wide = mid.astype(f32)
                spot = 16 * s + p
                left = jnp.where(
                    lane == 0,
                    pltpu.roll(ends, (block_cols - spot) % block_cols, 1),
                    pltpu.roll(wide, 1, 1),
                ).astype(bf16)
                right = jnp.where(
                    lane == block_cols - 1,
                    pltpu.roll(ends, (2 * block_cols - 1 - spot - 8) % block_cols, 1),
                    pltpu.roll(wide, block_cols - 1, 1),
                ).astype(bf16)
                for a in range(3):
                    i = p - a
                    if 0 <= i < block_rows:
                        for b, piece in enumerate((left, mid, right)):
                            taken[
                                s % 2,
                                pl.ds((3 * a + b) * channels + j * chan_local, chan_local),
                                pl.ds(i * block_cols, block_cols),
                            ] = piece
        conv = ein(conv_ref[...], taken[s % 2], ((1,), (0,))) + bias
        squares = jnp.sum(conv * conv, axis=0, keepdims=True)
        normed = (conv * lax.rsqrt(squares / channels + norm_eps) * gain).astype(bf16)
        step = min(hidden, 256)
        for h in range(0, hidden, step):
            pre = ein(in_ref[pl.ds(h, step), :], normed, ((1,), (0,)))
            pre = pre + hid_col_ref[pl.ds(h, step), 2:3]
            act = pre * (0.5 * lax.erf(pre * (0.5**0.5)) + 0.5)
            hid[s % 2, pl.ds(h, step), :] = act.astype(bf16)
        upd = ein(out_ref[...], hid[s % 2], ((1,), (0,))).astype(bf16)
        for j in range(groups):
            for i in range(block_rows):
                upd_ref[j, s, i] = upd[
                    j * chan_local : (j + 1) * chan_local, i * block_cols : (i + 1) * block_cols
                ]


def block_step(body, rims, weights):
    groups, per, block_rows, chan_local, block_cols = body.shape
    channels = groups * chan_local
    hidden = weights[1].shape[0]
    cells = per * block_rows * block_cols
    return pl.pallas_call(
        block_kernel,
        out_shape=shape(body.shape),
        in_specs=[VMEM] * 7,
        out_specs=VMEM,
        scratch_shapes=[
            pltpu.VMEM((2, 9 * channels, block_rows * block_cols), bf16),
            pltpu.VMEM((2, hidden, block_rows * block_cols), bf16),
        ],
        compiler_params=params(),
        cost_estimate=pl.CostEstimate(
            flops=2 * cells * (9 * channels * channels + 2 * channels * hidden),
            bytes_accessed=8 * 1024 * 1024,
            transcendentals=0,
        ),
        name="block_step",
    )(body, rims, *weights)


def forcing_kernel(starts_ref, row_ref, side_ref, *refs):
    *pieces, out_ref, wide, got = refs
    slot_count, block_rows, chan_local, block_cols = out_ref.shape
    lanes = wide.shape[1]
    for n, piece in enumerate(pieces):
        rows = piece.shape[0]
        start = pl.multiple_of(starts_ref[n] * rows, 8)
        wide[pl.ds(start, rows), :] = piece[...].astype(f32)

    def one(q, _):
        for k in range(block_cols):
            got[pl.ds(k, 1), :] = wide[pl.ds(row_ref[q, k], 1), :]
        across = got[...].T
        side = side_ref[pl.ds(q, 1), :]
        total = across[:chan_local]
        for k in range(1, lanes // chan_local):
            total = jnp.where(side == k, across[k * chan_local : (k + 1) * chan_local], total)
        out_ref[q // block_rows, q % block_rows] = total.astype(bf16)
        return 0

    lax.fori_loop(0, slot_count * block_rows, one, 0)


def gather_flux(flux):
    count = lax.axis_size("tile")
    if count > 4:
        return [lax.all_gather(flux, "tile", axis=0, tiled=True)], jnp.zeros((1,), jnp.int32)
    pieces = [flux]
    for d in range(1, count):
        turn = [(i, (i + d) % count) for i in range(count)]
        pieces.append(lax.ppermute(flux, "tile", turn))
    me = lax.axis_index("tile")
    return pieces, jnp.stack([(me - d) % count for d in range(count)])


def forcing_of(pieces, starts, remap, rows_local, chan_local):
    slot_count, block_rows, block_cols = remap.shape
    side_by = 128 // chan_local
    part = rows_local // side_by
    table_rows = sum(piece.shape[0] for piece in pieces)
    target = jnp.clip(remap, 0, table_rows * side_by - 1).reshape(-1, block_cols)
    tile_of = target // rows_local
    within = target - tile_of * rows_local
    side = within // part
    row = tile_of * part + within - side * part
    return pl.pallas_call(
        forcing_kernel,
        out_shape=shape((slot_count, block_rows, chan_local, block_cols)),
        in_specs=[SMEM, SMEM, VMEM] + [VMEM] * len(pieces),
        out_specs=VMEM,
        scratch_shapes=[
            pltpu.VMEM((table_rows, 128), f32),
            pltpu.VMEM((block_cols, 128), f32),
        ],
        compiler_params=params(),
        cost_estimate=pl.CostEstimate(
            flops=0, bytes_accessed=32 * 1024 * 1024, transcendentals=0
        ),
        name="forcing",
    )(starts, row, side, *pieces)


def final_kernel(xt_ref, upd_ref, forcing_ref, mask_ref, scale_ref, out_ref):
    slot_count, block_rows, chan_local, block_cols = xt_ref.shape
    scale = scale_ref[...].astype(f32)
    for s in range(slot_count):
        total = xt_ref[s].astype(f32) + scale[None] * upd_ref[s].astype(f32)
        total = total + forcing_ref[s].astype(f32)
        total = mask_ref[s].astype(f32)[:, None, :] * total
        out_ref[:, s] = jnp.swapaxes(total, 0, 1).astype(bf16)


def final_step(xt, update, forcing, cell_mask, layer_scale):
    slot_count, block_rows, chan_local, block_cols = xt.shape
    return pl.pallas_call(
        final_kernel,
        out_shape=shape((chan_local, slot_count, block_rows, block_cols)),
        in_specs=[VMEM] * 5,
        out_specs=VMEM,
        compiler_params=params(),
        name="final_step",
    )(xt, update, forcing, cell_mask, layer_scale[:, None])


def on_device(
    ocean_state,
    atmos,
    flux_weight,
    conv_weight,
    conv_bias,
    norm_gain,
    in_weight,
    in_bias,
    out_weight,
    layer_scale,
    cell_mask,
    neighbours,
    remap,
):
    chan_local, slot_count, block_rows, block_cols = ocean_state.shape
    groups = lax.axis_size(GROUP)
    tile_count = lax.axis_size("tile")
    per = slot_count // groups
    hid_local = in_weight.shape[1]

    xt, strips = prep(ocean_state)
    up = [(i, i + 1) for i in range(tile_count - 1)]
    strips_prev = lax.ppermute(strips, "tile", up)
    strips_next = lax.ppermute(strips, "tile", [(b, a) for a, b in up])
    body = lax.all_to_all(
        xt.reshape(groups, per, block_rows, chan_local, block_cols), GROUP, 0, 0, tiled=True
    )
    packed, part = pack_weights(
        lax.axis_index("ens"), conv_weight, conv_bias, norm_gain, in_weight, in_bias, out_weight
    )
    pieces, starts = exchange_weights(packed, part)
    weights = unpack_weights(pieces, starts, groups, chan_local, hid_local)
    flux = fluxes_of(atmos, flux_weight)
    strips_prev, strips_next, flux = lax.optimization_barrier((strips_prev, strips_next, flux))
    table, places = gather_flux(flux)

    first_slot = (lax.axis_index("tile") - 1) * slot_count
    rims = rims_of(strips_prev, strips, strips_next, neighbours, first_slot, groups)
    rims = lax.all_to_all(rims, GROUP, 0, 0, tiled=True)
    update = block_step(body, rims, weights)
    update, table = lax.optimization_barrier((update, table))
    update = lax.all_to_all(update, GROUP, 0, 0, tiled=True)
    update = update.reshape(xt.shape)
    forcing = forcing_of(table, places, remap, atmos.shape[0], chan_local)
    return final_step(xt, update, forcing, cell_mask, layer_scale)


def solution(mesh):
    placed = (
        P(("chan", "sec"), ("ens", "tile"), None, None),
        P(("ens", "tile"), None),
        P(None, ("chan", "sec")),
        P(None, None, ("chan", "sec")),
        P(("chan", "sec")),
        P(("chan", "sec")),
        P(None, ("chan", "sec")),
        P(("chan", "sec")),
        P(("chan", "sec"), None),
        P(("chan", "sec")),
        P("tile", None, None),
        P("tile", None),
        P("tile", None, None),
    )
    return jax.shard_map(
        on_device,
        mesh=mesh,
        in_specs=placed,
        out_specs=P(("chan", "sec"), ("ens", "tile"), None, None),
        check_vma=False,
    )
```

```python
import functools

import jax
import jax.numpy as jnp
from jax import lax
from jax.experimental import pallas as pl
from jax.experimental.pallas import tpu as pltpu
from jax.sharding import PartitionSpec as P

norm_eps = 1e-06
bf16 = jnp.bfloat16
f32 = jnp.float32
GROUP = ("chan", "sec")
BIAS_ROWS = 32
VMEM = pl.BlockSpec(memory_space=pltpu.VMEM)
SMEM = pl.BlockSpec(memory_space=pltpu.SMEM)
HBM = pl.BlockSpec(memory_space=pltpu.HBM)


def shape(dims, dtype=bf16):
    return jax.ShapeDtypeStruct(dims, dtype)


def params(mib=20):
    return pltpu.CompilerParams(vmem_limit_bytes=mib * 1024 * 1024)


def ein(a, b, dims):
    return lax.dot_general(a, b, (dims, ((), ())), preferred_element_type=f32)


def start_kernel(
    place_ref, state_ref, conv_ref, bias_ref, gain_ref, in_ref, in_bias_ref, out_ref, *refs
):
    *pieces, strips_ref, pack_ref, part_ref, state_v, conv_v, in_v, out_v, sems = refs
    groups, chan_local, per, block_rows, block_cols = state_v.shape
    taps, _, channels = conv_v.shape
    hid_local = out_v.shape[0]
    me = place_ref[0]
    copies = [
        pltpu.make_async_copy(conv_ref, conv_v, sems.at[groups]),
        pltpu.make_async_copy(in_ref, in_v, sems.at[groups + 1]),
        pltpu.make_async_copy(out_ref, out_v, sems.at[groups + 2]),
    ]
    for copy in copies:
        copy.start()
    loads = []
    for d in range(groups):
        first = jnp.bitwise_xor(me, d) * per
        loads.append(
            pltpu.make_async_copy(
                state_ref.at[:, pl.ds(first, per)], state_v.at[d], sems.at[d]
            )
        )
        loads[d].start()

    def widen(row):
        row = row.astype(f32)
        if row.shape[1] == channels:
            return row
        return jnp.concatenate([row, jnp.zeros((1, channels - row.shape[1]), f32)], axis=1)

    rest = jnp.zeros((BIAS_ROWS - 3, channels), f32)
    biases = jnp.concatenate(
        [widen(bias_ref[...]), widen(gain_ref[...]), widen(in_bias_ref[...]), rest], axis=0
    )
    at = taps * chan_local
    pack_ref[pl.ds(at + 2 * hid_local, BIAS_ROWS), :] = biases.astype(bf16)
    for copy in copies:
        copy.wait()
    for t in range(taps):
        pack_ref[pl.ds(t * chan_local, chan_local), :] = conv_v[t]
    pack_ref[pl.ds(at, hid_local), :] = in_v[...].astype(f32).T.astype(bf16)
    pack_ref[pl.ds(at + hid_local, hid_local), :] = out_v[...]
    part = part_ref.shape[0]
    part_ref[...] = pack_ref[pl.ds(pl.multiple_of(place_ref[1] * part, 16), part), :]

    lane = lax.broadcasted_iota(jnp.int32, (chan_local, block_cols), 1)
    cols = jnp.zeros((chan_local, block_cols), f32)
    for d in range(groups):
        loads[d].wait()
        first = jnp.bitwise_xor(me, d) * per
        for s in range(per):
            slot = first + s
            rows = jnp.swapaxes(state_v[d, :, s].astype(f32), 0, 1)
            packed = rows.astype(bf16)
            pieces[d][s] = packed
            strips_ref[2 * slot] = packed[0]
            strips_ref[2 * slot + 1] = packed[block_rows - 1]
            for r in range(block_rows):
                spot = 2 * (block_rows * slot + r)
                turned = pltpu.roll(rows[r], spot + 1, 1)
                cols = jnp.where((lane == spot) | (lane == spot + 1), turned, cols)
    strips_ref[strips_ref.shape[0] - 1] = cols.astype(bf16)


def start_step(
    place, groups, state, conv_weight, conv_bias, norm_gain, in_weight, in_bias, out_weight
):
    chan_local, slot_count, block_rows, block_cols = state.shape
    per = slot_count // groups
    taps, channels, _ = conv_weight.shape
    hid_local = out_weight.shape[0]
    rows = taps * chan_local + 2 * hid_local + BIAS_ROWS
    piece = shape((per, block_rows, chan_local, block_cols))
    *pieces, strips, packed, part = pl.pallas_call(
        start_kernel,
        out_shape=(piece,) * groups
        + (
            shape((2 * slot_count + 1, chan_local, block_cols)),
            shape((rows, channels)),
            shape((rows // 2, channels)),
        ),
        in_specs=[SMEM, HBM, HBM, VMEM, VMEM, HBM, VMEM, HBM],
        out_specs=(VMEM,) * (groups + 3),
        scratch_shapes=[
            pltpu.VMEM((groups, chan_local, per, block_rows, block_cols), bf16),
            pltpu.VMEM((taps, chan_local, channels), bf16),
            pltpu.VMEM((channels, hid_local), bf16),
            pltpu.VMEM((hid_local, channels), bf16),
            pltpu.SemaphoreType.DMA((groups + 3,)),
        ],
        compiler_params=params(),
        name="start_step",
    )(
        place,
        state,
        conv_weight.transpose(0, 2, 1),
        conv_bias.astype(f32)[None],
        norm_gain.astype(f32)[None],
        in_weight,
        in_bias.astype(f32)[None],
        out_weight,
    )
    return pieces, strips, packed, part


def trade(pieces):
    count = len(pieces)
    got = list(pieces)
    for d in list(range(count // 2, count)) + list(range(1, count // 2)):
        got[d] = lax.ppermute(pieces[d], GROUP, [(i, i ^ d) for i in range(count)])
    return got


def unpack_kernel(chan_local, hid_local, starts_ref, *refs):
    *pieces, conv_ref, in_ref, out_ref, col_ref, hid_col_ref, all_ref = refs
    groups, rows, channels = all_ref.shape
    unit = min(rows, *(piece.shape[0] for piece in pieces))
    for n, piece in enumerate(pieces):
        for k in range(piece.shape[0] // unit):
            at = starts_ref[n] + k
            parts = rows // unit
            start = pl.multiple_of((at % parts) * unit, 16)
            all_ref[at // parts, pl.ds(start, unit), :] = piece[pl.ds(k * unit, unit), :]
    at = 9 * chan_local
    for j in range(groups):
        for t in range(9):
            conv_ref[pl.ds(j * chan_local, chan_local), pl.ds(t * channels, channels)] = all_ref[
                j, pl.ds(t * chan_local, chan_local), :
            ]
        in_ref[pl.ds(j * hid_local, hid_local), :] = all_ref[j, pl.ds(at, hid_local), :]
        biases = all_ref[j, pl.ds(at + 2 * hid_local, BIAS_ROWS), :].astype(f32)
        across = biases.T
        col_ref[pl.ds(j * chan_local, chan_local), :] = across[:chan_local]
        hid_col_ref[pl.ds(j * hid_local, hid_local), :] = across[:hid_local]
    outs = jnp.concatenate(
        [all_ref[j, pl.ds(at + hid_local, hid_local), :] for j in range(groups)], axis=0
    )
    out_ref[...] = outs.astype(f32).T.astype(bf16)


def unpack_weights(pieces, starts, groups, chan_local, hid_local):
    rows = sum(piece.shape[0] for piece in pieces) // groups
    channels = groups * chan_local
    hidden = groups * hid_local
    return pl.pallas_call(
        functools.partial(unpack_kernel, chan_local, hid_local),
        out_shape=(
            shape((channels, 9 * channels)),
            shape((hidden, channels)),
            shape((channels, hidden)),
            shape((channels, BIAS_ROWS), f32),
            shape((hidden, BIAS_ROWS), f32),
        ),
        in_specs=[SMEM] + [VMEM] * len(pieces),
        out_specs=(VMEM,) * 5,
        scratch_shapes=[pltpu.VMEM((groups, rows, channels), bf16)],
        compiler_params=params(),
        name="unpack_weights",
    )(starts, *pieces)


def swap(value, axis):
    return lax.ppermute(value, axis, [(0, 1), (1, 0)])


def exchange_weights(packed, part):
    if lax.axis_size("ens") != 2 or lax.axis_size("chan") != 2 or lax.axis_size("sec") != 2:
        whole = lax.all_gather(packed, GROUP, axis=0, tiled=True)
        return [whole], jnp.zeros((1,), jnp.int32)
    ens, chan, sec = (lax.axis_index(name) for name in ("ens", "chan", "sec"))
    other = swap(packed, "sec")
    near = swap(part, "chan")
    far = swap(near, "ens")
    near_other = swap(near, "sec")
    far_other = swap(far, "sec")
    own = 2 * (2 * chan + sec)
    beside = 2 * (2 * chan + 1 - sec)
    across = 2 * (2 * (1 - chan) + sec)
    corner = 2 * (2 * (1 - chan) + 1 - sec)
    starts = [own, beside, across + ens, across + 1 - ens, corner + ens, corner + 1 - ens]
    return [packed, other, near, far, near_other, far_other], jnp.stack(starts)


def flux_kernel(atmos_ref, weight_ref, out_ref):
    rows, lanes = out_ref.shape
    chan_local, features = weight_ref.shape
    weight = weight_ref[...]
    total = jnp.zeros((rows, lanes), f32)
    for k in range(lanes // chan_local):
        parts = [weight if j == k else jnp.zeros_like(weight) for j in range(lanes // chan_local)]
        wide = jnp.concatenate(parts, axis=0)
        total = total + ein(atmos_ref[pl.ds(k * rows, rows), :], wide, ((1,), (1,)))
    out_ref[...] = total.astype(bf16)


def fluxes_of(atmos, flux_weight):
    side = 128 // flux_weight.shape[1]
    return pl.pallas_call(
        flux_kernel,
        out_shape=shape((atmos.shape[0] // side, 128)),
        in_specs=[VMEM, VMEM],
        out_specs=VMEM,
        compiler_params=params(),
        name="fluxes",
    )(atmos, flux_weight.T)


def onehot_kernel(at_ref, out_ref):
    spot = lax.broadcasted_iota(jnp.int32, out_ref.shape, 0)
    out_ref[...] = (spot == at_ref[...]).astype(f32).astype(bf16)


def onehot_of(at, rows):
    return pl.pallas_call(
        onehot_kernel,
        out_shape=shape((rows, at.shape[1])),
        in_specs=[VMEM],
        out_specs=VMEM,
        compiler_params=params(),
        name="onehot",
    )(at)


def rim_kernel(place_ref, entry_ref, chosen_ref, prev_ref, own_ref, next_ref, *refs):
    *rims, held, cols = refs
    tiles, chan_local, block_cols = own_ref.shape
    groups = len(rims)
    slot_count = (tiles - 1) // 2
    per = slot_count // groups
    ends = jnp.concatenate(
        [prev_ref[tiles - 1], own_ref[tiles - 1], next_ref[tiles - 1]], axis=1
    )
    picked = ein(ends, chosen_ref[...], ((1,), (0,))).astype(bf16)
    for k in range(cols.shape[0]):
        cols[k] = picked[:, k * block_cols : (k + 1) * block_cols]
    held[pl.ds(0, tiles)] = prev_ref[...]
    held[pl.ds(tiles, tiles)] = own_ref[...]
    held[pl.ds(2 * tiles, tiles)] = next_ref[...]
    held[3 * tiles] = jnp.zeros((chan_local, block_cols), bf16)
    for d in range(groups):
        group = jnp.bitwise_xor(place_ref[0], d)
        for s in range(per):
            rims[d][2 * s] = held[entry_ref[0, group * per + s]]
            rims[d][2 * s + 1] = held[entry_ref[1, group * per + s]]
        rims[d][2 * per] = cols[group * (16 * per) // block_cols]


def rim_places(neighbours, first_slot, block_rows):
    slot_count = neighbours.shape[0]
    tiles = 2 * slot_count + 1
    valid = neighbours >= 0
    slot = jnp.clip(neighbours - first_slot, 0, 3 * slot_count - 1)
    tile_of = slot // slot_count
    place = tile_of * tiles + 2 * (slot - tile_of * slot_count)
    entries = jnp.stack(
        [
            jnp.where(valid[:, 2], place[:, 2] + 1, 3 * tiles),
            jnp.where(valid[:, 3], place[:, 3], 3 * tiles),
        ]
    )
    base = jnp.where(valid, 2 * block_rows * slot, -4 * block_rows)
    last = 2 * (block_rows - 1)
    west = [base[:, 4] + last] + [base[:, 0] + 2 * r for r in range(block_rows)] + [base[:, 6]]
    east = [base[:, 5] + last] + [base[:, 1] + 2 * r for r in range(block_rows)] + [base[:, 7]]
    none = [jnp.full((slot_count,), -1, jnp.int32)] * (8 - block_rows - 2)
    at = jnp.stack(west + none + [e + 1 for e in east] + none, axis=1)
    return entries, at.reshape(1, slot_count * 16)


def rims_of(place, entries, chosen, strips_prev, strips, strips_next, groups):
    tiles, chan_local, block_cols = strips.shape
    per = (tiles - 1) // 2 // groups
    return pl.pallas_call(
        rim_kernel,
        out_shape=(shape((2 * per + 1, chan_local, block_cols)),) * groups,
        in_specs=[SMEM, SMEM, VMEM, VMEM, VMEM, VMEM],
        out_specs=(VMEM,) * groups,
        scratch_shapes=[
            pltpu.VMEM((3 * tiles + 1, chan_local, block_cols), bf16),
            pltpu.VMEM((chosen.shape[1] // block_cols, chan_local, block_cols), bf16),
        ],
        compiler_params=params(),
        name="rims",
    )(place, entries, chosen, strips_prev, strips, strips_next)


def block_kernel(groups, place_ref, *refs):
    bodies, refs = refs[:groups], refs[groups:]
    rims, refs = refs[:groups], refs[groups:]
    conv_ref, in_ref, out_ref, col_ref, hid_col_ref = refs[:5]
    updates, (taken, hid, upd_v) = refs[5 : 5 + groups], refs[5 + groups :]
    per, block_rows, chan_local, block_cols = bodies[0].shape
    channels = groups * chan_local
    hidden = in_ref.shape[0]
    me = place_ref[0]
    lane = lax.broadcasted_iota(jnp.int32, (chan_local, block_cols), 1)
    bias = col_ref[:, 0:1]
    gain = col_ref[:, 1:2]
    base = (me * (16 * per)) % block_cols
    for s in range(per):
        for d in range(groups):
            row = pl.multiple_of(jnp.bitwise_xor(me, d) * chan_local, chan_local)
            ends = rims[d][2 * per].astype(f32)
            for p in range(block_rows + 2):
                if p == 0:
                    mid = rims[d][2 * s]
                elif p == block_rows + 1:
                    mid = rims[d][2 * s + 1]
                else:
                    mid = bodies[d][s, p - 1]
                wide = mid.astype(f32)
                spot = 16 * s + p
                left = jnp.where(
                    lane == 0,
                    pltpu.roll(ends, 2 * block_cols - spot - base, 1),
                    pltpu.roll(wide, 1, 1),
                ).astype(bf16)
                right = jnp.where(
                    lane == block_cols - 1,
                    pltpu.roll(ends, 3 * block_cols - 1 - spot - 8 - base, 1),
                    pltpu.roll(wide, block_cols - 1, 1),
                ).astype(bf16)
                for a in range(3):
                    i = p - a
                    if 0 <= i < block_rows:
                        for b, piece in enumerate((left, mid, right)):
                            taken[
                                s % 2,
                                pl.ds((3 * a + b) * channels + row, chan_local),
                                pl.ds(i * block_cols, block_cols),
                            ] = piece
        conv = ein(conv_ref[...], taken[s % 2], ((1,), (0,))) + bias
        squares = jnp.sum(conv * conv, axis=0, keepdims=True)
        normed = (conv * lax.rsqrt(squares / channels + norm_eps) * gain).astype(bf16)
        step = min(hidden, 256)
        for h in range(0, hidden, step):
            pre = ein(in_ref[pl.ds(h, step), :], normed, ((1,), (0,)))
            pre = pre + hid_col_ref[pl.ds(h, step), 2:3]
            act = pre * (0.5 * lax.erf(pre * (0.5**0.5)) + 0.5)
            hid[s % 2, pl.ds(h, step), :] = act.astype(bf16)
        upd_v[s % 2] = ein(out_ref[...], hid[s % 2], ((1,), (0,))).astype(bf16)
        for d in range(groups):
            row = pl.multiple_of(jnp.bitwise_xor(me, d) * chan_local, chan_local)
            for i in range(block_rows):
                updates[d][s, i] = upd_v[
                    s % 2, pl.ds(row, chan_local), pl.ds(i * block_cols, block_cols)
                ]


def block_step(place, bodies, rims, weights):
    groups = len(bodies)
    per, block_rows, chan_local, block_cols = bodies[0].shape
    channels = groups * chan_local
    hidden = weights[1].shape[0]
    cells = per * block_rows * block_cols
    return pl.pallas_call(
        functools.partial(block_kernel, groups),
        out_shape=(shape(bodies[0].shape),) * groups,
        in_specs=[SMEM] + [VMEM] * (2 * groups + 5),
        out_specs=(VMEM,) * groups,
        scratch_shapes=[
            pltpu.VMEM((2, 9 * channels, block_rows * block_cols), bf16),
            pltpu.VMEM((2, hidden, block_rows * block_cols), bf16),
            pltpu.VMEM((2, channels, block_rows * block_cols), bf16),
        ],
        compiler_params=params(24),
        cost_estimate=pl.CostEstimate(
            flops=2 * cells * (9 * channels * channels + 2 * channels * hidden),
            bytes_accessed=8 * 1024 * 1024,
            transcendentals=0,
        ),
        name="block_step",
    )(place, *bodies, *rims, *weights)


def forcing_kernel(starts_ref, row_ref, side_ref, *refs):
    *pieces, out_ref, wide, even, odd = refs
    slot_count, block_rows, chan_local, block_cols = out_ref.shape
    lanes = wide.shape[1]
    for n, piece in enumerate(pieces):
        rows = piece.shape[0]
        start = pl.multiple_of(starts_ref[n] * rows, 8)
        wide[pl.ds(start, rows), :] = piece[...].astype(f32)

    row_at = lax.broadcasted_iota(jnp.int32, (lanes, lanes), 0)
    col_at = lax.broadcasted_iota(jnp.int32, (lanes, lanes), 1)
    eye = (row_at == col_at).astype(f32).astype(bf16)
    count = slot_count * block_rows

    def fetch(q, got):
        for k in range(block_cols):
            got[pl.ds(k, 1), :] = wide[pl.ds(row_ref[q, k], 1), :]

    def emit(q, got):
        across = ein(eye, got[...].astype(bf16), ((1,), (1,)))
        side = side_ref[pl.ds(q, 1), :]
        total = across[:chan_local]
        for k in range(1, lanes // chan_local):
            total = jnp.where(side == k, across[k * chan_local : (k + 1) * chan_local], total)
        out_ref[q // block_rows, q % block_rows] = total.astype(bf16)

    fetch(0, even)

    def two(n, _):
        q = 2 * n
        fetch(q + 1, odd)
        emit(q, even)
        fetch(jnp.minimum(q + 2, count - 1), even)
        emit(q + 1, odd)
        return 0

    lax.fori_loop(0, count // 2, two, 0)


def gather_flux(flux):
    count = lax.axis_size("tile")
    if count > 4:
        return [lax.all_gather(flux, "tile", axis=0, tiled=True)], jnp.zeros((1,), jnp.int32)
    pieces = [flux]
    for d in range(1, count):
        turn = [(i, (i + d) % count) for i in range(count)]
        pieces.append(lax.ppermute(flux, "tile", turn))
    me = lax.axis_index("tile")
    return pieces, jnp.stack([(me - d) % count for d in range(count)])


def forcing_of(pieces, starts, remap, rows_local, chan_local):
    slot_count, block_rows, block_cols = remap.shape
    side_by = 128 // chan_local
    part = rows_local // side_by
    table_rows = sum(piece.shape[0] for piece in pieces)
    target = jnp.clip(remap, 0, table_rows * side_by - 1).reshape(-1, block_cols)
    tile_of = target // rows_local
    within = target - tile_of * rows_local
    side = within // part
    row = tile_of * part + within - side * part
    return pl.pallas_call(
        forcing_kernel,
        out_shape=shape((slot_count, block_rows, chan_local, block_cols)),
        in_specs=[SMEM, SMEM, VMEM] + [VMEM] * len(pieces),
        out_specs=VMEM,
        scratch_shapes=[
            pltpu.VMEM((table_rows, 128), f32),
            pltpu.VMEM((block_cols, 128), f32),
            pltpu.VMEM((block_cols, 128), f32),
        ],
        compiler_params=params(),
        cost_estimate=pl.CostEstimate(
            flops=0, bytes_accessed=32 * 1024 * 1024, transcendentals=0
        ),
        name="forcing",
    )(starts, row, side, *pieces)


def final_kernel(groups, place_ref, *refs):
    pieces, updates, rest = refs[:groups], refs[groups : 2 * groups], refs[2 * groups :]
    forcing_ref, mask_ref, scale_ref, out_ref = rest
    per = pieces[0].shape[0]
    scale = scale_ref[...].astype(f32)
    for d in range(groups):
        for s in range(per):
            slot = jnp.bitwise_xor(place_ref[0], d) * per + s
            total = pieces[d][s].astype(f32) + scale[None] * updates[d][s].astype(f32)
            total = total + forcing_ref[slot].astype(f32)
            total = mask_ref[slot].astype(f32)[:, None, :] * total
            out_ref[:, slot] = jnp.swapaxes(total, 0, 1).astype(bf16)


def final_step(place, pieces, updates, forcing, cell_mask, layer_scale):
    slot_count, block_rows, chan_local, block_cols = forcing.shape
    groups = len(pieces)
    return pl.pallas_call(
        functools.partial(final_kernel, groups),
        out_shape=shape((chan_local, slot_count, block_rows, block_cols)),
        in_specs=[SMEM] + [VMEM] * (2 * groups + 3),
        out_specs=VMEM,
        compiler_params=params(),
        name="final_step",
    )(place, *pieces, *updates, forcing, cell_mask, layer_scale.astype(f32)[:, None])


def on_device(
    ocean_state,
    atmos,
    flux_weight,
    conv_weight,
    conv_bias,
    norm_gain,
    in_weight,
    in_bias,
    out_weight,
    layer_scale,
    cell_mask,
    neighbours,
    remap,
):
    chan_local, slot_count, block_rows, block_cols = ocean_state.shape
    groups = lax.axis_size(GROUP)
    tile_count = lax.axis_size("tile")
    hid_local = in_weight.shape[1]
    place = jnp.stack([lax.axis_index(GROUP), lax.axis_index("ens")])
    first_slot = (lax.axis_index("tile") - 1) * slot_count

    pieces, strips, packed, part = start_step(
        place, groups, ocean_state, conv_weight, conv_bias, norm_gain, in_weight, in_bias, out_weight
    )
    up = [(i, i + 1) for i in range(tile_count - 1)]
    strips_prev = lax.ppermute(strips, "tile", up)
    strips_next = lax.ppermute(strips, "tile", [(b, a) for a, b in up])
    parts, starts = exchange_weights(packed, part)
    bodies = trade(pieces)
    entries, at = rim_places(neighbours, first_slot, block_rows)
    chosen = onehot_of(at, 3 * block_cols)
    flux = fluxes_of(atmos, flux_weight)
    strips_prev, strips_next, flux = lax.optimization_barrier((strips_prev, strips_next, flux))
    rims = rims_of(place, entries, chosen, strips_prev, strips, strips_next, groups)
    rims = trade(rims)
    table, places = gather_flux(flux)
    weights = unpack_weights(parts, starts, groups, chan_local, hid_local)
    updates = block_step(place, bodies, rims, weights)
    updates, table = lax.optimization_barrier((updates, table))
    updates = trade(updates)
    forcing = forcing_of(table, places, remap, atmos.shape[0], chan_local)
    return final_step(place, pieces, updates, forcing, cell_mask, layer_scale)


def solution(mesh):
    placed = (
        P(("chan", "sec"), ("ens", "tile"), None, None),
        P(("ens", "tile"), None),
        P(None, ("chan", "sec")),
        P(None, None, ("chan", "sec")),
        P(("chan", "sec")),
        P(("chan", "sec")),
        P(None, ("chan", "sec")),
        P(("chan", "sec")),
        P(("chan", "sec"), None),
        P(("chan", "sec")),
        P("tile", None, None),
        P("tile", None),
        P("tile", None, None),
    )
    return jax.shard_map(
        on_device,
        mesh=mesh,
        in_specs=placed,
        out_specs=P(("chan", "sec"), ("ens", "tile"), None, None),
        check_vma=False,
    )
```

```python
import functools

import jax
import jax.numpy as jnp
from jax import lax
from jax.experimental import pallas as pl
from jax.experimental.pallas import tpu as pltpu
from jax.sharding import PartitionSpec as P

norm_eps = 1e-06
bf16 = jnp.bfloat16
f32 = jnp.float32
GROUP = ("chan", "sec")
BIAS_ROWS = 32
VMEM = pl.BlockSpec(memory_space=pltpu.VMEM)
SMEM = pl.BlockSpec(memory_space=pltpu.SMEM)
ANY = pl.BlockSpec(memory_space=pl.ANY)


def shape(dims, dtype=bf16):
    return jax.ShapeDtypeStruct(dims, dtype)


def params(mib=20):
    return pltpu.CompilerParams(vmem_limit_bytes=mib * 1024 * 1024)


def ein(a, b, dims):
    return lax.dot_general(a, b, (dims, ((), ())), preferred_element_type=f32)


def start_kernel(
    place_ref, state_ref, conv_ref, bias_ref, gain_ref, in_ref, in_bias_ref, out_ref, *refs
):
    xt_ref, strips_ref, pack_ref, part_ref, state_v, conv_v, in_v, out_v, sems = refs
    groups, chan_local, per, block_rows, block_cols = state_v.shape
    taps, _, channels = conv_v.shape
    hid_local = out_v.shape[0]
    copies = [
        pltpu.make_async_copy(conv_ref, conv_v, sems.at[groups]),
        pltpu.make_async_copy(in_ref, in_v, sems.at[groups + 1]),
        pltpu.make_async_copy(out_ref, out_v, sems.at[groups + 2]),
    ]
    for copy in copies:
        copy.start()
    loads = []
    for d in range(groups):
        loads.append(
            pltpu.make_async_copy(
                state_ref.at[:, pl.ds(d * per, per)], state_v.at[d], sems.at[d]
            )
        )
        loads[d].start()

    def widen(ref):
        rows = ref[...].astype(f32)
        row = jnp.concatenate([rows[k : k + 1] for k in range(rows.shape[0])], axis=1)
        if row.shape[1] == channels:
            return row
        return jnp.concatenate([row, jnp.zeros((1, channels - row.shape[1]), f32)], axis=1)

    rest = jnp.zeros((BIAS_ROWS - 3, channels), f32)
    biases = jnp.concatenate(
        [widen(bias_ref), widen(gain_ref), widen(in_bias_ref), rest], axis=0
    )
    at = taps * chan_local
    pack_ref[pl.ds(at + 2 * hid_local, BIAS_ROWS), :] = biases.astype(bf16)
    for copy in copies:
        copy.wait()
    for t in range(taps):
        pack_ref[pl.ds(t * chan_local, chan_local), :] = conv_v[t]
    pack_ref[pl.ds(at, hid_local), :] = in_v[...].astype(f32).T.astype(bf16)
    pack_ref[pl.ds(at + hid_local, hid_local), :] = out_v[...]
    part = part_ref.shape[0]
    part_ref[...] = pack_ref[pl.ds(pl.multiple_of(place_ref[1] * part, 16), part), :]

    lane = lax.broadcasted_iota(jnp.int32, (chan_local, block_cols), 1)
    cols = jnp.zeros((chan_local, block_cols), f32)
    for d in range(groups):
        loads[d].wait()
        for s in range(per):
            slot = d * per + s
            rows = jnp.swapaxes(state_v[d, :, s].astype(f32), 0, 1)
            packed = rows.astype(bf16)
            xt_ref[slot] = packed
            strips_ref[2 * slot] = packed[0]
            strips_ref[2 * slot + 1] = packed[block_rows - 1]
            for r in range(block_rows):
                spot = 2 * (block_rows * slot + r)
                turned = pltpu.roll(rows[r], spot + 1, 1)
                cols = jnp.where((lane == spot) | (lane == spot + 1), turned, cols)
    strips_ref[strips_ref.shape[0] - 1] = cols.astype(bf16)


def start_step(
    place, groups, state, conv_weight, conv_bias, norm_gain, in_weight, in_bias, out_weight
):
    chan_local, slot_count, block_rows, block_cols = state.shape
    per = slot_count // groups
    taps, channels, _ = conv_weight.shape
    hid_local = out_weight.shape[0]
    rows = taps * chan_local + 2 * hid_local + BIAS_ROWS
    return pl.pallas_call(
        start_kernel,
        out_shape=(
            shape((slot_count, block_rows, chan_local, block_cols)),
            shape((2 * slot_count + 1, chan_local, block_cols)),
            shape((rows, channels)),
            shape((rows // 2, channels)),
        ),
        in_specs=[SMEM, ANY, ANY, VMEM, VMEM, ANY, VMEM, ANY],
        out_specs=(VMEM,) * 4,
        scratch_shapes=[
            pltpu.VMEM((groups, chan_local, per, block_rows, block_cols), bf16),
            pltpu.VMEM((taps, chan_local, channels), bf16),
            pltpu.VMEM((channels, hid_local), bf16),
            pltpu.VMEM((hid_local, channels), bf16),
            pltpu.SemaphoreType.DMA((groups + 3,)),
        ],
        compiler_params=params(60),
        name="start_step",
    )(
        place,
        state,
        conv_weight.transpose(0, 2, 1),
        conv_bias.reshape(-1, min(128, chan_local)),
        norm_gain.reshape(-1, min(128, chan_local)),
        in_weight,
        in_bias.reshape(-1, min(128, hid_local)),
        out_weight,
    )


def send(piece, d, count):
    return lax.ppermute(piece, GROUP, [(i, i ^ d) for i in range(count)])


def trade(pieces):
    count = len(pieces)
    got = list(pieces)
    for d in list(range(count // 2, count)) + list(range(1, count // 2)):
        got[d] = send(pieces[d], d, count)
    return got


def unpack_kernel(chan_local, hid_local, starts_ref, *refs):
    *pieces, conv_ref, in_ref, out_ref, col_ref, hid_col_ref, all_ref = refs
    groups, rows, channels = all_ref.shape
    unit = min(rows, *(piece.shape[0] for piece in pieces))
    for n, piece in enumerate(pieces):
        for k in range(piece.shape[0] // unit):
            at = starts_ref[n] + k
            parts = rows // unit
            start = pl.multiple_of((at % parts) * unit, 16)
            all_ref[at // parts, pl.ds(start, unit), :] = piece[pl.ds(k * unit, unit), :]
    at = 9 * chan_local
    for j in range(groups):
        for t in range(9):
            conv_ref[pl.ds(j * chan_local, chan_local), pl.ds(t * channels, channels)] = all_ref[
                j, pl.ds(t * chan_local, chan_local), :
            ]
        in_ref[pl.ds(j * hid_local, hid_local), :] = all_ref[j, pl.ds(at, hid_local), :]
        biases = all_ref[j, pl.ds(at + 2 * hid_local, BIAS_ROWS), :].astype(f32)
        across = biases.T
        col_ref[pl.ds(j * chan_local, chan_local), :] = across[:chan_local]
        hid_col_ref[pl.ds(j * hid_local, hid_local), :] = across[:hid_local]
    outs = jnp.concatenate(
        [all_ref[j, pl.ds(at + hid_local, hid_local), :] for j in range(groups)], axis=0
    )
    out_ref[...] = outs.astype(f32).T.astype(bf16)


def unpack_weights(pieces, starts, groups, chan_local, hid_local):
    rows = sum(piece.shape[0] for piece in pieces) // groups
    channels = groups * chan_local
    hidden = groups * hid_local
    return pl.pallas_call(
        functools.partial(unpack_kernel, chan_local, hid_local),
        out_shape=(
            shape((channels, 9 * channels)),
            shape((hidden, channels)),
            shape((channels, hidden)),
            shape((channels, BIAS_ROWS), f32),
            shape((hidden, BIAS_ROWS), f32),
        ),
        in_specs=[SMEM] + [VMEM] * len(pieces),
        out_specs=(VMEM,) * 5,
        scratch_shapes=[pltpu.VMEM((groups, rows, channels), bf16)],
        compiler_params=params(),
        name="unpack_weights",
    )(starts, *pieces)


def swap(value, axis):
    return lax.ppermute(value, axis, [(0, 1), (1, 0)])


def exchange_weights(packed, part):
    if lax.axis_size("ens") != 2 or lax.axis_size("chan") != 2 or lax.axis_size("sec") != 2:
        whole = lax.all_gather(packed, GROUP, axis=0, tiled=True)
        return [whole], jnp.zeros((1,), jnp.int32)
    ens, chan, sec = (lax.axis_index(name) for name in ("ens", "chan", "sec"))
    near = swap(part, "chan")
    near, held = lax.optimization_barrier((near, packed))
    far = swap(near, "ens")
    other = swap(held, "sec")
    near_other = swap(near, "sec")
    far_other = swap(far, "sec")
    own = 2 * (2 * chan + sec)
    beside = 2 * (2 * chan + 1 - sec)
    across = 2 * (2 * (1 - chan) + sec)
    corner = 2 * (2 * (1 - chan) + 1 - sec)
    starts = [own, beside, across + ens, across + 1 - ens, corner + ens, corner + 1 - ens]
    return [packed, other, near, far, near_other, far_other], jnp.stack(starts)


def flux_kernel(atmos_ref, weight_ref, out_ref):
    rows, lanes = out_ref.shape
    chan_local, features = weight_ref.shape
    weight = weight_ref[...]
    total = jnp.zeros((rows, lanes), f32)
    for k in range(lanes // chan_local):
        parts = [weight if j == k else jnp.zeros_like(weight) for j in range(lanes // chan_local)]
        wide = jnp.concatenate(parts, axis=0)
        total = total + ein(atmos_ref[pl.ds(k * rows, rows), :], wide, ((1,), (1,)))
    out_ref[...] = total.astype(bf16)


def fluxes_of(atmos, flux_weight):
    side = 128 // flux_weight.shape[1]
    return pl.pallas_call(
        flux_kernel,
        out_shape=shape((atmos.shape[0] // side, 128)),
        in_specs=[VMEM, VMEM],
        out_specs=VMEM,
        compiler_params=params(),
        name="fluxes",
    )(atmos, flux_weight.T)


def onehot_kernel(at_ref, out_ref):
    spot = lax.broadcasted_iota(jnp.int32, out_ref.shape, 0)
    out_ref[...] = (spot == at_ref[...]).astype(f32).astype(bf16)


def onehot_of(at, rows):
    return pl.pallas_call(
        onehot_kernel,
        out_shape=shape((rows, at.shape[1])),
        in_specs=[VMEM],
        out_specs=VMEM,
        compiler_params=params(),
        name="onehot",
    )(at)


def rim_kernel(place_ref, entry_ref, chosen_ref, prev_ref, own_ref, next_ref, *refs):
    *rims, held, cols = refs
    tiles, chan_local, block_cols = own_ref.shape
    groups = len(rims)
    slot_count = (tiles - 1) // 2
    per = slot_count // groups
    ends = jnp.concatenate(
        [prev_ref[tiles - 1], own_ref[tiles - 1], next_ref[tiles - 1]], axis=1
    )
    picked = ein(ends, chosen_ref[...], ((1,), (0,))).astype(bf16)
    for k in range(cols.shape[0]):
        cols[k] = picked[:, k * block_cols : (k + 1) * block_cols]
    held[pl.ds(0, tiles)] = prev_ref[...]
    held[pl.ds(tiles, tiles)] = own_ref[...]
    held[pl.ds(2 * tiles, tiles)] = next_ref[...]
    held[3 * tiles] = jnp.zeros((chan_local, block_cols), bf16)
    for d in range(groups):
        group = jnp.bitwise_xor(place_ref[0], d)
        for s in range(per):
            rims[d][2 * s] = held[entry_ref[0, group * per + s]]
            rims[d][2 * s + 1] = held[entry_ref[1, group * per + s]]
        rims[d][2 * per] = cols[group * (16 * per) // block_cols]


def rim_places(neighbours, first_slot, block_rows):
    slot_count = neighbours.shape[0]
    tiles = 2 * slot_count + 1
    valid = neighbours >= 0
    slot = jnp.clip(neighbours - first_slot, 0, 3 * slot_count - 1)
    tile_of = slot // slot_count
    place = tile_of * tiles + 2 * (slot - tile_of * slot_count)
    entries = jnp.stack(
        [
            jnp.where(valid[:, 2], place[:, 2] + 1, 3 * tiles),
            jnp.where(valid[:, 3], place[:, 3], 3 * tiles),
        ]
    )
    base = jnp.where(valid, 2 * block_rows * slot, -4 * block_rows)
    last = 2 * (block_rows - 1)
    west = [base[:, 4] + last] + [base[:, 0] + 2 * r for r in range(block_rows)] + [base[:, 6]]
    east = [base[:, 5] + last] + [base[:, 1] + 2 * r for r in range(block_rows)] + [base[:, 7]]
    none = [jnp.full((slot_count,), -1, jnp.int32)] * (8 - block_rows - 2)
    at = jnp.stack(west + none + [e + 1 for e in east] + none, axis=1)
    return entries, at.reshape(1, slot_count * 16)


def rims_of(place, entries, chosen, strips_prev, strips, strips_next, groups):
    tiles, chan_local, block_cols = strips.shape
    per = (tiles - 1) // 2 // groups
    return pl.pallas_call(
        rim_kernel,
        out_shape=(shape((2 * per + 1, chan_local, block_cols)),) * groups,
        in_specs=[SMEM, SMEM, VMEM, VMEM, VMEM, VMEM],
        out_specs=(VMEM,) * groups,
        scratch_shapes=[
            pltpu.VMEM((3 * tiles + 1, chan_local, block_cols), bf16),
            pltpu.VMEM((chosen.shape[1] // block_cols, chan_local, block_cols), bf16),
        ],
        compiler_params=params(),
        name="rims",
    )(place, entries, chosen, strips_prev, strips, strips_next)


def block_kernel(groups, place_ref, *refs):
    body_ref, refs = refs[0], refs[1:]
    rims, refs = refs[:groups], refs[groups:]
    conv_ref, in_ref, out_ref, col_ref, hid_col_ref = refs[:5]
    updates, scratch = refs[5 : 5 + groups], refs[5 + groups :]
    _, per, block_rows, chan_local, block_cols = body_ref.shape
    channels = groups * chan_local
    hidden = in_ref.shape[0]
    me = place_ref[0]
    lane = lax.broadcasted_iota(jnp.int32, (chan_local, block_cols), 1)
    bias = col_ref[:, 0:1]
    gain = col_ref[:, 1:2]
    base = (me * (16 * per)) % block_cols
    rows = [
        pl.multiple_of(jnp.bitwise_xor(me, d) * chan_local, chan_local) for d in range(groups)
    ]
    rim_v, side_v = scratch[6:]
    for d in range(groups):
        source = jnp.bitwise_xor(me, d)
        rim_v[source] = rims[d][...]
        side_v[source] = pltpu.roll(rims[d][2 * per].astype(f32), block_cols - base, 1)
    for s in range(per):
        taken, hid, upd_v = scratch[3 * (s % 2) : 3 * (s % 2) + 3]
        for d in range(groups):
            for p in range(block_rows + 2):
                if p == 0:
                    mid = rim_v[d, 2 * s]
                elif p == block_rows + 1:
                    mid = rim_v[d, 2 * s + 1]
                else:
                    mid = body_ref[d, s, p - 1]
                wide = mid.astype(f32)
                spot = 16 * s + p
                left = jnp.where(
                    lane == 0,
                    pltpu.roll(side_v[d], (block_cols - spot) % block_cols, 1),
                    pltpu.roll(wide, 1, 1),
                ).astype(bf16)
                right = jnp.where(
                    lane == block_cols - 1,
                    pltpu.roll(side_v[d], (2 * block_cols - 1 - spot - 8) % block_cols, 1),
                    pltpu.roll(wide, block_cols - 1, 1),
                ).astype(bf16)
                for a in range(3):
                    i = p - a
                    if 0 <= i < block_rows:
                        for b, piece in enumerate((left, mid, right)):
                            taken[
                                3 * a + b,
                                pl.ds(d * chan_local, chan_local),
                                pl.ds(i * block_cols, block_cols),
                            ] = piece
        columns = taken[...].reshape(9 * channels, block_rows * block_cols)
        conv = ein(conv_ref[...], columns, ((1,), (0,))) + bias
        squares = jnp.sum(conv * conv, axis=0, keepdims=True)
        normed = (conv * lax.rsqrt(squares / channels + norm_eps) * gain).astype(bf16)
        step = min(hidden, 256)
        for h in range(0, hidden, step):
            pre = ein(in_ref[pl.ds(h, step), :], normed, ((1,), (0,)))
            pre = pre + hid_col_ref[pl.ds(h, step), 2:3]
            act = pre * (0.5 * lax.erf(pre * (0.5**0.5)) + 0.5)
            hid[pl.ds(h, step), :] = act.astype(bf16)
        upd_v[...] = ein(out_ref[...], hid[...], ((1,), (0,))).astype(bf16)
        for d in range(groups):
            for i in range(block_rows):
                updates[d][s, i] = upd_v[
                    pl.ds(rows[d], chan_local), pl.ds(i * block_cols, block_cols)
                ]


def block_step(place, bodies, rims, weights):
    groups, per, block_rows, chan_local, block_cols = bodies.shape
    channels = groups * chan_local
    hidden = weights[1].shape[0]
    cells = per * block_rows * block_cols
    return pl.pallas_call(
        functools.partial(block_kernel, groups),
        out_shape=(shape(bodies.shape[1:]),) * groups,
        in_specs=[SMEM] + [VMEM] * (groups + 6),
        out_specs=(VMEM,) * groups,
        scratch_shapes=[
            pltpu.VMEM((9, channels, block_rows * block_cols), bf16),
            pltpu.VMEM((hidden, block_rows * block_cols), bf16),
            pltpu.VMEM((channels, block_rows * block_cols), bf16),
        ]
        * 2
        + [
            pltpu.VMEM((groups,) + rims[0].shape, bf16),
            pltpu.VMEM((groups, chan_local, block_cols), f32),
        ],
        compiler_params=params(24),
        cost_estimate=pl.CostEstimate(
            flops=2 * cells * (9 * channels * channels + 2 * channels * hidden),
            bytes_accessed=8 * 1024 * 1024,
            transcendentals=0,
        ),
        name="block_step",
    )(place, bodies, *rims, *weights)


def forcing_kernel(row_ref, side_ref, wide, out_ref, even, odd):
    slot_count, block_rows, chan_local, block_cols = out_ref.shape
    lanes = wide.shape[2]
    row_at = lax.broadcasted_iota(jnp.int32, (lanes, lanes), 0)
    col_at = lax.broadcasted_iota(jnp.int32, (lanes, lanes), 1)
    eye = (row_at == col_at).astype(f32).astype(bf16)
    count = slot_count * block_rows

    def fetch(q, got):
        for k in range(block_cols):
            got[pl.ds(k, 1), :] = wide[row_ref[q, k]]

    def emit(q, got):
        across = ein(eye, got[...].astype(bf16), ((1,), (1,)))
        side = side_ref[pl.ds(q, 1), :]
        total = across[:chan_local]
        for k in range(1, lanes // chan_local):
            total = jnp.where(side == k, across[k * chan_local : (k + 1) * chan_local], total)
        out_ref[q // block_rows, q % block_rows] = total.astype(bf16)

    fetch(0, even)

    def two(n, _):
        q = 2 * n
        fetch(q + 1, odd)
        emit(q, even)
        fetch(jnp.minimum(q + 2, count - 1), even)
        emit(q + 1, odd)
        return 0

    lax.fori_loop(0, count // 2, two, 0)


def gather_flux(flux):
    count = lax.axis_size("tile")
    if count > 4:
        whole = lax.all_gather(flux, "tile", axis=0)
        me = lax.axis_index("tile")
        return [jnp.take(whole, (me - d) % count, axis=0) for d in range(count)]
    pieces = [flux]
    for d in range(1, count):
        turn = [(i, (i + d) % count) for i in range(count)]
        pieces.append(lax.ppermute(flux, "tile", turn))
    return pieces


def forcing_of(pieces, remap, rows_local, chan_local):
    slot_count, block_rows, block_cols = remap.shape
    count = len(pieces)
    side_by = 128 // chan_local
    part = rows_local // side_by
    target = jnp.clip(remap, 0, count * rows_local - 1).reshape(-1, block_cols)
    tile_of = target // rows_local
    within = target - tile_of * rows_local
    side = within // part
    behind = lax.axis_index("tile") - tile_of
    behind = jnp.where(behind < 0, behind + count, behind)
    row = behind * part + within - side * part
    table = lax.optimization_barrier(jnp.concatenate(pieces, axis=0).astype(f32))[:, None, :]
    return pl.pallas_call(
        forcing_kernel,
        out_shape=shape((slot_count, block_rows, chan_local, block_cols)),
        in_specs=[SMEM, VMEM, VMEM],
        out_specs=VMEM,
        scratch_shapes=[pltpu.VMEM((block_cols, 128), f32)] * 2,
        compiler_params=params(),
        cost_estimate=pl.CostEstimate(
            flops=0, bytes_accessed=32 * 1024 * 1024, transcendentals=0
        ),
        name="forcing",
    )(row, side, table)


def final_kernel(groups, place_ref, *refs):
    xt_ref, updates, rest = refs[0], refs[1 : 1 + groups], refs[1 + groups :]
    forcing_ref, mask_ref, scale_ref, out_ref, piece_v, upd_v, forcing_v, out_v, sems = rest
    per = piece_v.shape[1]
    loads = []
    for d in range(groups):
        first = jnp.bitwise_xor(place_ref[0], d) * per
        loads.append(
            [
                pltpu.make_async_copy(
                    xt_ref.at[pl.ds(first, per)], piece_v.at[d], sems.at[0, d]
                ),
                pltpu.make_async_copy(updates[d], upd_v.at[d], sems.at[1, d]),
                pltpu.make_async_copy(
                    forcing_ref.at[pl.ds(first, per)], forcing_v.at[d], sems.at[2, d]
                ),
            ]
        )
        for load in loads[d]:
            load.start()
    scale = scale_ref[...]
    stores = []
    for d in range(groups):
        first = jnp.bitwise_xor(place_ref[0], d) * per
        for load in loads[d]:
            load.wait()
        for s in range(per):
            total = piece_v[d, s].astype(f32) + scale[None] * upd_v[d, s].astype(f32)
            total = total + forcing_v[d, s].astype(f32)
            total = mask_ref[first + s].astype(f32)[:, None, :] * total
            out_v[d, :, s] = jnp.swapaxes(total, 0, 1).astype(bf16)
        stores.append(
            pltpu.make_async_copy(out_v.at[d], out_ref.at[:, pl.ds(first, per)], sems.at[3, d])
        )
        stores[d].start()
    for store in stores:
        store.wait()


def final_step(place, xt, updates, forcing, cell_mask, layer_scale):
    slot_count, block_rows, chan_local, block_cols = forcing.shape
    groups = len(updates)
    per = slot_count // groups
    return pl.pallas_call(
        functools.partial(final_kernel, groups),
        out_shape=shape((chan_local, slot_count, block_rows, block_cols)),
        in_specs=[SMEM] + [ANY] * (groups + 2) + [VMEM, VMEM],
        out_specs=ANY,
        scratch_shapes=[pltpu.VMEM((groups,) + updates[0].shape, bf16)] * 3
        + [
            pltpu.VMEM((groups, chan_local, per, block_rows, block_cols), bf16),
            pltpu.SemaphoreType.DMA((4, groups)),
        ],
        compiler_params=params(),
        name="final_step",
    )(place, xt, *updates, forcing, cell_mask, layer_scale.astype(f32)[:, None])


def on_device(
    ocean_state,
    atmos,
    flux_weight,
    conv_weight,
    conv_bias,
    norm_gain,
    in_weight,
    in_bias,
    out_weight,
    layer_scale,
    cell_mask,
    neighbours,
    remap,
):
    chan_local, slot_count, block_rows, block_cols = ocean_state.shape
    groups = lax.axis_size(GROUP)
    tile_count = lax.axis_size("tile")
    hid_local = in_weight.shape[1]
    place = jnp.stack([lax.axis_index(GROUP), lax.axis_index("ens")])
    first_slot = (lax.axis_index("tile") - 1) * slot_count

    xt, strips, packed, part = start_step(
        place, groups, ocean_state, conv_weight, conv_bias, norm_gain, in_weight, in_bias, out_weight
    )
    up = [(i, i + 1) for i in range(tile_count - 1)]
    strips_prev = lax.ppermute(strips, "tile", up)
    strips_next = lax.ppermute(strips, "tile", [(b, a) for a, b in up])
    parts, starts = exchange_weights(packed, part)
    bodies = lax.all_to_all(
        xt.reshape((groups, slot_count // groups) + xt.shape[1:]), GROUP, 0, 0, tiled=True
    )
    entries, at = rim_places(neighbours, first_slot, block_rows)
    chosen = onehot_of(at, 3 * block_cols)
    flux = fluxes_of(atmos, flux_weight)
    strips_prev, strips_next, flux = lax.optimization_barrier((strips_prev, strips_next, flux))
    rims = rims_of(place, entries, chosen, strips_prev, strips, strips_next, groups)
    rims = trade(rims)
    table = gather_flux(flux)
    weights = unpack_weights(parts, starts, groups, chan_local, hid_local)
    updates = block_step(place, bodies, rims, weights)
    _, table = lax.optimization_barrier((updates[0], table))
    updates = trade(updates)
    forcing = forcing_of(table, remap, atmos.shape[0], chan_local)
    return final_step(place, xt, updates, forcing, cell_mask, layer_scale)


def solution(mesh):
    placed = (
        P(("chan", "sec"), ("ens", "tile"), None, None),
        P(("ens", "tile"), None),
        P(None, ("chan", "sec")),
        P(None, None, ("chan", "sec")),
        P(("chan", "sec")),
        P(("chan", "sec")),
        P(None, ("chan", "sec")),
        P(("chan", "sec")),
        P(("chan", "sec"), None),
        P(("chan", "sec")),
        P("tile", None, None),
        P("tile", None),
        P("tile", None, None),
    )
    return jax.shard_map(
        on_device,
        mesh=mesh,
        in_specs=placed,
        out_specs=P(("chan", "sec"), ("ens", "tile"), None, None),
        check_vma=False,
    )
```

```python
import functools

import jax
import jax.numpy as jnp
from jax import lax
from jax.experimental import pallas as pl
from jax.experimental.pallas import tpu as pltpu
from jax.sharding import PartitionSpec as P

norm_eps = 1e-06
bf16 = jnp.bfloat16
f32 = jnp.float32
GROUP = ("chan", "sec")
BIAS_ROWS = 32
VMEM = pl.BlockSpec(memory_space=pltpu.VMEM)
SMEM = pl.BlockSpec(memory_space=pltpu.SMEM)
ANY = pl.BlockSpec(memory_space=pl.ANY)


def shape(dims, dtype=bf16):
    return jax.ShapeDtypeStruct(dims, dtype)


def params(mib=20):
    return pltpu.CompilerParams(vmem_limit_bytes=mib * 1024 * 1024)


def ein(a, b, dims):
    return lax.dot_general(a, b, (dims, ((), ())), preferred_element_type=f32)


def start_kernel(chips, *refs):
    state_ref, conv_ref, bias_ref, gain_ref, in_ref, in_bias_ref, out_ref = refs[:7]
    halves, strips_ref, pack_ref, part_ref = refs[7 : 7 + chips], *refs[7 + chips : 10 + chips]
    state_v, conv_v, in_v, out_v, half_v, strips_v, pack_v, sems = refs[10 + chips :]
    _, chan_local, span, block_rows, block_cols = state_v.shape
    taps, _, channels = conv_v.shape
    hid_local = out_v.shape[0]
    chan = lax.axis_index("chan")
    firsts = [jnp.bitwise_xor(chan, c) * span for c in range(chips)]
    loads = [
        pltpu.make_async_copy(
            state_ref.at[:, pl.ds(firsts[c], span)], state_v.at[c], sems.at[c]
        )
        for c in range(chips)
    ]
    copies = [
        pltpu.make_async_copy(conv_ref, conv_v, sems.at[chips]),
        pltpu.make_async_copy(in_ref, in_v, sems.at[chips + 1]),
        pltpu.make_async_copy(out_ref, out_v, sems.at[chips + 2]),
    ]
    for copy in loads + copies:
        copy.start()
    stores = []

    def store(source, target):
        stores.append(pltpu.make_async_copy(source, target, sems.at[chips + 3 + len(stores)]))
        stores[-1].start()

    lane = lax.broadcasted_iota(jnp.int32, (chan_local, block_cols), 1)
    ends = jnp.zeros((chan_local, block_cols), f32)
    for c in range(chips):
        loads[c].wait()
        cols = jnp.zeros((chan_local, block_cols), f32)
        for k in range(span):
            rows = jnp.swapaxes(state_v[c, :, k].astype(f32), 0, 1)
            packed = rows.astype(bf16)
            half_v[c, k] = packed
            strips_v[2 * (firsts[c] + k)] = packed[0]
            strips_v[2 * (firsts[c] + k) + 1] = packed[block_rows - 1]
            for r in range(block_rows):
                spot = 2 * (block_rows * k + r)
                turned = pltpu.roll(rows[r], spot + 1, 1)
                cols = jnp.where((lane == spot) | (lane == spot + 1), turned, cols)
        ends = ends + pltpu.roll(cols, firsts[c] * (2 * block_rows), 1)
        store(half_v.at[c], halves[c])
    strips_v[strips_v.shape[0] - 1] = ends.astype(bf16)
    store(strips_v, strips_ref)

    def widen(ref):
        rows = ref[...].astype(f32)
        row = jnp.concatenate([rows[k : k + 1] for k in range(rows.shape[0])], axis=1)
        if row.shape[1] == channels:
            return row
        return jnp.concatenate([row, jnp.zeros((1, channels - row.shape[1]), f32)], axis=1)

    rest = jnp.zeros((BIAS_ROWS - 3, channels), f32)
    biases = jnp.concatenate(
        [widen(bias_ref), widen(gain_ref), widen(in_bias_ref), rest], axis=0
    )
    at = taps * chan_local
    for copy in copies:
        copy.wait()
    for t in range(taps):
        pack_v[pl.ds(t * chan_local, chan_local), :] = conv_v[t]
    pack_v[pl.ds(at, hid_local), :] = in_v[...].astype(f32).T.astype(bf16)
    pack_v[pl.ds(at + hid_local, hid_local), :] = out_v[...]
    pack_v[pl.ds(at + 2 * hid_local, BIAS_ROWS), :] = biases.astype(bf16)
    part = part_ref.shape[0]
    store(pack_v, pack_ref)
    store(pack_v.at[pl.ds(pl.multiple_of(lax.axis_index("ens") * part, 16), part)], part_ref)
    for copy in stores:
        copy.wait()


def start_step(state, conv_weight, conv_bias, norm_gain, in_weight, in_bias, out_weight):
    chan_local, slot_count, block_rows, block_cols = state.shape
    chips = lax.axis_size("chan")
    span = slot_count // chips
    taps, channels, _ = conv_weight.shape
    hid_local = out_weight.shape[0]
    rows = taps * chan_local + 2 * hid_local + BIAS_ROWS
    half = (span, block_rows, chan_local, block_cols)
    strips = (2 * slot_count + 1, chan_local, block_cols)
    *halves, strips, packed, part = pl.pallas_call(
        functools.partial(start_kernel, chips),
        out_shape=(shape(half),) * chips
        + (shape(strips), shape((rows, channels)), shape((rows // 2, channels))),
        in_specs=[ANY, ANY, VMEM, VMEM, ANY, VMEM, ANY],
        out_specs=(ANY,) * (chips + 3),
        scratch_shapes=[
            pltpu.VMEM((chips, chan_local, span, block_rows, block_cols), bf16),
            pltpu.VMEM((taps, chan_local, channels), bf16),
            pltpu.VMEM((channels, hid_local), bf16),
            pltpu.VMEM((hid_local, channels), bf16),
            pltpu.VMEM((chips,) + half, bf16),
            pltpu.VMEM(strips, bf16),
            pltpu.VMEM((rows, channels), bf16),
            pltpu.SemaphoreType.DMA((2 * chips + 6,)),
        ],
        compiler_params=params(60),
        name="start_step",
    )(
        state,
        conv_weight.transpose(0, 2, 1),
        conv_bias.reshape(-1, min(128, chan_local)),
        norm_gain.reshape(-1, min(128, chan_local)),
        in_weight,
        in_bias.reshape(-1, min(128, hid_local)),
        out_weight,
    )
    return halves, strips, packed, part


def send(piece, d, count):
    return lax.ppermute(piece, GROUP, [(i, i ^ d) for i in range(count)])


def trade(pieces):
    count = len(pieces)
    got = list(pieces)
    for d in list(range(count // 2, count)) + list(range(1, count // 2)):
        got[d] = send(pieces[d], d, count)
    return got


def unpack_kernel(chan_local, hid_local, starts_ref, *refs):
    *pieces, conv_ref, in_ref, out_ref, col_ref, hid_col_ref, all_ref = refs
    groups, rows, channels = all_ref.shape
    unit = min(rows, *(piece.shape[0] for piece in pieces))
    for n, piece in enumerate(pieces):
        for k in range(piece.shape[0] // unit):
            at = starts_ref[n] + k
            parts = rows // unit
            start = pl.multiple_of((at % parts) * unit, 16)
            all_ref[at // parts, pl.ds(start, unit), :] = piece[pl.ds(k * unit, unit), :]
    at = 9 * chan_local
    for j in range(groups):
        for t in range(9):
            conv_ref[pl.ds(j * chan_local, chan_local), pl.ds(t * channels, channels)] = all_ref[
                j, pl.ds(t * chan_local, chan_local), :
            ]
        in_ref[pl.ds(j * hid_local, hid_local), :] = all_ref[j, pl.ds(at, hid_local), :]
        biases = all_ref[j, pl.ds(at + 2 * hid_local, BIAS_ROWS), :].astype(f32)
        across = biases.T
        col_ref[pl.ds(j * chan_local, chan_local), :] = across[:chan_local]
        hid_col_ref[pl.ds(j * hid_local, hid_local), :] = across[:hid_local]
    outs = jnp.concatenate(
        [all_ref[j, pl.ds(at + hid_local, hid_local), :] for j in range(groups)], axis=0
    )
    out_ref[...] = outs.astype(f32).T.astype(bf16)


def unpack_weights(pieces, starts, groups, chan_local, hid_local):
    rows = sum(piece.shape[0] for piece in pieces) // groups
    channels = groups * chan_local
    hidden = groups * hid_local
    return pl.pallas_call(
        functools.partial(unpack_kernel, chan_local, hid_local),
        out_shape=(
            shape((channels, 9 * channels)),
            shape((hidden, channels)),
            shape((channels, hidden)),
            shape((channels, BIAS_ROWS), f32),
            shape((hidden, BIAS_ROWS), f32),
        ),
        in_specs=[SMEM] + [VMEM] * len(pieces),
        out_specs=(VMEM,) * 5,
        scratch_shapes=[pltpu.VMEM((groups, rows, channels), bf16)],
        compiler_params=params(),
        name="unpack_weights",
    )(starts, *pieces)


def swap(value, axis):
    return lax.ppermute(value, axis, [(0, 1), (1, 0)])


def exchange_start(packed, part):
    near = swap(part, "chan")
    near, held = lax.optimization_barrier((near, packed))
    return near, swap(near, "ens"), swap(held, "sec"), swap(near, "sec")


def weight_places():
    ens, chan, sec = (lax.axis_index(name) for name in ("ens", "chan", "sec"))
    own = 2 * (2 * chan + sec)
    beside = 2 * (2 * chan + 1 - sec)
    across = 2 * (2 * (1 - chan) + sec)
    corner = 2 * (2 * (1 - chan) + 1 - sec)
    return jnp.stack([own, beside, across + ens, across + 1 - ens, corner + ens, corner + 1 - ens])


def spread(halves):
    chips = len(halves)
    got = list(halves)
    for c in range(1, chips):
        got[c] = lax.ppermute(halves[c], "chan", [(i, i ^ c) for i in range(chips)])
    return [pair for half in got for pair in (half, swap(half, "sec"))]


def flux_kernel(atmos_ref, weight_ref, out_ref):
    rows, lanes = out_ref.shape
    chan_local, features = weight_ref.shape
    weight = weight_ref[...]
    total = jnp.zeros((rows, lanes), f32)
    for k in range(lanes // chan_local):
        parts = [weight if j == k else jnp.zeros_like(weight) for j in range(lanes // chan_local)]
        wide = jnp.concatenate(parts, axis=0)
        total = total + ein(atmos_ref[pl.ds(k * rows, rows), :], wide, ((1,), (1,)))
    out_ref[...] = total.astype(bf16)


def fluxes_of(atmos, flux_weight):
    side = 128 // flux_weight.shape[1]
    return pl.pallas_call(
        flux_kernel,
        out_shape=shape((atmos.shape[0] // side, 128)),
        in_specs=[VMEM, VMEM],
        out_specs=VMEM,
        compiler_params=params(),
        name="fluxes",
    )(atmos, flux_weight.T)


def onehot_kernel(at_ref, out_ref):
    spot = lax.broadcasted_iota(jnp.int32, out_ref.shape, 0)
    out_ref[...] = (spot == at_ref[...]).astype(f32).astype(bf16)


def onehot_of(at, rows):
    return pl.pallas_call(
        onehot_kernel,
        out_shape=shape((rows, at.shape[1])),
        in_specs=[VMEM],
        out_specs=VMEM,
        compiler_params=params(),
        name="onehot",
    )(at)


def rim_kernel(place_ref, entry_ref, chosen_ref, prev_ref, own_ref, next_ref, *refs):
    *rims, held, cols = refs
    tiles, chan_local, block_cols = own_ref.shape
    groups = len(rims)
    slot_count = (tiles - 1) // 2
    per = slot_count // groups
    ends = jnp.concatenate(
        [prev_ref[tiles - 1], own_ref[tiles - 1], next_ref[tiles - 1]], axis=1
    )
    picked = ein(ends, chosen_ref[...], ((1,), (0,))).astype(bf16)
    for k in range(cols.shape[0]):
        cols[k] = picked[:, k * block_cols : (k + 1) * block_cols]
    held[pl.ds(0, tiles)] = prev_ref[...]
    held[pl.ds(tiles, tiles)] = own_ref[...]
    held[pl.ds(2 * tiles, tiles)] = next_ref[...]
    held[3 * tiles] = jnp.zeros((chan_local, block_cols), bf16)
    for d in range(groups):
        group = jnp.bitwise_xor(place_ref[0], d)
        for s in range(per):
            rims[d][2 * s] = held[entry_ref[0, group * per + s]]
            rims[d][2 * s + 1] = held[entry_ref[1, group * per + s]]
        rims[d][2 * per] = cols[group * (16 * per) // block_cols]


def rim_places(neighbours, first_slot, block_rows):
    slot_count = neighbours.shape[0]
    tiles = 2 * slot_count + 1
    valid = neighbours >= 0
    slot = jnp.clip(neighbours - first_slot, 0, 3 * slot_count - 1)
    tile_of = slot // slot_count
    place = tile_of * tiles + 2 * (slot - tile_of * slot_count)
    entries = jnp.stack(
        [
            jnp.where(valid[:, 2], place[:, 2] + 1, 3 * tiles),
            jnp.where(valid[:, 3], place[:, 3], 3 * tiles),
        ]
    )
    base = jnp.where(valid, 2 * block_rows * slot, -4 * block_rows)
    last = 2 * (block_rows - 1)
    west = [base[:, 4] + last] + [base[:, 0] + 2 * r for r in range(block_rows)] + [base[:, 6]]
    east = [base[:, 5] + last] + [base[:, 1] + 2 * r for r in range(block_rows)] + [base[:, 7]]
    none = [jnp.full((slot_count,), -1, jnp.int32)] * (8 - block_rows - 2)
    at = jnp.stack(west + none + [e + 1 for e in east] + none, axis=1)
    return entries, at.reshape(1, slot_count * 16)


def rims_of(place, entries, chosen, strips_prev, strips, strips_next, groups):
    tiles, chan_local, block_cols = strips.shape
    per = (tiles - 1) // 2 // groups
    return pl.pallas_call(
        rim_kernel,
        out_shape=(shape((2 * per + 1, chan_local, block_cols)),) * groups,
        in_specs=[SMEM, SMEM, VMEM, VMEM, VMEM, VMEM],
        out_specs=(VMEM,) * groups,
        scratch_shapes=[
            pltpu.VMEM((3 * tiles + 1, chan_local, block_cols), bf16),
            pltpu.VMEM((chosen.shape[1] // block_cols, chan_local, block_cols), bf16),
        ],
        compiler_params=params(),
        name="rims",
    )(place, entries, chosen, strips_prev, strips, strips_next)


def block_kernel(groups, place_ref, *refs):
    bodies, refs = refs[:groups], refs[groups:]
    rims, refs = refs[:groups], refs[groups:]
    conv_ref, in_ref, out_ref, col_ref, hid_col_ref = refs[:5]
    updates, scratch = refs[5 : 5 + groups], refs[5 + groups :]
    per = (rims[0].shape[0] - 1) // 2
    _, block_rows, chan_local, block_cols = bodies[0].shape
    channels = groups * chan_local
    hidden = in_ref.shape[0]
    me = place_ref[0]
    lane = lax.broadcasted_iota(jnp.int32, (chan_local, block_cols), 1)
    bias = col_ref[:, 0:1]
    gain = col_ref[:, 1:2]
    base = (me * (16 * per)) % block_cols
    rows = [
        pl.multiple_of(jnp.bitwise_xor(me, d) * chan_local, chan_local) for d in range(groups)
    ]
    rim_v, side_v, body_v = scratch[6:]
    first = me % (bodies[0].shape[0] // per) * per
    for d in range(groups):
        source = jnp.bitwise_xor(me, d)
        rim_v[source] = rims[d][...]
        body_v[source] = bodies[d][pl.ds(first, per)]
        side_v[source] = pltpu.roll(rims[d][2 * per].astype(f32), block_cols - base, 1)
    for s in range(per):
        taken, hid, upd_v = scratch[3 * (s % 2) : 3 * (s % 2) + 3]
        for d in range(groups):
            for p in range(block_rows + 2):
                if p == 0:
                    mid = rim_v[d, 2 * s]
                elif p == block_rows + 1:
                    mid = rim_v[d, 2 * s + 1]
                else:
                    mid = body_v[d, s, p - 1]
                wide = mid.astype(f32)
                spot = 16 * s + p
                left = jnp.where(
                    lane == 0,
                    pltpu.roll(side_v[d], (block_cols - spot) % block_cols, 1),
                    pltpu.roll(wide, 1, 1),
                ).astype(bf16)
                right = jnp.where(
                    lane == block_cols - 1,
                    pltpu.roll(side_v[d], (2 * block_cols - 1 - spot - 8) % block_cols, 1),
                    pltpu.roll(wide, block_cols - 1, 1),
                ).astype(bf16)
                for a in range(3):
                    i = p - a
                    if 0 <= i < block_rows:
                        for b, piece in enumerate((left, mid, right)):
                            taken[
                                3 * a + b,
                                pl.ds(d * chan_local, chan_local),
                                pl.ds(i * block_cols, block_cols),
                            ] = piece
        columns = taken[...].reshape(9 * channels, block_rows * block_cols)
        conv = ein(conv_ref[...], columns, ((1,), (0,))) + bias
        squares = jnp.sum(conv * conv, axis=0, keepdims=True)
        normed = (conv * lax.rsqrt(squares / channels + norm_eps) * gain).astype(bf16)
        step = min(hidden, 256)
        for h in range(0, hidden, step):
            pre = ein(in_ref[pl.ds(h, step), :], normed, ((1,), (0,)))
            pre = pre + hid_col_ref[pl.ds(h, step), 2:3]
            act = pre * (0.5 * lax.erf(pre * (0.5**0.5)) + 0.5)
            hid[pl.ds(h, step), :] = act.astype(bf16)
        upd_v[...] = ein(out_ref[...], hid[...], ((1,), (0,))).astype(bf16)
        for d in range(groups):
            for i in range(block_rows):
                updates[d][s, i] = upd_v[
                    pl.ds(rows[d], chan_local), pl.ds(i * block_cols, block_cols)
                ]


def block_step(place, bodies, rims, weights):
    groups = len(bodies)
    per = (rims[0].shape[0] - 1) // 2
    _, block_rows, chan_local, block_cols = bodies[0].shape
    piece = (per, block_rows, chan_local, block_cols)
    channels = groups * chan_local
    hidden = weights[1].shape[0]
    cells = per * block_rows * block_cols
    return pl.pallas_call(
        functools.partial(block_kernel, groups),
        out_shape=(shape(piece),) * groups,
        in_specs=[SMEM] + [VMEM] * (2 * groups + 5),
        out_specs=(VMEM,) * groups,
        scratch_shapes=[
            pltpu.VMEM((9, channels, block_rows * block_cols), bf16),
            pltpu.VMEM((hidden, block_rows * block_cols), bf16),
            pltpu.VMEM((channels, block_rows * block_cols), bf16),
        ]
        * 2
        + [
            pltpu.VMEM((groups,) + rims[0].shape, bf16),
            pltpu.VMEM((groups, chan_local, block_cols), f32),
            pltpu.VMEM((groups,) + piece, bf16),
        ],
        compiler_params=params(24),
        cost_estimate=pl.CostEstimate(
            flops=2 * cells * (9 * channels * channels + 2 * channels * hidden),
            bytes_accessed=8 * 1024 * 1024,
            transcendentals=0,
        ),
        name="block_step",
    )(place, *bodies, *rims, *weights)


def forcing_kernel(row_ref, side_ref, wide, out_ref, even, odd):
    slot_count, block_rows, chan_local, block_cols = out_ref.shape
    lanes = wide.shape[2]
    row_at = lax.broadcasted_iota(jnp.int32, (lanes, lanes), 0)
    col_at = lax.broadcasted_iota(jnp.int32, (lanes, lanes), 1)
    eye = (row_at == col_at).astype(f32).astype(bf16)
    count = slot_count * block_rows

    def fetch(q, got):
        for k in range(block_cols):
            got[pl.ds(k, 1), :] = wide[row_ref[q, k]]

    def emit(q, got):
        across = ein(eye, got[...].astype(bf16), ((1,), (1,)))
        side = side_ref[pl.ds(q, 1), :]
        total = across[:chan_local]
        for k in range(1, lanes // chan_local):
            total = jnp.where(side == k, across[k * chan_local : (k + 1) * chan_local], total)
        out_ref[q // block_rows, q % block_rows] = total.astype(bf16)

    fetch(0, even)

    def two(n, _):
        q = 2 * n
        fetch(q + 1, odd)
        emit(q, even)
        fetch(jnp.minimum(q + 2, count - 1), even)
        emit(q + 1, odd)
        return 0

    lax.fori_loop(0, count // 2, two, 0)


def gather_flux(flux):
    count = lax.axis_size("tile")
    if count > 4:
        whole = lax.all_gather(flux, "tile", axis=0)
        me = lax.axis_index("tile")
        return [jnp.take(whole, (me - d) % count, axis=0) for d in range(count)]
    pieces = [flux]
    for d in range(1, count):
        turn = [(i, (i + d) % count) for i in range(count)]
        pieces.append(lax.ppermute(flux, "tile", turn))
    return pieces


def forcing_of(pieces, remap, rows_local, chan_local):
    slot_count, block_rows, block_cols = remap.shape
    count = len(pieces)
    side_by = 128 // chan_local
    part = rows_local // side_by
    target = jnp.clip(remap, 0, count * rows_local - 1).reshape(-1, block_cols)
    tile_of = target // rows_local
    within = target - tile_of * rows_local
    side = within // part
    behind = lax.axis_index("tile") - tile_of
    behind = jnp.where(behind < 0, behind + count, behind)
    row = behind * part + within - side * part
    table = lax.optimization_barrier(jnp.concatenate(pieces, axis=0).astype(f32))[:, None, :]
    return pl.pallas_call(
        forcing_kernel,
        out_shape=shape((slot_count, block_rows, chan_local, block_cols)),
        in_specs=[SMEM, VMEM, VMEM],
        out_specs=VMEM,
        scratch_shapes=[pltpu.VMEM((block_cols, 128), f32)] * 2,
        compiler_params=params(),
        cost_estimate=pl.CostEstimate(
            flops=0, bytes_accessed=32 * 1024 * 1024, transcendentals=0
        ),
        name="forcing",
    )(row, side, table)


def final_kernel(chips, groups, place_ref, *refs):
    halves, updates = refs[:chips], refs[chips : chips + groups]
    forcing_ref, mask_ref, scale_ref, out_ref, piece_v, upd_v, forcing_v, out_v, sems = refs[
        chips + groups :
    ]
    per = piece_v.shape[1]
    cores = groups // chips
    loads = []
    for d in range(groups):
        group = jnp.bitwise_xor(place_ref[0], d)
        loads.append(
            [
                pltpu.make_async_copy(
                    halves[d // cores].at[pl.ds(group % cores * per, per)],
                    piece_v.at[d],
                    sems.at[0, d],
                ),
                pltpu.make_async_copy(updates[d], upd_v.at[d], sems.at[1, d]),
                pltpu.make_async_copy(
                    forcing_ref.at[pl.ds(group * per, per)], forcing_v.at[d], sems.at[2, d]
                ),
            ]
        )
        for load in loads[d]:
            load.start()
    scale = scale_ref[...]
    stores = []
    for d in range(groups):
        first = jnp.bitwise_xor(place_ref[0], d) * per
        for load in loads[d]:
            load.wait()
        for s in range(per):
            total = piece_v[d, s].astype(f32) + scale[None] * upd_v[d, s].astype(f32)
            total = total + forcing_v[d, s].astype(f32)
            total = mask_ref[first + s].astype(f32)[:, None, :] * total
            out_v[d, :, s] = jnp.swapaxes(total, 0, 1).astype(bf16)
        stores.append(
            pltpu.make_async_copy(out_v.at[d], out_ref.at[:, pl.ds(first, per)], sems.at[3, d])
        )
        stores[d].start()
    for store in stores:
        store.wait()


def final_step(place, halves, updates, forcing, cell_mask, layer_scale):
    slot_count, block_rows, chan_local, block_cols = forcing.shape
    groups = len(updates)
    per = slot_count // groups
    return pl.pallas_call(
        functools.partial(final_kernel, len(halves), groups),
        out_shape=shape((chan_local, slot_count, block_rows, block_cols)),
        in_specs=[SMEM] + [ANY] * (len(halves) + groups + 1) + [VMEM, VMEM],
        out_specs=ANY,
        scratch_shapes=[pltpu.VMEM((groups,) + updates[0].shape, bf16)] * 3
        + [
            pltpu.VMEM((groups, chan_local, per, block_rows, block_cols), bf16),
            pltpu.SemaphoreType.DMA((4, groups)),
        ],
        compiler_params=params(),
        name="final_step",
    )(place, *halves, *updates, forcing, cell_mask, layer_scale.astype(f32)[:, None])


def on_device(
    ocean_state,
    atmos,
    flux_weight,
    conv_weight,
    conv_bias,
    norm_gain,
    in_weight,
    in_bias,
    out_weight,
    layer_scale,
    cell_mask,
    neighbours,
    remap,
):
    chan_local, slot_count, block_rows, block_cols = ocean_state.shape
    groups = lax.axis_size(GROUP)
    tile_count = lax.axis_size("tile")
    hid_local = in_weight.shape[1]
    place = lax.axis_index(GROUP)[None]
    first_slot = (lax.axis_index("tile") - 1) * slot_count

    halves, strips, packed, part = start_step(
        ocean_state, conv_weight, conv_bias, norm_gain, in_weight, in_bias, out_weight
    )
    up = [(i, i + 1) for i in range(tile_count - 1)]
    strips_prev = lax.ppermute(strips, "tile", up)
    strips_next = lax.ppermute(strips, "tile", [(b, a) for a, b in up])
    staged = lax.axis_size("ens") == 2 and lax.axis_size("chan") == 2
    if staged:
        near, far, beside, near_beside = exchange_start(packed, part)
    bodies = spread(halves)
    entries, at = rim_places(neighbours, first_slot, block_rows)
    chosen = onehot_of(at, 3 * block_cols)
    flux = fluxes_of(atmos, flux_weight)
    strips_prev, strips_next, flux = lax.optimization_barrier((strips_prev, strips_next, flux))
    rims = rims_of(place, entries, chosen, strips_prev, strips, strips_next, groups)
    if staged:
        far, *rims = lax.optimization_barrier((far, *rims))
    rims = trade(rims)
    table = gather_flux(flux)
    if staged:
        parts = [packed, beside, near, far, near_beside, swap(far, "sec")]
        starts = weight_places()
    else:
        parts = [lax.all_gather(packed, GROUP, axis=0, tiled=True)]
        starts = jnp.zeros((1,), jnp.int32)
    weights = unpack_weights(parts, starts, groups, chan_local, hid_local)
    updates = block_step(place, bodies, rims, weights)
    _, table = lax.optimization_barrier((updates[0], table))
    updates = trade(updates)
    forcing = forcing_of(table, remap, atmos.shape[0], chan_local)
    return final_step(place, halves, updates, forcing, cell_mask, layer_scale)


def solution(mesh):
    placed = (
        P(("chan", "sec"), ("ens", "tile"), None, None),
        P(("ens", "tile"), None),
        P(None, ("chan", "sec")),
        P(None, None, ("chan", "sec")),
        P(("chan", "sec")),
        P(("chan", "sec")),
        P(None, ("chan", "sec")),
        P(("chan", "sec")),
        P(("chan", "sec"), None),
        P(("chan", "sec")),
        P("tile", None, None),
        P("tile", None),
        P("tile", None, None),
    )
    return jax.shard_map(
        on_device,
        mesh=mesh,
        in_specs=placed,
        out_specs=P(("chan", "sec"), ("ens", "tile"), None, None),
        check_vma=False,
    )
```

```python
import functools

import jax
import jax.numpy as jnp
from jax import lax
from jax.experimental import pallas as pl
from jax.experimental.pallas import tpu as pltpu
from jax.sharding import PartitionSpec as P

norm_eps = 1e-06
bf16 = jnp.bfloat16
f32 = jnp.float32
GROUP = ("chan", "sec")
BIAS_ROWS = 32
VMEM = pl.BlockSpec(memory_space=pltpu.VMEM)
SMEM = pl.BlockSpec(memory_space=pltpu.SMEM)
ANY = pl.BlockSpec(memory_space=pl.ANY)


def shape(dims, dtype=bf16):
    return jax.ShapeDtypeStruct(dims, dtype)


def params(mib=20):
    return pltpu.CompilerParams(vmem_limit_bytes=mib * 1024 * 1024)


def ein(a, b, dims):
    return lax.dot_general(a, b, (dims, ((), ())), preferred_element_type=f32)


def start_kernel(chips, *refs):
    state_ref, conv_ref, bias_ref, gain_ref, in_ref, in_bias_ref, out_ref = refs[:7]
    halves, strips_ref, pack_ref, part_ref = refs[7 : 7 + chips], *refs[7 + chips : 10 + chips]
    state_v, conv_v, in_v, out_v, half_v, strips_v, pack_v, sems = refs[10 + chips :]
    _, chan_local, span, block_rows, block_cols = state_v.shape
    taps, _, channels = conv_v.shape
    hid_local = out_v.shape[0]
    chan = lax.axis_index("chan")
    firsts = [jnp.bitwise_xor(chan, c) * span for c in range(chips)]
    loads = [
        pltpu.make_async_copy(
            state_ref.at[:, pl.ds(firsts[c], span)], state_v.at[c], sems.at[c]
        )
        for c in range(chips)
    ]
    copies = [
        pltpu.make_async_copy(conv_ref, conv_v, sems.at[chips]),
        pltpu.make_async_copy(in_ref, in_v, sems.at[chips + 1]),
        pltpu.make_async_copy(out_ref, out_v, sems.at[chips + 2]),
    ]
    for copy in loads + copies:
        copy.start()
    stores = []

    def store(source, target):
        stores.append(pltpu.make_async_copy(source, target, sems.at[chips + 3 + len(stores)]))
        stores[-1].start()

    lane = lax.broadcasted_iota(jnp.int32, (chan_local, block_cols), 1)
    ends = jnp.zeros((chan_local, block_cols), f32)
    for c in range(chips):
        loads[c].wait()
        cols = jnp.zeros((chan_local, block_cols), f32)
        for k in range(span):
            rows = jnp.swapaxes(state_v[c, :, k].astype(f32), 0, 1)
            packed = rows.astype(bf16)
            half_v[c, k] = packed
            strips_v[2 * (firsts[c] + k)] = packed[0]
            strips_v[2 * (firsts[c] + k) + 1] = packed[block_rows - 1]
            for r in range(block_rows):
                spot = 2 * (block_rows * k + r)
                turned = pltpu.roll(rows[r], spot + 1, 1)
                cols = jnp.where((lane == spot) | (lane == spot + 1), turned, cols)
        ends = ends + pltpu.roll(cols, firsts[c] * (2 * block_rows), 1)
        store(half_v.at[c], halves[c])
    strips_v[strips_v.shape[0] - 1] = ends.astype(bf16)
    store(strips_v, strips_ref)

    def widen(ref):
        rows = ref[...].astype(f32)
        row = jnp.concatenate([rows[k : k + 1] for k in range(rows.shape[0])], axis=1)
        if row.shape[1] == channels:
            return row
        return jnp.concatenate([row, jnp.zeros((1, channels - row.shape[1]), f32)], axis=1)

    rest = jnp.zeros((BIAS_ROWS - 3, channels), f32)
    biases = jnp.concatenate(
        [widen(bias_ref), widen(gain_ref), widen(in_bias_ref), rest], axis=0
    )
    at = taps * chan_local
    for copy in copies:
        copy.wait()
    for t in range(taps):
        pack_v[pl.ds(t * chan_local, chan_local), :] = conv_v[t]
    pack_v[pl.ds(at, hid_local), :] = in_v[...].astype(f32).T.astype(bf16)
    pack_v[pl.ds(at + hid_local, hid_local), :] = out_v[...]
    pack_v[pl.ds(at + 2 * hid_local, BIAS_ROWS), :] = biases.astype(bf16)
    part = part_ref.shape[0]
    store(pack_v, pack_ref)
    store(pack_v.at[pl.ds(pl.multiple_of(lax.axis_index("ens") * part, 16), part)], part_ref)
    for copy in stores:
        copy.wait()


def start_step(state, conv_weight, conv_bias, norm_gain, in_weight, in_bias, out_weight):
    chan_local, slot_count, block_rows, block_cols = state.shape
    chips = lax.axis_size("chan")
    span = slot_count // chips
    taps, channels, _ = conv_weight.shape
    hid_local = out_weight.shape[0]
    rows = taps * chan_local + 2 * hid_local + BIAS_ROWS
    half = (span, block_rows, chan_local, block_cols)
    strips = (2 * slot_count + 1, chan_local, block_cols)
    *halves, strips, packed, part = pl.pallas_call(
        functools.partial(start_kernel, chips),
        out_shape=(shape(half),) * chips
        + (shape(strips), shape((rows, channels)), shape((rows // 2, channels))),
        in_specs=[ANY, ANY, VMEM, VMEM, ANY, VMEM, ANY],
        out_specs=(ANY,) * (chips + 3),
        scratch_shapes=[
            pltpu.VMEM((chips, chan_local, span, block_rows, block_cols), bf16),
            pltpu.VMEM((taps, chan_local, channels), bf16),
            pltpu.VMEM((channels, hid_local), bf16),
            pltpu.VMEM((hid_local, channels), bf16),
            pltpu.VMEM((chips,) + half, bf16),
            pltpu.VMEM(strips, bf16),
            pltpu.VMEM((rows, channels), bf16),
            pltpu.SemaphoreType.DMA((2 * chips + 6,)),
        ],
        compiler_params=params(60),
        name="start_step",
    )(
        state,
        conv_weight.transpose(0, 2, 1),
        conv_bias.reshape(-1, min(128, chan_local)),
        norm_gain.reshape(-1, min(128, chan_local)),
        in_weight,
        in_bias.reshape(-1, min(128, hid_local)),
        out_weight,
    )
    return halves, strips, packed, part


def send(piece, d, count):
    return lax.ppermute(piece, GROUP, [(i, i ^ d) for i in range(count)])


def trade(pieces):
    count = len(pieces)
    got = list(pieces)
    for d in list(range(count // 2, count)) + list(range(1, count // 2)):
        got[d] = send(pieces[d], d, count)
    return got


def unpack_kernel(chan_local, hid_local, starts_ref, *refs):
    *pieces, conv_ref, in_ref, out_ref, col_ref, hid_col_ref, all_ref = refs
    groups, rows, channels = all_ref.shape
    unit = 0
    for piece in pieces:
        for k in range(piece.shape[0] // rows):
            all_ref[starts_ref[unit]] = piece[pl.ds(k * rows, rows), :]
            unit += 1
    at = 9 * chan_local
    for j in range(groups):
        for t in range(9):
            conv_ref[pl.ds(j * chan_local, chan_local), pl.ds(t * channels, channels)] = all_ref[
                j, pl.ds(t * chan_local, chan_local), :
            ]
        in_ref[pl.ds(j * hid_local, hid_local), :] = all_ref[j, pl.ds(at, hid_local), :]
        biases = all_ref[j, pl.ds(at + 2 * hid_local, BIAS_ROWS), :].astype(f32)
        across = biases.T
        col_ref[pl.ds(j * chan_local, chan_local), :] = across[:chan_local]
        hid_col_ref[pl.ds(j * hid_local, hid_local), :] = across[:hid_local]
    outs = jnp.concatenate(
        [all_ref[j, pl.ds(at + hid_local, hid_local), :] for j in range(groups)], axis=0
    )
    out_ref[...] = outs.astype(f32).T.astype(bf16)


def unpack_weights(pieces, starts, groups, chan_local, hid_local):
    rows = sum(piece.shape[0] for piece in pieces) // groups
    channels = groups * chan_local
    hidden = groups * hid_local
    return pl.pallas_call(
        functools.partial(unpack_kernel, chan_local, hid_local),
        out_shape=(
            shape((channels, 9 * channels)),
            shape((hidden, channels)),
            shape((channels, hidden)),
            shape((channels, BIAS_ROWS), f32),
            shape((hidden, BIAS_ROWS), f32),
        ),
        in_specs=[SMEM] + [VMEM] * len(pieces),
        out_specs=(VMEM,) * 5,
        scratch_shapes=[pltpu.VMEM((groups, rows, channels), bf16)],
        compiler_params=params(),
        name="unpack_weights",
    )(starts, *pieces)


def swap(value, axis):
    return lax.ppermute(value, axis, [(0, 1), (1, 0)])


def merge_kernel(
    packed_ref, near_ref, far_ref, flux_ref, got_ref, _, _r, all_ref, both_ref, sems
):
    rows, part, lines = packed_ref.shape[0], near_ref.shape[0], flux_ref.shape[0]
    ens = lax.axis_index("ens")
    here = pl.multiple_of(rows + ens * part, 16)
    there = pl.multiple_of(rows + (1 - ens) * part, 16)
    copies = [
        pltpu.make_async_copy(packed_ref, all_ref.at[pl.ds(0, rows)], sems.at[0]),
        pltpu.make_async_copy(near_ref, all_ref.at[pl.ds(here, part)], sems.at[1]),
        pltpu.make_async_copy(far_ref, all_ref.at[pl.ds(there, part)], sems.at[2]),
        pltpu.make_async_copy(flux_ref, both_ref.at[pl.ds(0, lines)], sems.at[3]),
        pltpu.make_async_copy(got_ref, both_ref.at[pl.ds(lines, lines)], sems.at[4]),
    ]
    for copy in copies:
        copy.start()
    for copy in copies:
        copy.wait()


def merge(packed, near, far, flux, got, after):
    return pl.pallas_call(
        merge_kernel,
        out_shape=(
            shape((2 * packed.shape[0], packed.shape[1])),
            shape((2 * flux.shape[0], flux.shape[1])),
        ),
        in_specs=[ANY] * 7,
        out_specs=(ANY, ANY),
        scratch_shapes=[pltpu.SemaphoreType.DMA((5,))],
        compiler_params=params(),
        name="merge",
    )(packed, near, far, flux, got, *after)


def cross(halves):
    chips = len(halves)
    return [halves[0]] + [
        lax.ppermute(halves[c], "chan", [(i, i ^ c) for i in range(chips)])
        for c in range(1, chips)
    ]


def flux_kernel(atmos_ref, weight_ref, out_ref):
    rows, lanes = out_ref.shape
    chan_local, features = weight_ref.shape
    weight = weight_ref[...]
    total = jnp.zeros((rows, lanes), f32)
    for k in range(lanes // chan_local):
        parts = [weight if j == k else jnp.zeros_like(weight) for j in range(lanes // chan_local)]
        wide = jnp.concatenate(parts, axis=0)
        total = total + ein(atmos_ref[pl.ds(k * rows, rows), :], wide, ((1,), (1,)))
    out_ref[...] = total.astype(bf16)


def fluxes_of(atmos, flux_weight):
    side = 128 // flux_weight.shape[1]
    return pl.pallas_call(
        flux_kernel,
        out_shape=shape((atmos.shape[0] // side, 128)),
        in_specs=[VMEM, VMEM],
        out_specs=VMEM,
        compiler_params=params(),
        name="fluxes",
    )(atmos, flux_weight.T)


def onehot_kernel(at_ref, out_ref):
    spot = lax.broadcasted_iota(jnp.int32, out_ref.shape, 0)
    out_ref[...] = (spot == at_ref[...]).astype(f32).astype(bf16)


def onehot_of(at, rows):
    return pl.pallas_call(
        onehot_kernel,
        out_shape=shape((rows, at.shape[1])),
        in_specs=[VMEM],
        out_specs=VMEM,
        compiler_params=params(),
        name="onehot",
    )(at)


def rim_kernel(place_ref, entry_ref, chosen_ref, prev_ref, own_ref, next_ref, *refs):
    *rims, held, cols = refs
    tiles, chan_local, block_cols = own_ref.shape
    groups = len(rims)
    slot_count = (tiles - 1) // 2
    per = slot_count // groups
    ends = jnp.concatenate(
        [prev_ref[tiles - 1], own_ref[tiles - 1], next_ref[tiles - 1]], axis=1
    )
    picked = ein(ends, chosen_ref[...], ((1,), (0,))).astype(bf16)
    for k in range(cols.shape[0]):
        cols[k] = picked[:, k * block_cols : (k + 1) * block_cols]
    held[pl.ds(0, tiles)] = prev_ref[...]
    held[pl.ds(tiles, tiles)] = own_ref[...]
    held[pl.ds(2 * tiles, tiles)] = next_ref[...]
    held[3 * tiles] = jnp.zeros((chan_local, block_cols), bf16)
    for d in range(groups):
        group = jnp.bitwise_xor(place_ref[0], d)
        for s in range(per):
            rims[d][2 * s] = held[entry_ref[0, group * per + s]]
            rims[d][2 * s + 1] = held[entry_ref[1, group * per + s]]
        rims[d][2 * per] = cols[group * (16 * per) // block_cols]


def rim_places(neighbours, first_slot, block_rows):
    slot_count = neighbours.shape[0]
    tiles = 2 * slot_count + 1
    valid = neighbours >= 0
    slot = jnp.clip(neighbours - first_slot, 0, 3 * slot_count - 1)
    tile_of = slot // slot_count
    place = tile_of * tiles + 2 * (slot - tile_of * slot_count)
    entries = jnp.stack(
        [
            jnp.where(valid[:, 2], place[:, 2] + 1, 3 * tiles),
            jnp.where(valid[:, 3], place[:, 3], 3 * tiles),
        ]
    )
    base = jnp.where(valid, 2 * block_rows * slot, -4 * block_rows)
    last = 2 * (block_rows - 1)
    west = [base[:, 4] + last] + [base[:, 0] + 2 * r for r in range(block_rows)] + [base[:, 6]]
    east = [base[:, 5] + last] + [base[:, 1] + 2 * r for r in range(block_rows)] + [base[:, 7]]
    none = [jnp.full((slot_count,), -1, jnp.int32)] * (8 - block_rows - 2)
    at = jnp.stack(west + none + [e + 1 for e in east] + none, axis=1)
    return entries, at.reshape(1, slot_count * 16)


def rims_of(place, entries, chosen, strips_prev, strips, strips_next, groups):
    tiles, chan_local, block_cols = strips.shape
    per = (tiles - 1) // 2 // groups
    return pl.pallas_call(
        rim_kernel,
        out_shape=(shape((2 * per + 1, chan_local, block_cols)),) * groups,
        in_specs=[SMEM, SMEM, VMEM, VMEM, VMEM, VMEM],
        out_specs=(VMEM,) * groups,
        scratch_shapes=[
            pltpu.VMEM((3 * tiles + 1, chan_local, block_cols), bf16),
            pltpu.VMEM((chosen.shape[1] // block_cols, chan_local, block_cols), bf16),
        ],
        compiler_params=params(),
        name="rims",
    )(place, entries, chosen, strips_prev, strips, strips_next)


def block_kernel(groups, start, place_ref, *refs):
    bodies, refs = refs[:groups], refs[groups:]
    rims, refs = refs[:groups], refs[groups:]
    conv_ref, in_ref, out_ref, col_ref, hid_col_ref = refs[:5]
    updates, scratch = refs[5 : 5 + groups], refs[5 + groups :]
    count = updates[0].shape[0]
    per = (rims[0].shape[0] - 1) // 2
    _, block_rows, chan_local, block_cols = bodies[0].shape
    channels = groups * chan_local
    hidden = in_ref.shape[0]
    me = place_ref[0]
    lane = lax.broadcasted_iota(jnp.int32, (chan_local, block_cols), 1)
    bias = col_ref[:, 0:1]
    gain = col_ref[:, 1:2]
    base = (me * (16 * per)) % block_cols
    rows = [
        pl.multiple_of(jnp.bitwise_xor(me, d) * chan_local, chan_local) for d in range(groups)
    ]
    rim_v, side_v, body_v = scratch[6:]
    first = me % (bodies[0].shape[0] // per) * per + start
    for d in range(groups):
        source = jnp.bitwise_xor(me, d)
        rim_v[source] = rims[d][pl.ds(2 * start, 2 * count)]
        body_v[source] = bodies[d][pl.ds(first, count)]
        side_v[source] = pltpu.roll(rims[d][2 * per].astype(f32), block_cols - base, 1)
    for s in range(count):
        taken, hid, upd_v = scratch[3 * (s % 2) : 3 * (s % 2) + 3]
        for d in range(groups):
            for p in range(block_rows + 2):
                if p == 0:
                    mid = rim_v[d, 2 * s]
                elif p == block_rows + 1:
                    mid = rim_v[d, 2 * s + 1]
                else:
                    mid = body_v[d, s, p - 1]
                wide = mid.astype(f32)
                spot = 16 * (start + s) + p
                left = jnp.where(
                    lane == 0,
                    pltpu.roll(side_v[d], (block_cols - spot) % block_cols, 1),
                    pltpu.roll(wide, 1, 1),
                ).astype(bf16)
                right = jnp.where(
                    lane == block_cols - 1,
                    pltpu.roll(side_v[d], (2 * block_cols - 1 - spot - 8) % block_cols, 1),
                    pltpu.roll(wide, block_cols - 1, 1),
                ).astype(bf16)
                for a in range(3):
                    i = p - a
                    if 0 <= i < block_rows:
                        for b, piece in enumerate((left, mid, right)):
                            taken[
                                3 * a + b,
                                pl.ds(d * chan_local, chan_local),
                                pl.ds(i * block_cols, block_cols),
                            ] = piece
        columns = taken[...].reshape(9 * channels, block_rows * block_cols)
        conv = ein(conv_ref[...], columns, ((1,), (0,))) + bias
        squares = jnp.sum(conv * conv, axis=0, keepdims=True)
        normed = (conv * lax.rsqrt(squares / channels + norm_eps) * gain).astype(bf16)
        step = min(hidden, 256)
        for h in range(0, hidden, step):
            pre = ein(in_ref[pl.ds(h, step), :], normed, ((1,), (0,)))
            pre = pre + hid_col_ref[pl.ds(h, step), 2:3]
            act = pre * (0.5 * lax.erf(pre * (0.5**0.5)) + 0.5)
            hid[pl.ds(h, step), :] = act.astype(bf16)
        upd_v[...] = ein(out_ref[...], hid[...], ((1,), (0,))).astype(bf16)
        for d in range(groups):
            for i in range(block_rows):
                updates[d][s, i] = upd_v[
                    pl.ds(rows[d], chan_local), pl.ds(i * block_cols, block_cols)
                ]


def block_step(start, count, place, bodies, rims, weights):
    groups = len(bodies)
    _, block_rows, chan_local, block_cols = bodies[0].shape
    piece = (count, block_rows, chan_local, block_cols)
    channels = groups * chan_local
    hidden = weights[1].shape[0]
    cells = count * block_rows * block_cols
    return pl.pallas_call(
        functools.partial(block_kernel, groups, start),
        out_shape=(shape(piece),) * groups,
        in_specs=[SMEM] + [VMEM] * (2 * groups + 5),
        out_specs=(VMEM,) * groups,
        scratch_shapes=[
            pltpu.VMEM((9, channels, block_rows * block_cols), bf16),
            pltpu.VMEM((hidden, block_rows * block_cols), bf16),
            pltpu.VMEM((channels, block_rows * block_cols), bf16),
        ]
        * 2
        + [
            pltpu.VMEM((groups, 2 * count, chan_local, block_cols), bf16),
            pltpu.VMEM((groups, chan_local, block_cols), f32),
            pltpu.VMEM((groups,) + piece, bf16),
        ],
        compiler_params=params(24),
        cost_estimate=pl.CostEstimate(
            flops=2 * cells * (9 * channels * channels + 2 * channels * hidden),
            bytes_accessed=8 * 1024 * 1024,
            transcendentals=0,
        ),
        name="block_step",
    )(place, *bodies, *rims, *weights)


def forcing_kernel(row_ref, side_ref, wide, out_ref, even, odd):
    slot_count, block_rows, chan_local, block_cols = out_ref.shape
    lanes = wide.shape[2]
    row_at = lax.broadcasted_iota(jnp.int32, (lanes, lanes), 0)
    col_at = lax.broadcasted_iota(jnp.int32, (lanes, lanes), 1)
    eye = (row_at == col_at).astype(f32).astype(bf16)
    count = slot_count * block_rows

    def fetch(q, got):
        for k in range(block_cols):
            got[pl.ds(k, 1), :] = wide[row_ref[q, k]]

    def emit(q, got):
        across = ein(eye, got[...].astype(bf16), ((1,), (1,)))
        side = side_ref[pl.ds(q, 1), :]
        total = across[:chan_local]
        for k in range(1, lanes // chan_local):
            total = jnp.where(side == k, across[k * chan_local : (k + 1) * chan_local], total)
        out_ref[q // block_rows, q % block_rows] = total.astype(bf16)

    fetch(0, even)

    def two(n, _):
        q = 2 * n
        fetch(q + 1, odd)
        emit(q, even)
        fetch(jnp.minimum(q + 2, count - 1), even)
        emit(q + 1, odd)
        return 0

    lax.fori_loop(0, count // 2, two, 0)


def flux_hop(block, bit):
    count = lax.axis_size("tile")
    return lax.ppermute(block, "tile", [(i, i ^ bit) for i in range(count)])


def forcing_of(table, remap, rows_local, chan_local):
    slot_count, block_rows, block_cols = remap.shape
    count = lax.axis_size("tile")
    side_by = 128 // chan_local
    part = rows_local // side_by
    target = jnp.clip(remap, 0, count * rows_local - 1).reshape(-1, block_cols)
    tile_of = target // rows_local
    within = target - tile_of * rows_local
    side = within // part
    rest = jnp.bitwise_xor(tile_of, lax.axis_index("tile"))
    block = jnp.zeros_like(rest)
    bit = 1
    while bit < count:
        block = 2 * block + rest % 2
        rest = rest // 2
        bit *= 2
    row = block * part + within - side * part
    table = lax.optimization_barrier(table.astype(f32))[:, None, :]
    return pl.pallas_call(
        forcing_kernel,
        out_shape=shape((slot_count, block_rows, chan_local, block_cols)),
        in_specs=[SMEM, VMEM, VMEM],
        out_specs=VMEM,
        scratch_shapes=[pltpu.VMEM((block_cols, 128), f32)] * 2,
        compiler_params=params(),
        cost_estimate=pl.CostEstimate(
            flops=0, bytes_accessed=32 * 1024 * 1024, transcendentals=0
        ),
        name="forcing",
    )(row, side, table)


def final_kernel(chips, groups, parts, place_ref, *refs):
    halves, updates = refs[:chips], refs[chips : chips + groups * parts]
    forcing_ref, mask_ref, scale_ref, out_ref, piece_v, upd_v, forcing_v, out_v, sems = refs[
        chips + groups * parts :
    ]
    per = piece_v.shape[1]
    count = per // parts
    cores = groups // chips
    loads = []
    for d in range(groups):
        group = jnp.bitwise_xor(place_ref[0], d)
        loads.append(
            [
                pltpu.make_async_copy(
                    halves[d // cores].at[pl.ds(group % cores * per, per)],
                    piece_v.at[d],
                    sems.at[0, d],
                ),
                pltpu.make_async_copy(
                    forcing_ref.at[pl.ds(group * per, per)], forcing_v.at[d], sems.at[1, d]
                ),
            ]
            + [
                pltpu.make_async_copy(
                    updates[h * groups + d],
                    upd_v.at[d, pl.ds(h * count, count)],
                    sems.at[3 + h, d],
                )
                for h in range(parts)
            ]
        )
        for load in loads[d]:
            load.start()
    scale = scale_ref[...]
    stores = []
    for d in range(groups):
        first = jnp.bitwise_xor(place_ref[0], d) * per
        for load in loads[d]:
            load.wait()
        for s in range(per):
            total = piece_v[d, s].astype(f32) + scale[None] * upd_v[d, s].astype(f32)
            total = total + forcing_v[d, s].astype(f32)
            total = mask_ref[first + s].astype(f32)[:, None, :] * total
            out_v[d, :, s] = jnp.swapaxes(total, 0, 1).astype(bf16)
        stores.append(
            pltpu.make_async_copy(out_v.at[d], out_ref.at[:, pl.ds(first, per)], sems.at[2, d])
        )
        stores[d].start()
    for store in stores:
        store.wait()


def final_step(place, halves, updates, forcing, cell_mask, layer_scale):
    slot_count, block_rows, chan_local, block_cols = forcing.shape
    parts = len(updates)
    groups = len(updates[0])
    per = slot_count // groups
    piece = (groups, per, block_rows, chan_local, block_cols)
    return pl.pallas_call(
        functools.partial(final_kernel, len(halves), groups, parts),
        out_shape=shape((chan_local, slot_count, block_rows, block_cols)),
        in_specs=[SMEM] + [ANY] * (len(halves) + groups * parts + 1) + [VMEM, VMEM],
        out_specs=ANY,
        scratch_shapes=[pltpu.VMEM(piece, bf16)] * 3
        + [
            pltpu.VMEM((groups, chan_local, per, block_rows, block_cols), bf16),
            pltpu.SemaphoreType.DMA((3 + parts, groups)),
        ],
        compiler_params=params(),
        name="final_step",
    )(
        place,
        *halves,
        *[piece for update in updates for piece in update],
        forcing,
        cell_mask,
        layer_scale.astype(f32)[:, None],
    )


def on_device(
    ocean_state,
    atmos,
    flux_weight,
    conv_weight,
    conv_bias,
    norm_gain,
    in_weight,
    in_bias,
    out_weight,
    layer_scale,
    cell_mask,
    neighbours,
    remap,
):
    chan_local, slot_count, block_rows, block_cols = ocean_state.shape
    groups = lax.axis_size(GROUP)
    tile_count = lax.axis_size("tile")
    hid_local = in_weight.shape[1]
    place = lax.axis_index(GROUP)[None]
    first_slot = (lax.axis_index("tile") - 1) * slot_count

    halves, strips, packed, part = start_step(
        ocean_state, conv_weight, conv_bias, norm_gain, in_weight, in_bias, out_weight
    )
    up = [(i, i + 1) for i in range(tile_count - 1)]
    strips_prev = lax.ppermute(strips, "tile", up)
    strips_next = lax.ppermute(strips, "tile", [(b, a) for a, b in up])
    crossed = cross(halves)
    entries, at = rim_places(neighbours, first_slot, block_rows)
    chosen = onehot_of(at, 3 * block_cols)
    rims = rims_of(place, entries, chosen, strips_prev, strips, strips_next, groups)
    flux = fluxes_of(atmos, flux_weight)
    bit = tile_count // 2
    got = flux_hop(flux, bit)
    if lax.axis_size("ens") == 2 and lax.axis_size("chan") == 2:
        near = swap(part, "chan")
        far = swap(near, "ens")
        merged, table = merge(
            packed, near, far, flux, got, (rims[0], crossed[1])
        )
        parts = [merged, swap(merged, "sec")]
        chan, sec = lax.axis_index("chan"), lax.axis_index("sec")
        own, across = 2 * chan + sec, 2 * (1 - chan) + sec
        starts = jnp.stack(
            [own, across, jnp.bitwise_xor(own, 1), jnp.bitwise_xor(across, 1)]
        )
    else:
        parts = [lax.all_gather(packed, GROUP, axis=0, tiled=True)]
        starts = jnp.arange(groups, dtype=jnp.int32)
        table = jnp.concatenate([flux, got], axis=0)
    while bit > 1:
        bit //= 2
        table = jnp.concatenate([table, flux_hop(table, bit)], axis=0)
    bodies = [pair for half in crossed for pair in (half, swap(half, "sec"))]
    rims = trade(rims)
    weights = unpack_weights(parts, starts, groups, chan_local, hid_local)
    per = slot_count // groups
    count = per // 2 if per % 2 == 0 else per
    updates = [
        trade(block_step(start, count, place, bodies, rims, weights))
        for start in range(0, per, count)
    ]
    forcing = forcing_of(table, remap, atmos.shape[0], chan_local)
    return final_step(place, halves, updates, forcing, cell_mask, layer_scale)


def solution(mesh):
    placed = (
        P(("chan", "sec"), ("ens", "tile"), None, None),
        P(("ens", "tile"), None),
        P(None, ("chan", "sec")),
        P(None, None, ("chan", "sec")),
        P(("chan", "sec")),
        P(("chan", "sec")),
        P(None, ("chan", "sec")),
        P(("chan", "sec")),
        P(("chan", "sec"), None),
        P(("chan", "sec")),
        P("tile", None, None),
        P("tile", None),
        P("tile", None, None),
    )
    return jax.shard_map(
        on_device,
        mesh=mesh,
        in_specs=placed,
        out_specs=P(("chan", "sec"), ("ens", "tile"), None, None),
        check_vma=False,
    )
```

```python
import functools

import jax
import jax.numpy as jnp
from jax import lax
from jax.experimental import pallas as pl
from jax.experimental.pallas import tpu as pltpu
from jax.sharding import PartitionSpec as P

norm_eps = 1e-06
bf16 = jnp.bfloat16
f32 = jnp.float32
GROUP = ("chan", "sec")
BIAS_ROWS = 32
VMEM = pl.BlockSpec(memory_space=pltpu.VMEM)
SMEM = pl.BlockSpec(memory_space=pltpu.SMEM)
ANY = pl.BlockSpec(memory_space=pl.ANY)


def shape(dims, dtype=bf16):
    return jax.ShapeDtypeStruct(dims, dtype)


def params(mib=20):
    return pltpu.CompilerParams(vmem_limit_bytes=mib * 1024 * 1024)


def ein(a, b, dims):
    return lax.dot_general(a, b, (dims, ((), ())), preferred_element_type=f32)


def start_kernel(*refs):
    state_ref, conv_ref, bias_ref, gain_ref, in_ref, in_bias_ref, out_ref = refs[:7]
    xt_ref, strips_ref, pack_ref, part_ref = refs[7:11]
    state_v, conv_v, in_v, out_v, half_v, strips_v, pack_v, sems = refs[11:]
    chunks, chan_local, span, block_rows, block_cols = state_v.shape
    taps, _, channels = conv_v.shape
    hid_local = out_v.shape[0]
    loads = [
        pltpu.make_async_copy(
            state_ref.at[:, pl.ds(c * span, span)], state_v.at[c], sems.at[c]
        )
        for c in range(chunks)
    ]
    copies = [
        pltpu.make_async_copy(conv_ref, conv_v, sems.at[chunks]),
        pltpu.make_async_copy(in_ref, in_v, sems.at[chunks + 1]),
        pltpu.make_async_copy(out_ref, out_v, sems.at[chunks + 2]),
    ]
    for copy in loads + copies:
        copy.start()
    stores = []

    def store(source, target):
        stores.append(pltpu.make_async_copy(source, target, sems.at[chunks + 3 + len(stores)]))
        stores[-1].start()

    lane = lax.broadcasted_iota(jnp.int32, (chan_local, block_cols), 1)
    ends = jnp.zeros((chan_local, block_cols), f32)
    for c in range(chunks):
        loads[c].wait()
        for k in range(span):
            rows = jnp.swapaxes(state_v[c, :, k].astype(f32), 0, 1)
            packed = rows.astype(bf16)
            half_v[c, k] = packed
            slot = c * span + k
            strips_v[2 * slot] = packed[0]
            strips_v[2 * slot + 1] = packed[block_rows - 1]
            for r in range(block_rows):
                spot = 2 * (block_rows * slot + r)
                turned = pltpu.roll(rows[r], spot + 1, 1)
                ends = jnp.where((lane == spot) | (lane == spot + 1), turned, ends)
        store(half_v.at[c], xt_ref.at[pl.ds(c * span, span)])
    strips_v[strips_v.shape[0] - 1] = ends.astype(bf16)
    store(strips_v, strips_ref)

    def widen(ref):
        rows = ref[...].astype(f32)
        row = jnp.concatenate([rows[k : k + 1] for k in range(rows.shape[0])], axis=1)
        if row.shape[1] == channels:
            return row
        return jnp.concatenate([row, jnp.zeros((1, channels - row.shape[1]), f32)], axis=1)

    rest = jnp.zeros((BIAS_ROWS - 3, channels), f32)
    biases = jnp.concatenate(
        [widen(bias_ref), widen(gain_ref), widen(in_bias_ref), rest], axis=0
    )
    at = taps * chan_local
    for copy in copies:
        copy.wait()
    for t in range(taps):
        pack_v[pl.ds(t * chan_local, chan_local), :] = conv_v[t]
    pack_v[pl.ds(at, hid_local), :] = in_v[...].astype(f32).T.astype(bf16)
    pack_v[pl.ds(at + hid_local, hid_local), :] = out_v[...]
    pack_v[pl.ds(at + 2 * hid_local, BIAS_ROWS), :] = biases.astype(bf16)
    part = part_ref.shape[0]
    store(pack_v, pack_ref)
    store(pack_v.at[pl.ds(pl.multiple_of(lax.axis_index("ens") * part, 16), part)], part_ref)
    for copy in stores:
        copy.wait()


def start_step(state, conv_weight, conv_bias, norm_gain, in_weight, in_bias, out_weight):
    chan_local, slot_count, block_rows, block_cols = state.shape
    chunks = 4
    span = slot_count // chunks
    taps, channels, _ = conv_weight.shape
    hid_local = out_weight.shape[0]
    rows = taps * chan_local + 2 * hid_local + BIAS_ROWS
    half = (span, block_rows, chan_local, block_cols)
    strips = (2 * slot_count + 1, chan_local, block_cols)
    return pl.pallas_call(
        start_kernel,
        out_shape=(shape((slot_count,) + half[1:]),)
        + (shape(strips), shape((rows, channels)), shape((rows // 2, channels))),
        in_specs=[ANY, ANY, VMEM, VMEM, ANY, VMEM, ANY],
        out_specs=(ANY,) * 4,
        scratch_shapes=[
            pltpu.VMEM((chunks, chan_local, span, block_rows, block_cols), bf16),
            pltpu.VMEM((taps, chan_local, channels), bf16),
            pltpu.VMEM((channels, hid_local), bf16),
            pltpu.VMEM((hid_local, channels), bf16),
            pltpu.VMEM((chunks,) + half, bf16),
            pltpu.VMEM(strips, bf16),
            pltpu.VMEM((rows, channels), bf16),
            pltpu.SemaphoreType.DMA((2 * chunks + 6,)),
        ],
        compiler_params=params(60),
        name="start_step",
    )(
        state,
        conv_weight.transpose(0, 2, 1),
        conv_bias.reshape(-1, min(128, chan_local)),
        norm_gain.reshape(-1, min(128, chan_local)),
        in_weight,
        in_bias.reshape(-1, min(128, hid_local)),
        out_weight,
    )


def send(piece, d, count):
    return lax.ppermute(piece, GROUP, [(i, i ^ d) for i in range(count)])


def trade(pieces):
    count = len(pieces)
    got = list(pieces)
    for d in list(range(count // 2, count)) + list(range(1, count // 2)):
        got[d] = send(pieces[d], d, count)
    return got


def unpack_kernel(count, chan_local, hid_local, starts_ref, *refs):
    pieces = refs[:count]
    *_, conv_ref, in_ref, out_ref, col_ref, hid_col_ref, all_ref = refs
    groups, rows, channels = all_ref.shape
    unit = min(rows, *(piece.shape[0] for piece in pieces))
    for n, piece in enumerate(pieces):
        for k in range(piece.shape[0] // unit):
            at = starts_ref[n] + k
            parts = rows // unit
            start = pl.multiple_of((at % parts) * unit, 16)
            all_ref[at // parts, pl.ds(start, unit), :] = piece[pl.ds(k * unit, unit), :]
    at = 9 * chan_local
    for j in range(groups):
        for t in range(9):
            conv_ref[pl.ds(j * chan_local, chan_local), pl.ds(t * channels, channels)] = all_ref[
                j, pl.ds(t * chan_local, chan_local), :
            ]
        in_ref[pl.ds(j * hid_local, hid_local), :] = all_ref[j, pl.ds(at, hid_local), :]
        biases = all_ref[j, pl.ds(at + 2 * hid_local, BIAS_ROWS), :].astype(f32)
        across = biases.T
        col_ref[pl.ds(j * chan_local, chan_local), :] = across[:chan_local]
        hid_col_ref[pl.ds(j * hid_local, hid_local), :] = across[:hid_local]
    outs = jnp.concatenate(
        [all_ref[j, pl.ds(at + hid_local, hid_local), :] for j in range(groups)], axis=0
    )
    out_ref[...] = outs.astype(f32).T.astype(bf16)


def unpack_weights(pieces, starts, groups, chan_local, hid_local, after):
    rows = sum(piece.shape[0] for piece in pieces) // groups
    channels = groups * chan_local
    hidden = groups * hid_local
    return pl.pallas_call(
        functools.partial(unpack_kernel, len(pieces), chan_local, hid_local),
        out_shape=(
            shape((channels, 9 * channels)),
            shape((hidden, channels)),
            shape((channels, hidden)),
            shape((channels, BIAS_ROWS), f32),
            shape((hidden, BIAS_ROWS), f32),
        ),
        in_specs=[SMEM] + [VMEM] * len(pieces) + [ANY],
        out_specs=(VMEM,) * 5,
        scratch_shapes=[pltpu.VMEM((groups, rows, channels), bf16)],
        compiler_params=params(),
        name="unpack_weights",
    )(starts, *pieces, after)


def swap(value, axis):
    return lax.ppermute(value, axis, [(0, 1), (1, 0)])


def gate_kernel(*refs):
    pass


def gate(values, *after):
    count = len(values)
    return pl.pallas_call(
        gate_kernel,
        out_shape=tuple(shape(value.shape) for value in values),
        in_specs=[ANY] * (count + len(after)),
        out_specs=(ANY,) * count,
        input_output_aliases={k: k for k in range(count)},
        compiler_params=params(),
        name="gate",
    )(*values, *after)


def weight_places():
    ens, chan, sec = (lax.axis_index(name) for name in ("ens", "chan", "sec"))
    own = 2 * (2 * chan + sec)
    beside = 2 * (2 * chan + 1 - sec)
    across = 2 * (2 * (1 - chan) + sec)
    corner = 2 * (2 * (1 - chan) + 1 - sec)
    return jnp.stack([own, beside, across + ens, across + 1 - ens, corner + ens, corner + 1 - ens])


def flux_kernel(atmos_ref, weight_ref, out_ref):
    rows, lanes = out_ref.shape
    chan_local, features = weight_ref.shape
    weight = weight_ref[...]
    total = jnp.zeros((rows, lanes), f32)
    for k in range(lanes // chan_local):
        parts = [weight if j == k else jnp.zeros_like(weight) for j in range(lanes // chan_local)]
        wide = jnp.concatenate(parts, axis=0)
        total = total + ein(atmos_ref[pl.ds(k * rows, rows), :], wide, ((1,), (1,)))
    out_ref[...] = total.astype(bf16)


def fluxes_of(atmos, flux_weight):
    side = 128 // flux_weight.shape[1]
    return pl.pallas_call(
        flux_kernel,
        out_shape=shape((atmos.shape[0] // side, 128)),
        in_specs=[VMEM, VMEM],
        out_specs=VMEM,
        compiler_params=params(),
        name="fluxes",
    )(atmos, flux_weight.T)


def onehot_kernel(at_ref, out_ref):
    spot = lax.broadcasted_iota(jnp.int32, out_ref.shape, 0)
    out_ref[...] = (spot == at_ref[...]).astype(f32).astype(bf16)


def onehot_of(at, rows):
    return pl.pallas_call(
        onehot_kernel,
        out_shape=shape((rows, at.shape[1])),
        in_specs=[VMEM],
        out_specs=VMEM,
        compiler_params=params(),
        name="onehot",
    )(at)


def rim_kernel(place_ref, entry_ref, chosen_ref, prev_ref, own_ref, next_ref, *refs):
    *rims, held, cols = refs
    tiles, chan_local, block_cols = own_ref.shape
    groups = len(rims)
    slot_count = (tiles - 1) // 2
    per = slot_count // groups
    ends = jnp.concatenate(
        [prev_ref[tiles - 1], own_ref[tiles - 1], next_ref[tiles - 1]], axis=1
    )
    picked = ein(ends, chosen_ref[...], ((1,), (0,))).astype(bf16)
    for k in range(cols.shape[0]):
        cols[k] = picked[:, k * block_cols : (k + 1) * block_cols]
    held[pl.ds(0, tiles)] = prev_ref[...]
    held[pl.ds(tiles, tiles)] = own_ref[...]
    held[pl.ds(2 * tiles, tiles)] = next_ref[...]
    held[3 * tiles] = jnp.zeros((chan_local, block_cols), bf16)
    for d in range(groups):
        group = jnp.bitwise_xor(place_ref[0], d)
        for s in range(per):
            rims[d][2 * s] = held[entry_ref[0, group * per + s]]
            rims[d][2 * s + 1] = held[entry_ref[1, group * per + s]]
        rims[d][2 * per] = cols[group * (16 * per) // block_cols]


def rim_places(neighbours, first_slot, block_rows):
    slot_count = neighbours.shape[0]
    tiles = 2 * slot_count + 1
    valid = neighbours >= 0
    slot = jnp.clip(neighbours - first_slot, 0, 3 * slot_count - 1)
    tile_of = slot // slot_count
    place = tile_of * tiles + 2 * (slot - tile_of * slot_count)
    entries = jnp.stack(
        [
            jnp.where(valid[:, 2], place[:, 2] + 1, 3 * tiles),
            jnp.where(valid[:, 3], place[:, 3], 3 * tiles),
        ]
    )
    base = jnp.where(valid, 2 * block_rows * slot, -4 * block_rows)
    last = 2 * (block_rows - 1)
    west = [base[:, 4] + last] + [base[:, 0] + 2 * r for r in range(block_rows)] + [base[:, 6]]
    east = [base[:, 5] + last] + [base[:, 1] + 2 * r for r in range(block_rows)] + [base[:, 7]]
    none = [jnp.full((slot_count,), -1, jnp.int32)] * (8 - block_rows - 2)
    at = jnp.stack(west + none + [e + 1 for e in east] + none, axis=1)
    return entries, at.reshape(1, slot_count * 16)


def rims_of(place, entries, chosen, strips_prev, strips, strips_next, groups):
    tiles, chan_local, block_cols = strips.shape
    per = (tiles - 1) // 2 // groups
    return pl.pallas_call(
        rim_kernel,
        out_shape=(shape((2 * per + 1, chan_local, block_cols)),) * groups,
        in_specs=[SMEM, SMEM, VMEM, VMEM, VMEM, VMEM],
        out_specs=(VMEM,) * groups,
        scratch_shapes=[
            pltpu.VMEM((3 * tiles + 1, chan_local, block_cols), bf16),
            pltpu.VMEM((chosen.shape[1] // block_cols, chan_local, block_cols), bf16),
        ],
        compiler_params=params(),
        name="rims",
    )(place, entries, chosen, strips_prev, strips, strips_next)


def block_kernel(groups, place_ref, *refs):
    body_ref, refs = refs[0], refs[1:]
    rims, refs = refs[:groups], refs[groups:]
    conv_ref, in_ref, out_ref, col_ref, hid_col_ref = refs[:5]
    updates, scratch = refs[5 : 5 + groups], refs[5 + groups :]
    _, per, block_rows, chan_local, block_cols = body_ref.shape
    channels = groups * chan_local
    hidden = in_ref.shape[0]
    me = place_ref[0]
    lane = lax.broadcasted_iota(jnp.int32, (chan_local, block_cols), 1)
    bias = col_ref[:, 0:1]
    gain = col_ref[:, 1:2]
    base = (me * (16 * per)) % block_cols
    rows = [
        pl.multiple_of(jnp.bitwise_xor(me, d) * chan_local, chan_local) for d in range(groups)
    ]
    rim_v, side_v = scratch[6:]
    for d in range(groups):
        source = jnp.bitwise_xor(me, d)
        rim_v[source] = rims[d][...]
        side_v[source] = pltpu.roll(rims[d][2 * per].astype(f32), block_cols - base, 1)
    for s in range(per):
        taken, hid, upd_v = scratch[3 * (s % 2) : 3 * (s % 2) + 3]
        for d in range(groups):
            for p in range(block_rows + 2):
                if p == 0:
                    mid = rim_v[d, 2 * s]
                elif p == block_rows + 1:
                    mid = rim_v[d, 2 * s + 1]
                else:
                    mid = body_ref[d, s, p - 1]
                wide = mid.astype(f32)
                spot = 16 * s + p
                left = jnp.where(
                    lane == 0,
                    pltpu.roll(side_v[d], (block_cols - spot) % block_cols, 1),
                    pltpu.roll(wide, 1, 1),
                ).astype(bf16)
                right = jnp.where(
                    lane == block_cols - 1,
                    pltpu.roll(side_v[d], (2 * block_cols - 1 - spot - 8) % block_cols, 1),
                    pltpu.roll(wide, block_cols - 1, 1),
                ).astype(bf16)
                for a in range(3):
                    i = p - a
                    if 0 <= i < block_rows:
                        for b, piece in enumerate((left, mid, right)):
                            taken[
                                3 * a + b,
                                pl.ds(d * chan_local, chan_local),
                                pl.ds(i * block_cols, block_cols),
                            ] = piece
        columns = taken[...].reshape(9 * channels, block_rows * block_cols)
        conv = ein(conv_ref[...], columns, ((1,), (0,))) + bias
        squares = jnp.sum(conv * conv, axis=0, keepdims=True)
        normed = (conv * lax.rsqrt(squares / channels + norm_eps) * gain).astype(bf16)
        step = min(hidden, 256)
        for h in range(0, hidden, step):
            pre = ein(in_ref[pl.ds(h, step), :], normed, ((1,), (0,)))
            pre = pre + hid_col_ref[pl.ds(h, step), 2:3]
            act = pre * (0.5 * lax.erf(pre * (0.5**0.5)) + 0.5)
            hid[pl.ds(h, step), :] = act.astype(bf16)
        upd_v[...] = ein(out_ref[...], hid[...], ((1,), (0,))).astype(bf16)
        for d in range(groups):
            for i in range(block_rows):
                updates[d][s, i] = upd_v[
                    pl.ds(rows[d], chan_local), pl.ds(i * block_cols, block_cols)
                ]


def block_step(place, bodies, rims, weights):
    groups, per, block_rows, chan_local, block_cols = bodies.shape
    channels = groups * chan_local
    hidden = weights[1].shape[0]
    cells = per * block_rows * block_cols
    return pl.pallas_call(
        functools.partial(block_kernel, groups),
        out_shape=(shape(bodies.shape[1:]),) * groups,
        in_specs=[SMEM] + [VMEM] * (groups + 6),
        out_specs=(VMEM,) * groups,
        scratch_shapes=[
            pltpu.VMEM((9, channels, block_rows * block_cols), bf16),
            pltpu.VMEM((hidden, block_rows * block_cols), bf16),
            pltpu.VMEM((channels, block_rows * block_cols), bf16),
        ]
        * 2
        + [
            pltpu.VMEM((groups,) + rims[0].shape, bf16),
            pltpu.VMEM((groups, chan_local, block_cols), f32),
        ],
        compiler_params=params(24),
        cost_estimate=pl.CostEstimate(
            flops=2 * cells * (9 * channels * channels + 2 * channels * hidden),
            bytes_accessed=8 * 1024 * 1024,
            transcendentals=0,
        ),
        name="block_step",
    )(place, bodies, *rims, *weights)


def forcing_kernel(row_ref, side_ref, wide, out_ref, even, odd):
    slot_count, block_rows, chan_local, block_cols = out_ref.shape
    lanes = wide.shape[2]
    row_at = lax.broadcasted_iota(jnp.int32, (lanes, lanes), 0)
    col_at = lax.broadcasted_iota(jnp.int32, (lanes, lanes), 1)
    eye = (row_at == col_at).astype(f32).astype(bf16)
    count = slot_count * block_rows

    def fetch(q, got):
        for k in range(block_cols):
            got[pl.ds(k, 1), :] = wide[row_ref[q, k]]

    def emit(q, got):
        across = ein(eye, got[...].astype(bf16), ((1,), (1,)))
        side = side_ref[pl.ds(q, 1), :]
        total = across[:chan_local]
        for k in range(1, lanes // chan_local):
            total = jnp.where(side == k, across[k * chan_local : (k + 1) * chan_local], total)
        out_ref[q // block_rows, q % block_rows] = total.astype(bf16)

    fetch(0, even)

    def two(n, _):
        q = 2 * n
        fetch(q + 1, odd)
        emit(q, even)
        fetch(jnp.minimum(q + 2, count - 1), even)
        emit(q + 1, odd)
        return 0

    lax.fori_loop(0, count // 2, two, 0)


def gather_flux(flux):
    count = lax.axis_size("tile")
    if count > 4:
        whole = lax.all_gather(flux, "tile", axis=0)
        me = lax.axis_index("tile")
        return [jnp.take(whole, (me - d) % count, axis=0) for d in range(count)]
    pieces = [flux]
    for d in range(1, count):
        turn = [(i, (i + d) % count) for i in range(count)]
        pieces.append(lax.ppermute(flux, "tile", turn))
    return pieces


def forcing_of(pieces, remap, rows_local, chan_local):
    slot_count, block_rows, block_cols = remap.shape
    count = len(pieces)
    side_by = 128 // chan_local
    part = rows_local // side_by
    target = jnp.clip(remap, 0, count * rows_local - 1).reshape(-1, block_cols)
    tile_of = target // rows_local
    within = target - tile_of * rows_local
    side = within // part
    behind = lax.axis_index("tile") - tile_of
    behind = jnp.where(behind < 0, behind + count, behind)
    row = behind * part + within - side * part
    table = lax.optimization_barrier(jnp.concatenate(pieces, axis=0).astype(f32))[:, None, :]
    return pl.pallas_call(
        forcing_kernel,
        out_shape=shape((slot_count, block_rows, chan_local, block_cols)),
        in_specs=[SMEM, VMEM, VMEM],
        out_specs=VMEM,
        scratch_shapes=[pltpu.VMEM((block_cols, 128), f32)] * 2,
        compiler_params=params(),
        cost_estimate=pl.CostEstimate(
            flops=0, bytes_accessed=32 * 1024 * 1024, transcendentals=0
        ),
        name="forcing",
    )(row, side, table)


def final_kernel(groups, place_ref, *refs):
    xt_ref, updates, rest = refs[0], refs[1 : 1 + groups], refs[1 + groups :]
    forcing_ref, mask_ref, scale_ref, out_ref, piece_v, upd_v, forcing_v, out_v, sems = rest
    per = piece_v.shape[1]
    loads = []
    for d in range(groups):
        first = jnp.bitwise_xor(place_ref[0], d) * per
        loads.append(
            [
                pltpu.make_async_copy(
                    xt_ref.at[pl.ds(first, per)], piece_v.at[d], sems.at[0, d]
                ),
                pltpu.make_async_copy(updates[d], upd_v.at[d], sems.at[1, d]),
                pltpu.make_async_copy(
                    forcing_ref.at[pl.ds(first, per)], forcing_v.at[d], sems.at[2, d]
                ),
            ]
        )
        for load in loads[d]:
            load.start()
    scale = scale_ref[...]
    stores = []
    for d in range(groups):
        first = jnp.bitwise_xor(place_ref[0], d) * per
        for load in loads[d]:
            load.wait()
        for s in range(per):
            total = piece_v[d, s].astype(f32) + scale[None] * upd_v[d, s].astype(f32)
            total = total + forcing_v[d, s].astype(f32)
            total = mask_ref[first + s].astype(f32)[:, None, :] * total
            out_v[d, :, s] = jnp.swapaxes(total, 0, 1).astype(bf16)
        stores.append(
            pltpu.make_async_copy(out_v.at[d], out_ref.at[:, pl.ds(first, per)], sems.at[3, d])
        )
        stores[d].start()
    for store in stores:
        store.wait()


def final_step(place, xt, updates, forcing, cell_mask, layer_scale):
    slot_count, block_rows, chan_local, block_cols = forcing.shape
    groups = len(updates)
    per = slot_count // groups
    return pl.pallas_call(
        functools.partial(final_kernel, groups),
        out_shape=shape((chan_local, slot_count, block_rows, block_cols)),
        in_specs=[SMEM] + [ANY] * (groups + 2) + [VMEM, VMEM],
        out_specs=ANY,
        scratch_shapes=[pltpu.VMEM((groups,) + updates[0].shape, bf16)] * 3
        + [
            pltpu.VMEM((groups, chan_local, per, block_rows, block_cols), bf16),
            pltpu.SemaphoreType.DMA((4, groups)),
        ],
        compiler_params=params(),
        name="final_step",
    )(place, xt, *updates, forcing, cell_mask, layer_scale.astype(f32)[:, None])


def on_device(
    ocean_state,
    atmos,
    flux_weight,
    conv_weight,
    conv_bias,
    norm_gain,
    in_weight,
    in_bias,
    out_weight,
    layer_scale,
    cell_mask,
    neighbours,
    remap,
):
    chan_local, slot_count, block_rows, block_cols = ocean_state.shape
    groups = lax.axis_size(GROUP)
    tile_count = lax.axis_size("tile")
    hid_local = in_weight.shape[1]
    place = lax.axis_index(GROUP)[None]
    first_slot = (lax.axis_index("tile") - 1) * slot_count

    xt, strips, packed, part = start_step(
        ocean_state, conv_weight, conv_bias, norm_gain, in_weight, in_bias, out_weight
    )
    up = [(i, i + 1) for i in range(tile_count - 1)]
    strips_prev = lax.ppermute(strips, "tile", up)
    strips_next = lax.ppermute(strips, "tile", [(b, a) for a, b in up])
    entries, at = rim_places(neighbours, first_slot, block_rows)
    chosen = onehot_of(at, 3 * block_cols)
    picked = rims_of(place, entries, chosen, strips_prev, strips, strips_next, groups)
    if lax.axis_size("ens") == 2 and lax.axis_size("chan") == 2:
        near = swap(part, "chan")
        (far,) = gate([swap(near, "ens")], picked[0])
        parts = [packed, swap(packed, "sec"), near, far, swap(near, "sec"), swap(far, "sec")]
        starts = weight_places()
    else:
        parts = [lax.all_gather(packed, GROUP, axis=0, tiled=True)]
        starts = jnp.zeros((1,), jnp.int32)
    bodies = lax.all_to_all(
        xt.reshape((groups, slot_count // groups) + xt.shape[1:]), GROUP, 0, 0, tiled=True
    )
    flux = fluxes_of(atmos, flux_weight)
    rims = trade(picked)
    table = gather_flux(flux)
    weights = unpack_weights(parts, starts, groups, chan_local, hid_local, bodies)
    updates = trade(block_step(place, bodies, rims, weights))
    forcing = forcing_of(table, remap, atmos.shape[0], chan_local)
    return final_step(place, xt, updates, forcing, cell_mask, layer_scale)


def solution(mesh):
    placed = (
        P(("chan", "sec"), ("ens", "tile"), None, None),
        P(("ens", "tile"), None),
        P(None, ("chan", "sec")),
        P(None, None, ("chan", "sec")),
        P(("chan", "sec")),
        P(("chan", "sec")),
        P(None, ("chan", "sec")),
        P(("chan", "sec")),
        P(("chan", "sec"), None),
        P(("chan", "sec")),
        P("tile", None, None),
        P("tile", None),
        P("tile", None, None),
    )
    return jax.shard_map(
        on_device,
        mesh=mesh,
        in_specs=placed,
        out_specs=P(("chan", "sec"), ("ens", "tile"), None, None),
        check_vma=False,
    )
```

```python
import functools

import jax
import jax.numpy as jnp
from jax import lax
from jax.experimental import pallas as pl
from jax.experimental.pallas import tpu as pltpu
from jax.sharding import PartitionSpec as P

norm_eps = 1e-06
bf16 = jnp.bfloat16
f32 = jnp.float32
GROUP = ("chan", "sec")
BIAS_ROWS = 32
VMEM = pl.BlockSpec(memory_space=pltpu.VMEM)
SMEM = pl.BlockSpec(memory_space=pltpu.SMEM)
ANY = pl.BlockSpec(memory_space=pl.ANY)


def shape(dims, dtype=bf16):
    return jax.ShapeDtypeStruct(dims, dtype)


def params(mib=20):
    return pltpu.CompilerParams(vmem_limit_bytes=mib * 1024 * 1024)


def ein(a, b, dims):
    return lax.dot_general(a, b, (dims, ((), ())), preferred_element_type=f32)


def start_kernel(*refs):
    state_ref, conv_ref, bias_ref, gain_ref, in_ref, in_bias_ref, out_ref, atmos_ref, flux_ref = (
        refs[:9]
    )
    xt_ref, strips_ref, pack_ref, part_ref = refs[9:13]
    state_v, conv_v, in_v, out_v, atmos_v, half_v, strips_v, pack_v, sems = refs[13:]
    chunks, chan_local, span, block_rows, block_cols = state_v.shape
    taps, _, channels = conv_v.shape
    hid_local = out_v.shape[0]
    loads = [
        pltpu.make_async_copy(
            state_ref.at[:, pl.ds(c * span, span)], state_v.at[c], sems.at[c]
        )
        for c in range(chunks)
    ]
    copies = [
        pltpu.make_async_copy(conv_ref, conv_v, sems.at[chunks]),
        pltpu.make_async_copy(in_ref, in_v, sems.at[chunks + 1]),
        pltpu.make_async_copy(out_ref, out_v, sems.at[chunks + 2]),
    ]
    air = pltpu.make_async_copy(atmos_ref, atmos_v, sems.at[chunks + 3])
    for copy in loads + [air] + copies:
        copy.start()
    stores = []

    def store(source, target):
        stores.append(pltpu.make_async_copy(source, target, sems.at[chunks + 4 + len(stores)]))
        stores[-1].start()

    lane = lax.broadcasted_iota(jnp.int32, (chan_local, block_cols), 1)
    ends = jnp.zeros((chan_local, block_cols), f32)
    for c in range(chunks):
        loads[c].wait()
        for k in range(span):
            rows = jnp.swapaxes(state_v[c, :, k].astype(f32), 0, 1)
            packed = rows.astype(bf16)
            half_v[c, k] = packed
            slot = c * span + k
            strips_v[2 * slot] = packed[0]
            strips_v[2 * slot + 1] = packed[block_rows - 1]
            for r in range(block_rows):
                spot = 2 * (block_rows * slot + r)
                turned = pltpu.roll(rows[r], spot + 1, 1)
                ends = jnp.where((lane == spot) | (lane == spot + 1), turned, ends)
        store(half_v.at[c], xt_ref.at[pl.ds(c * span, span)])
    tiles = 2 * chunks * span + 1
    strips_v[tiles - 1] = ends.astype(bf16)
    air.wait()
    weight = flux_ref[...]
    side_by = block_cols // chan_local
    lines = atmos_v.shape[0] // side_by
    total = jnp.zeros((lines, block_cols), f32)
    for k in range(side_by):
        wide = [weight if j == k else jnp.zeros_like(weight) for j in range(side_by)]
        wide = jnp.concatenate(wide, axis=0)
        total = total + ein(atmos_v[pl.ds(k * lines, lines), :], wide, ((1,), (1,)))
    total = total.astype(bf16).reshape(lines // chan_local, chan_local, block_cols)
    strips_v[pl.ds(tiles, lines // chan_local)] = total
    store(strips_v, strips_ref)

    def widen(ref):
        rows = ref[...].astype(f32)
        row = jnp.concatenate([rows[k : k + 1] for k in range(rows.shape[0])], axis=1)
        if row.shape[1] == channels:
            return row
        return jnp.concatenate([row, jnp.zeros((1, channels - row.shape[1]), f32)], axis=1)

    rest = jnp.zeros((BIAS_ROWS - 3, channels), f32)
    biases = jnp.concatenate(
        [widen(bias_ref), widen(gain_ref), widen(in_bias_ref), rest], axis=0
    )
    at = taps * chan_local
    for copy in copies:
        copy.wait()
    for t in range(taps):
        pack_v[pl.ds(t * chan_local, chan_local), :] = conv_v[t]
    pack_v[pl.ds(at, hid_local), :] = in_v[...].astype(f32).T.astype(bf16)
    pack_v[pl.ds(at + hid_local, hid_local), :] = out_v[...]
    pack_v[pl.ds(at + 2 * hid_local, BIAS_ROWS), :] = biases.astype(bf16)
    part = part_ref.shape[0]
    store(pack_v, pack_ref)
    store(pack_v.at[pl.ds(pl.multiple_of(lax.axis_index("ens") * part, 16), part)], part_ref)
    for copy in stores:
        copy.wait()


def start_step(
    state, conv_weight, conv_bias, norm_gain, in_weight, in_bias, out_weight, atmos, flux_weight
):
    chan_local, slot_count, block_rows, block_cols = state.shape
    chunks = 4
    span = slot_count // chunks
    taps, channels, _ = conv_weight.shape
    hid_local = out_weight.shape[0]
    rows = taps * chan_local + 2 * hid_local + BIAS_ROWS
    half = (span, block_rows, chan_local, block_cols)
    lines = atmos.shape[0] * chan_local // block_cols
    strips = (2 * slot_count + 1 + lines // chan_local, chan_local, block_cols)
    return pl.pallas_call(
        start_kernel,
        out_shape=(shape((slot_count,) + half[1:]),)
        + (shape(strips), shape((rows, channels)), shape((rows // 2, channels))),
        in_specs=[ANY, ANY, VMEM, VMEM, ANY, VMEM, ANY, ANY, VMEM],
        out_specs=(ANY,) * 4,
        scratch_shapes=[
            pltpu.VMEM((chunks, chan_local, span, block_rows, block_cols), bf16),
            pltpu.VMEM((taps, chan_local, channels), bf16),
            pltpu.VMEM((channels, hid_local), bf16),
            pltpu.VMEM((hid_local, channels), bf16),
            pltpu.VMEM(atmos.shape, bf16),
            pltpu.VMEM((chunks,) + half, bf16),
            pltpu.VMEM(strips, bf16),
            pltpu.VMEM((rows, channels), bf16),
            pltpu.SemaphoreType.DMA((2 * chunks + 7,)),
        ],
        compiler_params=params(60),
        name="start_step",
    )(
        state,
        conv_weight.transpose(0, 2, 1),
        conv_bias.reshape(-1, min(128, chan_local)),
        norm_gain.reshape(-1, min(128, chan_local)),
        in_weight,
        in_bias.reshape(-1, min(128, hid_local)),
        out_weight,
        atmos,
        flux_weight.T,
    )


def send(piece, d, count):
    return lax.ppermute(piece, GROUP, [(i, i ^ d) for i in range(count)])


def trade(pieces):
    count = len(pieces)
    got = list(pieces)
    for d in list(range(count // 2, count)) + list(range(1, count // 2)):
        got[d] = send(pieces[d], d, count)
    return got


def unpack_kernel(count, chan_local, hid_local, starts_ref, *refs):
    pieces = refs[:count]
    *_, conv_ref, in_ref, out_ref, col_ref, hid_col_ref, all_ref = refs
    groups, rows, channels = all_ref.shape
    unit = min(rows, *(piece.shape[0] for piece in pieces))
    for n, piece in enumerate(pieces):
        for k in range(piece.shape[0] // unit):
            at = starts_ref[n] + k
            parts = rows // unit
            start = pl.multiple_of((at % parts) * unit, 16)
            all_ref[at // parts, pl.ds(start, unit), :] = piece[pl.ds(k * unit, unit), :]
    at = 9 * chan_local
    for j in range(groups):
        for t in range(9):
            conv_ref[pl.ds(j * chan_local, chan_local), pl.ds(t * channels, channels)] = all_ref[
                j, pl.ds(t * chan_local, chan_local), :
            ]
        in_ref[pl.ds(j * hid_local, hid_local), :] = all_ref[j, pl.ds(at, hid_local), :]
        biases = all_ref[j, pl.ds(at + 2 * hid_local, BIAS_ROWS), :].astype(f32)
        across = biases.T
        col_ref[pl.ds(j * chan_local, chan_local), :] = across[:chan_local]
        hid_col_ref[pl.ds(j * hid_local, hid_local), :] = across[:hid_local]
    outs = jnp.concatenate(
        [all_ref[j, pl.ds(at + hid_local, hid_local), :] for j in range(groups)], axis=0
    )
    out_ref[...] = outs.astype(f32).T.astype(bf16)


def unpack_weights(pieces, starts, groups, chan_local, hid_local, after):
    rows = sum(piece.shape[0] for piece in pieces) // groups
    channels = groups * chan_local
    hidden = groups * hid_local
    return pl.pallas_call(
        functools.partial(unpack_kernel, len(pieces), chan_local, hid_local),
        out_shape=(
            shape((channels, 9 * channels)),
            shape((hidden, channels)),
            shape((channels, hidden)),
            shape((channels, BIAS_ROWS), f32),
            shape((hidden, BIAS_ROWS), f32),
        ),
        in_specs=[SMEM] + [VMEM] * len(pieces) + [ANY],
        out_specs=(VMEM,) * 5,
        scratch_shapes=[pltpu.VMEM((groups, rows, channels), bf16)],
        compiler_params=params(),
        name="unpack_weights",
    )(starts, *pieces, after)


def swap(value, axis):
    return lax.ppermute(value, axis, [(0, 1), (1, 0)])


def gate_kernel(*refs):
    pass


def gate(values, *after):
    count = len(values)
    return pl.pallas_call(
        gate_kernel,
        out_shape=tuple(shape(value.shape) for value in values),
        in_specs=[ANY] * (count + len(after)),
        out_specs=(ANY,) * count,
        input_output_aliases={k: k for k in range(count)},
        compiler_params=params(),
        name="gate",
    )(*values, *after)


def weight_places():
    ens, chan, sec = (lax.axis_index(name) for name in ("ens", "chan", "sec"))
    own = 2 * (2 * chan + sec)
    beside = 2 * (2 * chan + 1 - sec)
    across = 2 * (2 * (1 - chan) + sec)
    corner = 2 * (2 * (1 - chan) + 1 - sec)
    return jnp.stack([own, beside, across + ens, across + 1 - ens, corner + ens, corner + 1 - ens])


def onehot_kernel(at_ref, out_ref):
    spot = lax.broadcasted_iota(jnp.int32, out_ref.shape, 0)
    out_ref[...] = (spot == at_ref[...]).astype(f32).astype(bf16)


def onehot_of(at, rows):
    return pl.pallas_call(
        onehot_kernel,
        out_shape=shape((rows, at.shape[1])),
        in_specs=[VMEM],
        out_specs=VMEM,
        compiler_params=params(),
        name="onehot",
    )(at)


def rim_kernel(place_ref, entry_ref, chosen_ref, prev_ref, own_ref, next_ref, *refs):
    *rims, up_ref, down_ref, held, cols = refs
    _, chan_local, block_cols = own_ref.shape
    groups = len(rims)
    per = (rims[0].shape[0] - 1) // 2
    tiles = 2 * per * groups + 1
    flux = pl.ds(tiles, up_ref.shape[0])
    up_ref[...] = prev_ref[flux]
    down_ref[...] = next_ref[flux]
    ends = jnp.concatenate(
        [prev_ref[tiles - 1], own_ref[tiles - 1], next_ref[tiles - 1]], axis=1
    )
    picked = ein(ends, chosen_ref[...], ((1,), (0,))).astype(bf16)
    for k in range(cols.shape[0]):
        cols[k] = picked[:, k * block_cols : (k + 1) * block_cols]
    for k, ref in enumerate((prev_ref, own_ref, next_ref)):
        held[pl.ds(k * tiles, tiles)] = ref[pl.ds(0, tiles)]
    held[3 * tiles] = jnp.zeros((chan_local, block_cols), bf16)
    for d in range(groups):
        group = jnp.bitwise_xor(place_ref[0], d)
        for s in range(per):
            rims[d][2 * s] = held[entry_ref[0, group * per + s]]
            rims[d][2 * s + 1] = held[entry_ref[1, group * per + s]]
        rims[d][2 * per] = cols[group * (16 * per) // block_cols]


def rim_places(neighbours, first_slot, block_rows):
    slot_count = neighbours.shape[0]
    tiles = 2 * slot_count + 1
    valid = neighbours >= 0
    slot = jnp.clip(neighbours - first_slot, 0, 3 * slot_count - 1)
    tile_of = slot // slot_count
    place = tile_of * tiles + 2 * (slot - tile_of * slot_count)
    entries = jnp.stack(
        [
            jnp.where(valid[:, 2], place[:, 2] + 1, 3 * tiles),
            jnp.where(valid[:, 3], place[:, 3], 3 * tiles),
        ]
    )
    base = jnp.where(valid, 2 * block_rows * slot, -4 * block_rows)
    last = 2 * (block_rows - 1)
    west = [base[:, 4] + last] + [base[:, 0] + 2 * r for r in range(block_rows)] + [base[:, 6]]
    east = [base[:, 5] + last] + [base[:, 1] + 2 * r for r in range(block_rows)] + [base[:, 7]]
    none = [jnp.full((slot_count,), -1, jnp.int32)] * (8 - block_rows - 2)
    at = jnp.stack(west + none + [e + 1 for e in east] + none, axis=1)
    return entries, at.reshape(1, slot_count * 16)


def rims_of(place, entries, chosen, strips_prev, strips, strips_next, groups):
    count, chan_local, block_cols = strips.shape
    slot_count = entries.shape[1]
    per = slot_count // groups
    tiles = 2 * slot_count + 1
    *rims, up, down = pl.pallas_call(
        rim_kernel,
        out_shape=(shape((2 * per + 1, chan_local, block_cols)),) * groups
        + (shape((count - tiles, chan_local, block_cols)),) * 2,
        in_specs=[SMEM, SMEM, VMEM, VMEM, VMEM, VMEM],
        out_specs=(VMEM,) * (groups + 2),
        scratch_shapes=[
            pltpu.VMEM((3 * tiles + 1, chan_local, block_cols), bf16),
            pltpu.VMEM((chosen.shape[1] // block_cols, chan_local, block_cols), bf16),
        ],
        compiler_params=params(),
        name="rims",
    )(place, entries, chosen, strips_prev, strips, strips_next)
    return rims, up, down


def block_kernel(groups, place_ref, *refs):
    body_ref, refs = refs[0], refs[1:]
    rims, refs = refs[:groups], refs[groups:]
    conv_ref, in_ref, out_ref, col_ref, hid_col_ref = refs[:5]
    updates, scratch = refs[5 : 5 + groups], refs[5 + groups :]
    _, per, block_rows, chan_local, block_cols = body_ref.shape
    channels = groups * chan_local
    hidden = in_ref.shape[0]
    me = place_ref[0]
    lane = lax.broadcasted_iota(jnp.int32, (chan_local, block_cols), 1)
    bias = col_ref[:, 0:1]
    gain = col_ref[:, 1:2]
    base = (me * (16 * per)) % block_cols
    rows = [
        pl.multiple_of(jnp.bitwise_xor(me, d) * chan_local, chan_local) for d in range(groups)
    ]
    rim_v, side_v = scratch[6:]
    for d in range(groups):
        source = jnp.bitwise_xor(me, d)
        rim_v[source] = rims[d][...]
        side_v[source] = pltpu.roll(rims[d][2 * per].astype(f32), block_cols - base, 1)
    for s in range(per):
        taken, hid, upd_v = scratch[3 * (s % 2) : 3 * (s % 2) + 3]
        for d in range(groups):
            for p in range(block_rows + 2):
                if p == 0:
                    mid = rim_v[d, 2 * s]
                elif p == block_rows + 1:
                    mid = rim_v[d, 2 * s + 1]
                else:
                    mid = body_ref[d, s, p - 1]
                wide = mid.astype(f32)
                spot = 16 * s + p
                left = jnp.where(
                    lane == 0,
                    pltpu.roll(side_v[d], (block_cols - spot) % block_cols, 1),
                    pltpu.roll(wide, 1, 1),
                ).astype(bf16)
                right = jnp.where(
                    lane == block_cols - 1,
                    pltpu.roll(side_v[d], (2 * block_cols - 1 - spot - 8) % block_cols, 1),
                    pltpu.roll(wide, block_cols - 1, 1),
                ).astype(bf16)
                for a in range(3):
                    i = p - a
                    if 0 <= i < block_rows:
                        for b, piece in enumerate((left, mid, right)):
                            taken[
                                3 * a + b,
                                pl.ds(d * chan_local, chan_local),
                                pl.ds(i * block_cols, block_cols),
                            ] = piece
        columns = taken[...].reshape(9 * channels, block_rows * block_cols)
        conv = ein(conv_ref[...], columns, ((1,), (0,))) + bias
        squares = jnp.sum(conv * conv, axis=0, keepdims=True)
        normed = (conv * lax.rsqrt(squares / channels + norm_eps) * gain).astype(bf16)
        step = min(hidden, 256)
        for h in range(0, hidden, step):
            pre = ein(in_ref[pl.ds(h, step), :], normed, ((1,), (0,)))
            pre = pre + hid_col_ref[pl.ds(h, step), 2:3]
            act = pre * (0.5 * lax.erf(pre * (0.5**0.5)) + 0.5)
            hid[pl.ds(h, step), :] = act.astype(bf16)
        upd_v[...] = ein(out_ref[...], hid[...], ((1,), (0,))).astype(bf16)
        for d in range(groups):
            for i in range(block_rows):
                updates[d][s, i] = upd_v[
                    pl.ds(rows[d], chan_local), pl.ds(i * block_cols, block_cols)
                ]


def block_step(place, bodies, rims, weights):
    groups, per, block_rows, chan_local, block_cols = bodies.shape
    channels = groups * chan_local
    hidden = weights[1].shape[0]
    cells = per * block_rows * block_cols
    return pl.pallas_call(
        functools.partial(block_kernel, groups),
        out_shape=(shape(bodies.shape[1:]),) * groups,
        in_specs=[SMEM] + [VMEM] * (groups + 6),
        out_specs=(VMEM,) * groups,
        scratch_shapes=[
            pltpu.VMEM((9, channels, block_rows * block_cols), bf16),
            pltpu.VMEM((hidden, block_rows * block_cols), bf16),
            pltpu.VMEM((channels, block_rows * block_cols), bf16),
        ]
        * 2
        + [
            pltpu.VMEM((groups,) + rims[0].shape, bf16),
            pltpu.VMEM((groups, chan_local, block_cols), f32),
        ],
        compiler_params=params(24),
        cost_estimate=pl.CostEstimate(
            flops=2 * cells * (9 * channels * channels + 2 * channels * hidden),
            bytes_accessed=8 * 1024 * 1024,
            transcendentals=0,
        ),
        name="block_step",
    )(place, bodies, *rims, *weights)


def forcing_kernel(row_ref, side_ref, wide, out_ref, even, odd):
    slot_count, block_rows, chan_local, block_cols = out_ref.shape
    lanes = wide.shape[2]
    row_at = lax.broadcasted_iota(jnp.int32, (lanes, lanes), 0)
    col_at = lax.broadcasted_iota(jnp.int32, (lanes, lanes), 1)
    eye = (row_at == col_at).astype(f32).astype(bf16)
    count = slot_count * block_rows

    def fetch(q, got):
        for k in range(block_cols):
            got[pl.ds(k, 1), :] = wide[row_ref[q, k]]

    def emit(q, got):
        across = ein(eye, got[...].astype(bf16), ((1,), (1,)))
        side = side_ref[pl.ds(q, 1), :]
        total = across[:chan_local]
        for k in range(1, lanes // chan_local):
            total = jnp.where(side == k, across[k * chan_local : (k + 1) * chan_local], total)
        out_ref[q // block_rows, q % block_rows] = total.astype(bf16)

    fetch(0, even)

    def two(n, _):
        q = 2 * n
        fetch(q + 1, odd)
        emit(q, even)
        fetch(jnp.minimum(q + 2, count - 1), even)
        emit(q + 1, odd)
        return 0

    lax.fori_loop(0, count // 2, two, 0)


def pass_on(own, up, down):
    count = lax.axis_size("tile")
    steps = [(i, i + 1) for i in range(count - 1)]
    ups, downs = [up], [down]
    for _ in range(count - 2):
        ups.append(lax.ppermute(ups[-1], "tile", steps))
        downs.append(lax.ppermute(downs[-1], "tile", [(b, a) for a, b in steps]))
    pieces = [own] + [ups[d - 1] + downs[count - d - 1] for d in range(1, count)]
    return [piece.reshape(-1, piece.shape[-1]) for piece in pieces]


def forcing_of(pieces, remap, rows_local, chan_local):
    slot_count, block_rows, block_cols = remap.shape
    count = len(pieces)
    side_by = 128 // chan_local
    part = rows_local // side_by
    target = jnp.clip(remap, 0, count * rows_local - 1).reshape(-1, block_cols)
    tile_of = target // rows_local
    within = target - tile_of * rows_local
    side = within // part
    behind = lax.axis_index("tile") - tile_of
    behind = jnp.where(behind < 0, behind + count, behind)
    row = behind * part + within - side * part
    table = lax.optimization_barrier(jnp.concatenate(pieces, axis=0).astype(f32))[:, None, :]
    return pl.pallas_call(
        forcing_kernel,
        out_shape=shape((slot_count, block_rows, chan_local, block_cols)),
        in_specs=[SMEM, VMEM, VMEM],
        out_specs=VMEM,
        scratch_shapes=[pltpu.VMEM((block_cols, 128), f32)] * 2,
        compiler_params=params(),
        cost_estimate=pl.CostEstimate(
            flops=0, bytes_accessed=32 * 1024 * 1024, transcendentals=0
        ),
        name="forcing",
    )(row, side, table)


def final_kernel(groups, place_ref, *refs):
    xt_ref, updates, rest = refs[0], refs[1 : 1 + groups], refs[1 + groups :]
    forcing_ref, mask_ref, scale_ref, out_ref, piece_v, upd_v, forcing_v, out_v, sems = rest
    per = piece_v.shape[1]
    loads = []
    for d in range(groups):
        first = jnp.bitwise_xor(place_ref[0], d) * per
        loads.append(
            [
                pltpu.make_async_copy(
                    xt_ref.at[pl.ds(first, per)], piece_v.at[d], sems.at[0, d]
                ),
                pltpu.make_async_copy(updates[d], upd_v.at[d], sems.at[1, d]),
                pltpu.make_async_copy(
                    forcing_ref.at[pl.ds(first, per)], forcing_v.at[d], sems.at[2, d]
                ),
            ]
        )
        for load in loads[d]:
            load.start()
    scale = scale_ref[...]
    stores = []
    for d in range(groups):
        first = jnp.bitwise_xor(place_ref[0], d) * per
        for load in loads[d]:
            load.wait()
        for s in range(per):
            total = piece_v[d, s].astype(f32) + scale[None] * upd_v[d, s].astype(f32)
            total = total + forcing_v[d, s].astype(f32)
            total = mask_ref[first + s].astype(f32)[:, None, :] * total
            out_v[d, :, s] = jnp.swapaxes(total, 0, 1).astype(bf16)
        stores.append(
            pltpu.make_async_copy(out_v.at[d], out_ref.at[:, pl.ds(first, per)], sems.at[3, d])
        )
        stores[d].start()
    for store in stores:
        store.wait()


def final_step(place, xt, updates, forcing, cell_mask, layer_scale):
    slot_count, block_rows, chan_local, block_cols = forcing.shape
    groups = len(updates)
    per = slot_count // groups
    return pl.pallas_call(
        functools.partial(final_kernel, groups),
        out_shape=shape((chan_local, slot_count, block_rows, block_cols)),
        in_specs=[SMEM] + [ANY] * (groups + 2) + [VMEM, VMEM],
        out_specs=ANY,
        scratch_shapes=[pltpu.VMEM((groups,) + updates[0].shape, bf16)] * 3
        + [
            pltpu.VMEM((groups, chan_local, per, block_rows, block_cols), bf16),
            pltpu.SemaphoreType.DMA((4, groups)),
        ],
        compiler_params=params(),
        name="final_step",
    )(place, xt, *updates, forcing, cell_mask, layer_scale.astype(f32)[:, None])


def on_device(
    ocean_state,
    atmos,
    flux_weight,
    conv_weight,
    conv_bias,
    norm_gain,
    in_weight,
    in_bias,
    out_weight,
    layer_scale,
    cell_mask,
    neighbours,
    remap,
):
    chan_local, slot_count, block_rows, block_cols = ocean_state.shape
    groups = lax.axis_size(GROUP)
    tile_count = lax.axis_size("tile")
    hid_local = in_weight.shape[1]
    place = lax.axis_index(GROUP)[None]
    first_slot = (lax.axis_index("tile") - 1) * slot_count

    xt, strips, packed, part = start_step(
        ocean_state,
        conv_weight,
        conv_bias,
        norm_gain,
        in_weight,
        in_bias,
        out_weight,
        atmos,
        flux_weight,
    )
    up = [(i, i + 1) for i in range(tile_count - 1)]
    strips_prev = lax.ppermute(strips, "tile", up)
    strips_next = lax.ppermute(strips, "tile", [(b, a) for a, b in up])
    entries, at = rim_places(neighbours, first_slot, block_rows)
    chosen = onehot_of(at, 3 * block_cols)
    picked, from_below, from_above = rims_of(
        place, entries, chosen, strips_prev, strips, strips_next, groups
    )
    if lax.axis_size("ens") == 2 and lax.axis_size("chan") == 2:
        near = swap(part, "chan")
        (xt,) = gate([xt], near)
        (far,) = gate([swap(near, "ens")], picked[0])
        parts = [packed, swap(packed, "sec"), near, far, swap(near, "sec"), swap(far, "sec")]
        starts = weight_places()
    else:
        parts = [lax.all_gather(packed, GROUP, axis=0, tiled=True)]
        starts = jnp.zeros((1,), jnp.int32)
    bodies = lax.all_to_all(
        xt.reshape((groups, slot_count // groups) + xt.shape[1:]), GROUP, 0, 0, tiled=True
    )
    rims = trade(picked)
    table = pass_on(strips[2 * slot_count + 1 :], from_below, from_above)
    weights = unpack_weights(parts, starts, groups, chan_local, hid_local, bodies)
    updates = trade(block_step(place, bodies, rims, weights))
    forcing = forcing_of(table, remap, atmos.shape[0], chan_local)
    return final_step(place, xt, updates, forcing, cell_mask, layer_scale)


def solution(mesh):
    placed = (
        P(("chan", "sec"), ("ens", "tile"), None, None),
        P(("ens", "tile"), None),
        P(None, ("chan", "sec")),
        P(None, None, ("chan", "sec")),
        P(("chan", "sec")),
        P(("chan", "sec")),
        P(None, ("chan", "sec")),
        P(("chan", "sec")),
        P(("chan", "sec"), None),
        P(("chan", "sec")),
        P("tile", None, None),
        P("tile", None),
        P("tile", None, None),
    )
    return jax.shard_map(
        on_device,
        mesh=mesh,
        in_specs=placed,
        out_specs=P(("chan", "sec"), ("ens", "tile"), None, None),
        check_vma=False,
    )
```

```python
import functools

import jax
import jax.numpy as jnp
from jax import lax
from jax.experimental import pallas as pl
from jax.experimental.pallas import tpu as pltpu
from jax.sharding import PartitionSpec as P

norm_eps = 1e-06
bf16 = jnp.bfloat16
f32 = jnp.float32
GROUP = ("chan", "sec")
BIAS_ROWS = 32
VMEM = pl.BlockSpec(memory_space=pltpu.VMEM)
SMEM = pl.BlockSpec(memory_space=pltpu.SMEM)
ANY = pl.BlockSpec(memory_space=pl.ANY)


def shape(dims, dtype=bf16):
    return jax.ShapeDtypeStruct(dims, dtype)


def params(mib=20):
    return pltpu.CompilerParams(vmem_limit_bytes=mib * 1024 * 1024)


def ein(a, b, dims):
    return lax.dot_general(a, b, (dims, ((), ())), preferred_element_type=f32)


def start_kernel(*refs):
    state_ref, conv_ref, bias_ref, gain_ref, in_ref, in_bias_ref, out_ref, atmos_ref, flux_ref = (
        refs[:9]
    )
    xt_ref, strips_ref, pack_ref, part_ref, own_ref = refs[9:14]
    state_v, conv_v, in_v, out_v, atmos_v, half_v, strips_v, pack_v, sems = refs[14:]
    chunks, chan_local, span, block_rows, block_cols = state_v.shape
    taps, _, channels = conv_v.shape
    hid_local = out_v.shape[0]
    loads = [
        pltpu.make_async_copy(
            state_ref.at[:, pl.ds(c * span, span)], state_v.at[c], sems.at[c]
        )
        for c in range(chunks)
    ]
    copies = [
        pltpu.make_async_copy(conv_ref, conv_v, sems.at[chunks]),
        pltpu.make_async_copy(in_ref, in_v, sems.at[chunks + 1]),
        pltpu.make_async_copy(out_ref, out_v, sems.at[chunks + 2]),
    ]
    air = pltpu.make_async_copy(atmos_ref, atmos_v, sems.at[chunks + 3])
    for copy in loads + [air] + copies:
        copy.start()
    stores = []

    def store(source, target):
        stores.append(pltpu.make_async_copy(source, target, sems.at[chunks + 4 + len(stores)]))
        stores[-1].start()

    lane = lax.broadcasted_iota(jnp.int32, (chan_local, block_cols), 1)
    ends = jnp.zeros((chan_local, block_cols), f32)
    for c in range(chunks):
        loads[c].wait()
        for k in range(span):
            rows = jnp.swapaxes(state_v[c, :, k].astype(f32), 0, 1)
            packed = rows.astype(bf16)
            half_v[c, k] = packed
            slot = c * span + k
            strips_v[2 * slot] = packed[0]
            strips_v[2 * slot + 1] = packed[block_rows - 1]
            for r in range(block_rows):
                spot = 2 * (block_rows * slot + r)
                turned = pltpu.roll(rows[r], spot + 1, 1)
                ends = jnp.where((lane == spot) | (lane == spot + 1), turned, ends)
        store(half_v.at[c], xt_ref.at[pl.ds(c * span, span)])
    tiles = 2 * chunks * span + 1
    strips_v[tiles - 1] = ends.astype(bf16)
    air.wait()
    weight = flux_ref[...]
    side_by = block_cols // chan_local
    lines = atmos_v.shape[0] // side_by
    total = jnp.zeros((lines, block_cols), f32)
    for k in range(side_by):
        wide = [weight if j == k else jnp.zeros_like(weight) for j in range(side_by)]
        wide = jnp.concatenate(wide, axis=0)
        total = total + ein(atmos_v[pl.ds(k * lines, lines), :], wide, ((1,), (1,)))
    total = total.astype(bf16).reshape(lines // chan_local, chan_local, block_cols)
    strips_v[pl.ds(tiles, lines // chan_local)] = total
    store(strips_v, strips_ref)
    store(strips_v.at[pl.ds(tiles, lines // chan_local)], own_ref)

    def widen(ref):
        rows = ref[...].astype(f32)
        row = jnp.concatenate([rows[k : k + 1] for k in range(rows.shape[0])], axis=1)
        if row.shape[1] == channels:
            return row
        return jnp.concatenate([row, jnp.zeros((1, channels - row.shape[1]), f32)], axis=1)

    rest = jnp.zeros((BIAS_ROWS - 3, channels), f32)
    biases = jnp.concatenate(
        [widen(bias_ref), widen(gain_ref), widen(in_bias_ref), rest], axis=0
    )
    at = taps * chan_local
    for copy in copies:
        copy.wait()
    for t in range(taps):
        pack_v[pl.ds(t * chan_local, chan_local), :] = conv_v[t]
    pack_v[pl.ds(at, hid_local), :] = in_v[...].astype(f32).T.astype(bf16)
    pack_v[pl.ds(at + hid_local, hid_local), :] = out_v[...]
    pack_v[pl.ds(at + 2 * hid_local, BIAS_ROWS), :] = biases.astype(bf16)
    part = part_ref.shape[0]
    store(pack_v, pack_ref)
    store(pack_v.at[pl.ds(pl.multiple_of(lax.axis_index("ens") * part, 16), part)], part_ref)
    for copy in stores:
        copy.wait()


def start_step(
    state, conv_weight, conv_bias, norm_gain, in_weight, in_bias, out_weight, atmos, flux_weight
):
    chan_local, slot_count, block_rows, block_cols = state.shape
    chunks = 4
    span = slot_count // chunks
    taps, channels, _ = conv_weight.shape
    hid_local = out_weight.shape[0]
    rows = taps * chan_local + 2 * hid_local + BIAS_ROWS
    half = (span, block_rows, chan_local, block_cols)
    lines = atmos.shape[0] * chan_local // block_cols
    strips = (2 * slot_count + 1 + lines // chan_local, chan_local, block_cols)
    return pl.pallas_call(
        start_kernel,
        out_shape=(shape((slot_count,) + half[1:]),)
        + (
            shape(strips),
            shape((rows, channels)),
            shape((rows // 2, channels)),
            shape((lines // chan_local,) + strips[1:]),
        ),
        in_specs=[ANY, ANY, VMEM, VMEM, ANY, VMEM, ANY, ANY, VMEM],
        out_specs=(ANY,) * 5,
        scratch_shapes=[
            pltpu.VMEM((chunks, chan_local, span, block_rows, block_cols), bf16),
            pltpu.VMEM((taps, chan_local, channels), bf16),
            pltpu.VMEM((channels, hid_local), bf16),
            pltpu.VMEM((hid_local, channels), bf16),
            pltpu.VMEM(atmos.shape, bf16),
            pltpu.VMEM((chunks,) + half, bf16),
            pltpu.VMEM(strips, bf16),
            pltpu.VMEM((rows, channels), bf16),
            pltpu.SemaphoreType.DMA((2 * chunks + 8,)),
        ],
        compiler_params=params(60),
        name="start_step",
    )(
        state,
        conv_weight.transpose(0, 2, 1),
        conv_bias.reshape(-1, min(128, chan_local)),
        norm_gain.reshape(-1, min(128, chan_local)),
        in_weight,
        in_bias.reshape(-1, min(128, hid_local)),
        out_weight,
        atmos,
        flux_weight.T,
    )


def send(piece, d, count):
    return lax.ppermute(piece, GROUP, [(i, i ^ d) for i in range(count)])


def trade(pieces):
    count = len(pieces)
    got = list(pieces)
    for d in list(range(count // 2, count)) + list(range(1, count // 2)):
        got[d] = send(pieces[d], d, count)
    return got


def unpack_kernel(count, chan_local, hid_local, starts_ref, *refs):
    pieces = refs[:count]
    *_, conv_ref, in_ref, out_ref, col_ref, hid_col_ref, all_ref = refs
    groups, rows, channels = all_ref.shape
    unit = min(rows, *(piece.shape[0] for piece in pieces))
    for n, piece in enumerate(pieces):
        for k in range(piece.shape[0] // unit):
            at = starts_ref[n] + k
            parts = rows // unit
            start = pl.multiple_of((at % parts) * unit, 16)
            all_ref[at // parts, pl.ds(start, unit), :] = piece[pl.ds(k * unit, unit), :]
    at = 9 * chan_local
    for j in range(groups):
        for t in range(9):
            conv_ref[pl.ds(j * chan_local, chan_local), pl.ds(t * channels, channels)] = all_ref[
                j, pl.ds(t * chan_local, chan_local), :
            ]
        in_ref[pl.ds(j * hid_local, hid_local), :] = all_ref[j, pl.ds(at, hid_local), :]
        biases = all_ref[j, pl.ds(at + 2 * hid_local, BIAS_ROWS), :].astype(f32)
        across = biases.T
        col_ref[pl.ds(j * chan_local, chan_local), :] = across[:chan_local]
        hid_col_ref[pl.ds(j * hid_local, hid_local), :] = across[:hid_local]
    outs = jnp.concatenate(
        [all_ref[j, pl.ds(at + hid_local, hid_local), :] for j in range(groups)], axis=0
    )
    out_ref[...] = outs.astype(f32).T.astype(bf16)


def unpack_weights(pieces, starts, groups, chan_local, hid_local, after):
    rows = sum(piece.shape[0] for piece in pieces) // groups
    channels = groups * chan_local
    hidden = groups * hid_local
    return pl.pallas_call(
        functools.partial(unpack_kernel, len(pieces), chan_local, hid_local),
        out_shape=(
            shape((channels, 9 * channels)),
            shape((hidden, channels)),
            shape((channels, hidden)),
            shape((channels, BIAS_ROWS), f32),
            shape((hidden, BIAS_ROWS), f32),
        ),
        in_specs=[SMEM] + [VMEM] * len(pieces) + [ANY],
        out_specs=(VMEM,) * 5,
        scratch_shapes=[pltpu.VMEM((groups, rows, channels), bf16)],
        compiler_params=params(),
        name="unpack_weights",
    )(starts, *pieces, after)


def swap(value, axis):
    return lax.ppermute(value, axis, [(0, 1), (1, 0)])


def gate_kernel(*refs):
    pass


def gate(values, *after):
    count = len(values)
    return pl.pallas_call(
        gate_kernel,
        out_shape=tuple(shape(value.shape) for value in values),
        in_specs=[ANY] * (count + len(after)),
        out_specs=(ANY,) * count,
        input_output_aliases={k: k for k in range(count)},
        compiler_params=params(),
        name="gate",
    )(*values, *after)


def weight_places():
    ens, chan, sec = (lax.axis_index(name) for name in ("ens", "chan", "sec"))
    own = 2 * (2 * chan + sec)
    beside = 2 * (2 * chan + 1 - sec)
    across = 2 * (2 * (1 - chan) + sec)
    corner = 2 * (2 * (1 - chan) + 1 - sec)
    return jnp.stack([own, beside, across + ens, across + 1 - ens, corner + ens, corner + 1 - ens])


def onehot_kernel(at_ref, out_ref):
    spot = lax.broadcasted_iota(jnp.int32, out_ref.shape, 0)
    out_ref[...] = (spot == at_ref[...]).astype(f32).astype(bf16)


def onehot_of(at, rows):
    return pl.pallas_call(
        onehot_kernel,
        out_shape=shape((rows, at.shape[1])),
        in_specs=[VMEM],
        out_specs=VMEM,
        compiler_params=params(),
        name="onehot",
    )(at)


def rim_kernel(place_ref, entry_ref, chosen_ref, prev_ref, own_ref, next_ref, *refs):
    *rims, up_ref, down_ref, held, cols = refs
    _, chan_local, block_cols = own_ref.shape
    groups = len(rims)
    per = (rims[0].shape[0] - 1) // 2
    tiles = 2 * per * groups + 1
    flux = pl.ds(tiles, up_ref.shape[0])
    up_ref[...] = prev_ref[flux]
    down_ref[...] = next_ref[flux]
    ends = jnp.concatenate(
        [prev_ref[tiles - 1], own_ref[tiles - 1], next_ref[tiles - 1]], axis=1
    )
    picked = ein(ends, chosen_ref[...], ((1,), (0,))).astype(bf16)
    for k in range(cols.shape[0]):
        cols[k] = picked[:, k * block_cols : (k + 1) * block_cols]
    for k, ref in enumerate((prev_ref, own_ref, next_ref)):
        held[pl.ds(k * tiles, tiles)] = ref[pl.ds(0, tiles)]
    held[3 * tiles] = jnp.zeros((chan_local, block_cols), bf16)
    for d in range(groups):
        group = jnp.bitwise_xor(place_ref[0], d)
        for s in range(per):
            rims[d][2 * s] = held[entry_ref[0, group * per + s]]
            rims[d][2 * s + 1] = held[entry_ref[1, group * per + s]]
        rims[d][2 * per] = cols[group * (16 * per) // block_cols]


def rim_places(neighbours, first_slot, block_rows):
    slot_count = neighbours.shape[0]
    tiles = 2 * slot_count + 1
    valid = neighbours >= 0
    slot = jnp.clip(neighbours - first_slot, 0, 3 * slot_count - 1)
    tile_of = slot // slot_count
    place = tile_of * tiles + 2 * (slot - tile_of * slot_count)
    entries = jnp.stack(
        [
            jnp.where(valid[:, 2], place[:, 2] + 1, 3 * tiles),
            jnp.where(valid[:, 3], place[:, 3], 3 * tiles),
        ]
    )
    base = jnp.where(valid, 2 * block_rows * slot, -4 * block_rows)
    last = 2 * (block_rows - 1)
    west = [base[:, 4] + last] + [base[:, 0] + 2 * r for r in range(block_rows)] + [base[:, 6]]
    east = [base[:, 5] + last] + [base[:, 1] + 2 * r for r in range(block_rows)] + [base[:, 7]]
    none = [jnp.full((slot_count,), -1, jnp.int32)] * (8 - block_rows - 2)
    at = jnp.stack(west + none + [e + 1 for e in east] + none, axis=1)
    return entries, at.reshape(1, slot_count * 16)


def rims_of(place, entries, chosen, strips_prev, strips, strips_next, groups):
    count, chan_local, block_cols = strips.shape
    slot_count = entries.shape[1]
    per = slot_count // groups
    tiles = 2 * slot_count + 1
    *rims, up, down = pl.pallas_call(
        rim_kernel,
        out_shape=(shape((2 * per + 1, chan_local, block_cols)),) * groups
        + (shape((count - tiles, chan_local, block_cols)),) * 2,
        in_specs=[SMEM, SMEM, VMEM, VMEM, VMEM, VMEM],
        out_specs=(VMEM,) * (groups + 2),
        scratch_shapes=[
            pltpu.VMEM((3 * tiles + 1, chan_local, block_cols), bf16),
            pltpu.VMEM((chosen.shape[1] // block_cols, chan_local, block_cols), bf16),
        ],
        compiler_params=params(),
        name="rims",
    )(place, entries, chosen, strips_prev, strips, strips_next)
    return rims, up, down


def block_kernel(groups, place_ref, *refs):
    body_ref, refs = refs[0], refs[1:]
    rims, refs = refs[:groups], refs[groups:]
    conv_ref, in_ref, out_ref, col_ref, hid_col_ref = refs[:5]
    updates, scratch = refs[5 : 5 + groups], refs[5 + groups :]
    _, per, block_rows, chan_local, block_cols = body_ref.shape
    channels = groups * chan_local
    hidden = in_ref.shape[0]
    me = place_ref[0]
    lane = lax.broadcasted_iota(jnp.int32, (chan_local, block_cols), 1)
    bias = col_ref[:, 0:1]
    gain = col_ref[:, 1:2]
    base = (me * (16 * per)) % block_cols
    rows = [
        pl.multiple_of(jnp.bitwise_xor(me, d) * chan_local, chan_local) for d in range(groups)
    ]
    rim_v, side_v = scratch[6:]
    for d in range(groups):
        source = jnp.bitwise_xor(me, d)
        rim_v[source] = rims[d][...]
        side_v[source] = pltpu.roll(rims[d][2 * per].astype(f32), block_cols - base, 1)
    for s in range(per):
        taken, hid, upd_v = scratch[3 * (s % 2) : 3 * (s % 2) + 3]
        for d in range(groups):
            for p in range(block_rows + 2):
                if p == 0:
                    mid = rim_v[d, 2 * s]
                elif p == block_rows + 1:
                    mid = rim_v[d, 2 * s + 1]
                else:
                    mid = body_ref[d, s, p - 1]
                wide = mid.astype(f32)
                spot = 16 * s + p
                left = jnp.where(
                    lane == 0,
                    pltpu.roll(side_v[d], (block_cols - spot) % block_cols, 1),
                    pltpu.roll(wide, 1, 1),
                ).astype(bf16)
                right = jnp.where(
                    lane == block_cols - 1,
                    pltpu.roll(side_v[d], (2 * block_cols - 1 - spot - 8) % block_cols, 1),
                    pltpu.roll(wide, block_cols - 1, 1),
                ).astype(bf16)
                for a in range(3):
                    i = p - a
                    if 0 <= i < block_rows:
                        for b, piece in enumerate((left, mid, right)):
                            taken[
                                3 * a + b,
                                pl.ds(d * chan_local, chan_local),
                                pl.ds(i * block_cols, block_cols),
                            ] = piece
        columns = taken[...].reshape(9 * channels, block_rows * block_cols)
        conv = ein(conv_ref[...], columns, ((1,), (0,))) + bias
        squares = jnp.sum(conv * conv, axis=0, keepdims=True)
        normed = (conv * lax.rsqrt(squares / channels + norm_eps) * gain).astype(bf16)
        step = min(hidden, 256)
        for h in range(0, hidden, step):
            pre = ein(in_ref[pl.ds(h, step), :], normed, ((1,), (0,)))
            pre = pre + hid_col_ref[pl.ds(h, step), 2:3]
            act = pre * (0.5 * lax.erf(pre * (0.5**0.5)) + 0.5)
            hid[pl.ds(h, step), :] = act.astype(bf16)
        upd_v[...] = ein(out_ref[...], hid[...], ((1,), (0,))).astype(bf16)
        for d in range(groups):
            for i in range(block_rows):
                updates[d][s, i] = upd_v[
                    pl.ds(rows[d], chan_local), pl.ds(i * block_cols, block_cols)
                ]


def block_step(place, bodies, rims, weights):
    groups, per, block_rows, chan_local, block_cols = bodies.shape
    channels = groups * chan_local
    hidden = weights[1].shape[0]
    cells = per * block_rows * block_cols
    return pl.pallas_call(
        functools.partial(block_kernel, groups),
        out_shape=(shape(bodies.shape[1:]),) * groups,
        in_specs=[SMEM] + [VMEM] * (groups + 6),
        out_specs=(VMEM,) * groups,
        scratch_shapes=[
            pltpu.VMEM((9, channels, block_rows * block_cols), bf16),
            pltpu.VMEM((hidden, block_rows * block_cols), bf16),
            pltpu.VMEM((channels, block_rows * block_cols), bf16),
        ]
        * 2
        + [
            pltpu.VMEM((groups,) + rims[0].shape, bf16),
            pltpu.VMEM((groups, chan_local, block_cols), f32),
        ],
        compiler_params=params(24),
        cost_estimate=pl.CostEstimate(
            flops=2 * cells * (9 * channels * channels + 2 * channels * hidden),
            bytes_accessed=8 * 1024 * 1024,
            transcendentals=0,
        ),
        name="block_step",
    )(place, bodies, *rims, *weights)


def forcing_kernel(row_ref, side_ref, wide, out_ref, even, odd):
    slot_count, block_rows, chan_local, block_cols = out_ref.shape
    lanes = wide.shape[2]
    row_at = lax.broadcasted_iota(jnp.int32, (lanes, lanes), 0)
    col_at = lax.broadcasted_iota(jnp.int32, (lanes, lanes), 1)
    eye = (row_at == col_at).astype(f32).astype(bf16)
    count = slot_count * block_rows
    batch = even.shape[0] // block_cols

    def fetch(q, got):
        for j in range(batch):
            for k in range(block_cols):
                got[pl.ds(j * block_cols + k, 1), :] = wide[row_ref[q + j, k]]

    def emit(q, got):
        across = ein(eye, got[...].astype(bf16), ((1,), (1,)))
        for j in range(batch):
            mine = across[:, j * block_cols : (j + 1) * block_cols]
            side = side_ref[pl.ds(q + j, 1), :]
            total = mine[:chan_local]
            for k in range(1, lanes // chan_local):
                total = jnp.where(side == k, mine[k * chan_local : (k + 1) * chan_local], total)
            out_ref[q // block_rows, j] = total.astype(bf16)

    fetch(0, even)

    def two(n, _):
        q = 2 * batch * n
        fetch(q + batch, odd)
        emit(q, even)
        fetch(jnp.minimum(q + 2 * batch, count - batch), even)
        emit(q + batch, odd)
        return 0

    lax.fori_loop(0, count // (2 * batch), two, 0)


def gather_flux(flux, below, above):
    count = lax.axis_size("tile")
    me = lax.axis_index("tile")
    if count == 4:
        two = lax.ppermute(flux, "tile", [(i, i ^ 2) for i in range(count)])
        three = lax.ppermute(flux, "tile", [(0, 3), (3, 0)])
        pieces = [piece.reshape(-1, 128) for piece in (flux, below, above, two, three)]

        def piece_of(tile):
            far = jnp.abs(tile - me)
            return jnp.where(far > 1, far + 1, jnp.where(tile > me, 2, far))

        return pieces, piece_of
    whole = lax.all_gather(flux, "tile", axis=0)
    return [piece.reshape(-1, 128) for piece in whole], lambda tile: tile


def forcing_of(pieces, piece_of, remap, rows_local, chan_local):
    slot_count, block_rows, block_cols = remap.shape
    side_by = 128 // chan_local
    part = rows_local // side_by
    target = jnp.clip(remap, 0, lax.axis_size("tile") * rows_local - 1).reshape(-1, block_cols)
    tile_of = target // rows_local
    within = target - tile_of * rows_local
    side = within // part
    row = piece_of(tile_of) * part + within - side * part
    table = lax.optimization_barrier(jnp.concatenate(pieces, axis=0).astype(f32))[:, None, :]
    return pl.pallas_call(
        forcing_kernel,
        out_shape=shape((slot_count, block_rows, chan_local, block_cols)),
        in_specs=[SMEM, VMEM, VMEM],
        out_specs=VMEM,
        scratch_shapes=[pltpu.VMEM((block_rows * block_cols, 128), f32)] * 2,
        compiler_params=params(),
        cost_estimate=pl.CostEstimate(
            flops=0, bytes_accessed=32 * 1024 * 1024, transcendentals=0
        ),
        name="forcing",
    )(row, side, table)


def final_kernel(groups, place_ref, *refs):
    xt_ref, updates, rest = refs[0], refs[1 : 1 + groups], refs[1 + groups :]
    forcing_ref, mask_ref, scale_ref, out_ref, piece_v, upd_v, forcing_v, out_v, sems = rest
    per = piece_v.shape[1]
    loads = []
    for d in range(groups):
        first = jnp.bitwise_xor(place_ref[0], d) * per
        loads.append(
            [
                pltpu.make_async_copy(
                    xt_ref.at[pl.ds(first, per)], piece_v.at[d], sems.at[0, d]
                ),
                pltpu.make_async_copy(updates[d], upd_v.at[d], sems.at[1, d]),
                pltpu.make_async_copy(
                    forcing_ref.at[pl.ds(first, per)], forcing_v.at[d], sems.at[2, d]
                ),
            ]
        )
        for load in loads[d]:
            load.start()
    scale = scale_ref[...]
    stores = []
    for d in range(groups):
        first = jnp.bitwise_xor(place_ref[0], d) * per
        for load in loads[d]:
            load.wait()
        for s in range(per):
            total = piece_v[d, s].astype(f32) + scale[None] * upd_v[d, s].astype(f32)
            total = total + forcing_v[d, s].astype(f32)
            total = mask_ref[first + s].astype(f32)[:, None, :] * total
            out_v[d, :, s] = jnp.swapaxes(total, 0, 1).astype(bf16)
        stores.append(
            pltpu.make_async_copy(out_v.at[d], out_ref.at[:, pl.ds(first, per)], sems.at[3, d])
        )
        stores[d].start()
    for store in stores:
        store.wait()


def final_step(place, xt, updates, forcing, cell_mask, layer_scale):
    slot_count, block_rows, chan_local, block_cols = forcing.shape
    groups = len(updates)
    per = slot_count // groups
    return pl.pallas_call(
        functools.partial(final_kernel, groups),
        out_shape=shape((chan_local, slot_count, block_rows, block_cols)),
        in_specs=[SMEM] + [ANY] * (groups + 2) + [VMEM, VMEM],
        out_specs=ANY,
        scratch_shapes=[pltpu.VMEM((groups,) + updates[0].shape, bf16)] * 3
        + [
            pltpu.VMEM((groups, chan_local, per, block_rows, block_cols), bf16),
            pltpu.SemaphoreType.DMA((4, groups)),
        ],
        compiler_params=params(),
        name="final_step",
    )(place, xt, *updates, forcing, cell_mask, layer_scale.astype(f32)[:, None])


def on_device(
    ocean_state,
    atmos,
    flux_weight,
    conv_weight,
    conv_bias,
    norm_gain,
    in_weight,
    in_bias,
    out_weight,
    layer_scale,
    cell_mask,
    neighbours,
    remap,
):
    chan_local, slot_count, block_rows, block_cols = ocean_state.shape
    groups = lax.axis_size(GROUP)
    tile_count = lax.axis_size("tile")
    hid_local = in_weight.shape[1]
    place = lax.axis_index(GROUP)[None]
    first_slot = (lax.axis_index("tile") - 1) * slot_count

    xt, strips, packed, part, flux = start_step(
        ocean_state,
        conv_weight,
        conv_bias,
        norm_gain,
        in_weight,
        in_bias,
        out_weight,
        atmos,
        flux_weight,
    )
    up = [(i, i + 1) for i in range(tile_count - 1)]
    strips_prev = lax.ppermute(strips, "tile", up)
    strips_next = lax.ppermute(strips, "tile", [(b, a) for a, b in up])
    entries, at = rim_places(neighbours, first_slot, block_rows)
    chosen = onehot_of(at, 3 * block_cols)
    picked, from_below, from_above = rims_of(
        place, entries, chosen, strips_prev, strips, strips_next, groups
    )
    if lax.axis_size("ens") == 2 and lax.axis_size("chan") == 2:
        near = swap(part, "chan")
        (xt,) = gate([xt], near)
        (far,) = gate([swap(near, "ens")], picked[0])
        parts = [packed, swap(packed, "sec"), near, far, swap(near, "sec"), swap(far, "sec")]
        starts = weight_places()
    else:
        parts = [lax.all_gather(packed, GROUP, axis=0, tiled=True)]
        starts = jnp.zeros((1,), jnp.int32)
    bodies = lax.all_to_all(
        xt.reshape((groups, slot_count // groups) + xt.shape[1:]), GROUP, 0, 0, tiled=True
    )
    rims = trade(picked)
    table, piece_of = gather_flux(flux, from_below, from_above)
    weights = unpack_weights(parts, starts, groups, chan_local, hid_local, bodies)
    updates = trade(block_step(place, bodies, rims, weights))
    forcing = forcing_of(table, piece_of, remap, atmos.shape[0], chan_local)
    return final_step(place, xt, updates, forcing, cell_mask, layer_scale)


def solution(mesh):
    placed = (
        P(("chan", "sec"), ("ens", "tile"), None, None),
        P(("ens", "tile"), None),
        P(None, ("chan", "sec")),
        P(None, None, ("chan", "sec")),
        P(("chan", "sec")),
        P(("chan", "sec")),
        P(None, ("chan", "sec")),
        P(("chan", "sec")),
        P(("chan", "sec"), None),
        P(("chan", "sec")),
        P("tile", None, None),
        P("tile", None),
        P("tile", None, None),
    )
    return jax.shard_map(
        on_device,
        mesh=mesh,
        in_specs=placed,
        out_specs=P(("chan", "sec"), ("ens", "tile"), None, None),
        check_vma=False,
    )
```

```python
import functools

import jax
import jax.numpy as jnp
from jax import lax
from jax.experimental import pallas as pl
from jax.experimental.pallas import tpu as pltpu
from jax.sharding import PartitionSpec as P

norm_eps = 1e-06
bf16 = jnp.bfloat16
f32 = jnp.float32
GROUP = ("chan", "sec")
BIAS_ROWS = 32
VMEM = pl.BlockSpec(memory_space=pltpu.VMEM)
SMEM = pl.BlockSpec(memory_space=pltpu.SMEM)
ANY = pl.BlockSpec(memory_space=pl.ANY)


def shape(dims, dtype=bf16):
    return jax.ShapeDtypeStruct(dims, dtype)


def params(mib=20):
    return pltpu.CompilerParams(vmem_limit_bytes=mib * 1024 * 1024)


def ein(a, b, dims):
    return lax.dot_general(a, b, (dims, ((), ())), preferred_element_type=f32)


def start_kernel(*refs):
    state_ref, conv_ref, bias_ref, gain_ref, in_ref, in_bias_ref, out_ref, atmos_ref, flux_ref = (
        refs[:9]
    )
    xt_ref, strips_ref, pack_ref, part_ref, own_ref = refs[9:14]
    state_v, conv_v, in_v, out_v, atmos_v, half_v, strips_v, pack_v, sems = refs[14:]
    chunks, chan_local, span, block_rows, block_cols = state_v.shape
    taps, _, channels = conv_v.shape
    hid_local = out_v.shape[0]
    loads = [
        pltpu.make_async_copy(
            state_ref.at[:, pl.ds(c * span, span)], state_v.at[c], sems.at[c]
        )
        for c in range(chunks)
    ]
    copies = [
        pltpu.make_async_copy(conv_ref, conv_v, sems.at[chunks]),
        pltpu.make_async_copy(in_ref, in_v, sems.at[chunks + 1]),
        pltpu.make_async_copy(out_ref, out_v, sems.at[chunks + 2]),
    ]
    air = pltpu.make_async_copy(atmos_ref, atmos_v, sems.at[chunks + 3])
    for copy in loads + [air] + copies:
        copy.start()
    stores = []

    def store(source, target):
        stores.append(pltpu.make_async_copy(source, target, sems.at[chunks + 4 + len(stores)]))
        stores[-1].start()

    lane = lax.broadcasted_iota(jnp.int32, (chan_local, block_cols), 1)
    ends = jnp.zeros((chan_local, block_cols), f32)
    for c in range(chunks):
        loads[c].wait()
        for k in range(span):
            rows = jnp.swapaxes(state_v[c, :, k].astype(f32), 0, 1)
            packed = rows.astype(bf16)
            half_v[c, k] = packed
            slot = c * span + k
            strips_v[2 * slot] = packed[0]
            strips_v[2 * slot + 1] = packed[block_rows - 1]
            for r in range(block_rows):
                spot = 2 * (block_rows * slot + r)
                turned = pltpu.roll(rows[r], spot + 1, 1)
                ends = jnp.where((lane == spot) | (lane == spot + 1), turned, ends)
        store(half_v.at[c], xt_ref.at[pl.ds(c * span, span)])
    tiles = 2 * chunks * span + 1
    strips_v[tiles - 1] = ends.astype(bf16)
    air.wait()
    weight = flux_ref[...]
    side_by = block_cols // chan_local
    lines = atmos_v.shape[0] // side_by
    total = jnp.zeros((lines, block_cols), f32)
    for k in range(side_by):
        wide = [weight if j == k else jnp.zeros_like(weight) for j in range(side_by)]
        wide = jnp.concatenate(wide, axis=0)
        total = total + ein(atmos_v[pl.ds(k * lines, lines), :], wide, ((1,), (1,)))
    total = total.astype(bf16).reshape(lines // chan_local, chan_local, block_cols)
    strips_v[pl.ds(tiles, lines // chan_local)] = total
    store(strips_v, strips_ref)
    store(strips_v.at[pl.ds(tiles, lines // chan_local)], own_ref)

    def widen(ref):
        rows = ref[...].astype(f32)
        row = jnp.concatenate([rows[k : k + 1] for k in range(rows.shape[0])], axis=1)
        if row.shape[1] == channels:
            return row
        return jnp.concatenate([row, jnp.zeros((1, channels - row.shape[1]), f32)], axis=1)

    rest = jnp.zeros((BIAS_ROWS - 3, channels), f32)
    biases = jnp.concatenate(
        [widen(bias_ref), widen(gain_ref), widen(in_bias_ref), rest], axis=0
    )
    at = taps * chan_local
    for copy in copies:
        copy.wait()
    for t in range(taps):
        pack_v[pl.ds(t * chan_local, chan_local), :] = conv_v[t]
    pack_v[pl.ds(at, hid_local), :] = in_v[...].astype(f32).T.astype(bf16)
    pack_v[pl.ds(at + hid_local, hid_local), :] = out_v[...]
    pack_v[pl.ds(at + 2 * hid_local, BIAS_ROWS), :] = biases.astype(bf16)
    part = part_ref.shape[0]
    store(pack_v, pack_ref)
    store(pack_v.at[pl.ds(pl.multiple_of(lax.axis_index("ens") * part, 16), part)], part_ref)
    for copy in stores:
        copy.wait()


def start_step(
    state, conv_weight, conv_bias, norm_gain, in_weight, in_bias, out_weight, atmos, flux_weight
):
    chan_local, slot_count, block_rows, block_cols = state.shape
    chunks = 4
    span = slot_count // chunks
    taps, channels, _ = conv_weight.shape
    hid_local = out_weight.shape[0]
    rows = taps * chan_local + 2 * hid_local + BIAS_ROWS
    half = (span, block_rows, chan_local, block_cols)
    lines = atmos.shape[0] * chan_local // block_cols
    strips = (2 * slot_count + 1 + lines // chan_local, chan_local, block_cols)
    return pl.pallas_call(
        start_kernel,
        out_shape=(shape((slot_count,) + half[1:]),)
        + (
            shape(strips),
            shape((rows, channels)),
            shape((rows // 2, channels)),
            shape((lines // chan_local,) + strips[1:]),
        ),
        in_specs=[ANY, ANY, VMEM, VMEM, ANY, VMEM, ANY, ANY, VMEM],
        out_specs=(ANY,) * 5,
        scratch_shapes=[
            pltpu.VMEM((chunks, chan_local, span, block_rows, block_cols), bf16),
            pltpu.VMEM((taps, chan_local, channels), bf16),
            pltpu.VMEM((channels, hid_local), bf16),
            pltpu.VMEM((hid_local, channels), bf16),
            pltpu.VMEM(atmos.shape, bf16),
            pltpu.VMEM((chunks,) + half, bf16),
            pltpu.VMEM(strips, bf16),
            pltpu.VMEM((rows, channels), bf16),
            pltpu.SemaphoreType.DMA((2 * chunks + 8,)),
        ],
        compiler_params=params(60),
        name="start_step",
    )(
        state,
        conv_weight.transpose(0, 2, 1),
        conv_bias.reshape(-1, min(128, chan_local)),
        norm_gain.reshape(-1, min(128, chan_local)),
        in_weight,
        in_bias.reshape(-1, min(128, hid_local)),
        out_weight,
        atmos,
        flux_weight.T,
    )


def send(piece, d, count):
    return lax.ppermute(piece, GROUP, [(i, i ^ d) for i in range(count)])


def trade(pieces):
    count = len(pieces)
    got = list(pieces)
    for d in list(range(count // 2, count)) + list(range(1, count // 2)):
        got[d] = send(pieces[d], d, count)
    return got


def unpack_kernel(count, chan_local, hid_local, starts_ref, *refs):
    pieces = refs[:count]
    *_, conv_ref, in_ref, out_ref, col_ref, hid_col_ref, all_ref = refs
    groups, rows, channels = all_ref.shape
    unit = min(rows, *(piece.shape[0] for piece in pieces))
    for n, piece in enumerate(pieces):
        for k in range(piece.shape[0] // unit):
            at = starts_ref[n] + k
            parts = rows // unit
            start = pl.multiple_of((at % parts) * unit, 16)
            all_ref[at // parts, pl.ds(start, unit), :] = piece[pl.ds(k * unit, unit), :]
    at = 9 * chan_local
    for j in range(groups):
        for t in range(9):
            conv_ref[pl.ds(j * chan_local, chan_local), pl.ds(t * channels, channels)] = all_ref[
                j, pl.ds(t * chan_local, chan_local), :
            ]
        in_ref[pl.ds(j * hid_local, hid_local), :] = all_ref[j, pl.ds(at, hid_local), :]
        biases = all_ref[j, pl.ds(at + 2 * hid_local, BIAS_ROWS), :].astype(f32)
        across = biases.T
        col_ref[pl.ds(j * chan_local, chan_local), :] = across[:chan_local]
        hid_col_ref[pl.ds(j * hid_local, hid_local), :] = across[:hid_local]
    outs = jnp.concatenate(
        [all_ref[j, pl.ds(at + hid_local, hid_local), :] for j in range(groups)], axis=0
    )
    out_ref[...] = outs.astype(f32).T.astype(bf16)


def unpack_weights(pieces, starts, groups, chan_local, hid_local, after):
    rows = sum(piece.shape[0] for piece in pieces) // groups
    channels = groups * chan_local
    hidden = groups * hid_local
    return pl.pallas_call(
        functools.partial(unpack_kernel, len(pieces), chan_local, hid_local),
        out_shape=(
            shape((channels, 9 * channels)),
            shape((hidden, channels)),
            shape((channels, hidden)),
            shape((channels, BIAS_ROWS), f32),
            shape((hidden, BIAS_ROWS), f32),
        ),
        in_specs=[SMEM] + [VMEM] * len(pieces) + [ANY],
        out_specs=(VMEM,) * 5,
        scratch_shapes=[pltpu.VMEM((groups, rows, channels), bf16)],
        compiler_params=params(),
        name="unpack_weights",
    )(starts, *pieces, after)


def swap(value, axis):
    return lax.ppermute(value, axis, [(0, 1), (1, 0)])


def gate_kernel(*refs):
    pass


def gate(values, after, mib=20):
    count = len(values)
    return pl.pallas_call(
        gate_kernel,
        out_shape=tuple(shape(value.shape) for value in values),
        in_specs=[ANY] * (count + 1),
        out_specs=(ANY,) * count,
        input_output_aliases={k: k for k in range(count)},
        compiler_params=params(mib),
        name="gate",
    )(*values, after)


def weight_places():
    ens, chan, sec = (lax.axis_index(name) for name in ("ens", "chan", "sec"))
    own = 2 * (2 * chan + sec)
    beside = 2 * (2 * chan + 1 - sec)
    across = 2 * (2 * (1 - chan) + sec)
    corner = 2 * (2 * (1 - chan) + 1 - sec)
    return jnp.stack([own, beside, across + ens, across + 1 - ens, corner + ens, corner + 1 - ens])


def onehot_kernel(at_ref, out_ref):
    spot = lax.broadcasted_iota(jnp.int32, out_ref.shape, 0)
    out_ref[...] = (spot == at_ref[...]).astype(f32).astype(bf16)


def onehot_of(at, rows):
    return pl.pallas_call(
        onehot_kernel,
        out_shape=shape((rows, at.shape[1])),
        in_specs=[VMEM],
        out_specs=VMEM,
        compiler_params=params(),
        name="onehot",
    )(at)


def rim_kernel(place_ref, entry_ref, chosen_ref, prev_ref, own_ref, next_ref, *refs):
    *rims, up_ref, down_ref, both_ref, held, cols = refs
    _, chan_local, block_cols = own_ref.shape
    groups = len(rims)
    per = (rims[0].shape[0] - 1) // 2
    tiles = 2 * per * groups + 1
    flux = pl.ds(tiles, up_ref.shape[0])
    up_ref[...] = prev_ref[flux]
    down_ref[...] = next_ref[flux]
    lines = up_ref.shape[0]
    both_ref[pl.ds(0, lines)] = own_ref[flux]
    upper = lax.axis_index("tile") >= lax.axis_size("tile") // 2

    @pl.when(upper)
    def _():
        both_ref[pl.ds(lines, lines)] = next_ref[flux]

    @pl.when(jnp.logical_not(upper))
    def _():
        both_ref[pl.ds(lines, lines)] = prev_ref[flux]

    ends = jnp.concatenate(
        [prev_ref[tiles - 1], own_ref[tiles - 1], next_ref[tiles - 1]], axis=1
    )
    picked = ein(ends, chosen_ref[...], ((1,), (0,))).astype(bf16)
    for k in range(cols.shape[0]):
        cols[k] = picked[:, k * block_cols : (k + 1) * block_cols]
    for k, ref in enumerate((prev_ref, own_ref, next_ref)):
        held[pl.ds(k * tiles, tiles)] = ref[pl.ds(0, tiles)]
    held[3 * tiles] = jnp.zeros((chan_local, block_cols), bf16)
    for d in range(groups):
        group = jnp.bitwise_xor(place_ref[0], d)
        for s in range(per):
            rims[d][2 * s] = held[entry_ref[0, group * per + s]]
            rims[d][2 * s + 1] = held[entry_ref[1, group * per + s]]
        rims[d][2 * per] = cols[group * (16 * per) // block_cols]


def rim_places(neighbours, first_slot, block_rows):
    slot_count = neighbours.shape[0]
    tiles = 2 * slot_count + 1
    valid = neighbours >= 0
    slot = jnp.clip(neighbours - first_slot, 0, 3 * slot_count - 1)
    tile_of = slot // slot_count
    place = tile_of * tiles + 2 * (slot - tile_of * slot_count)
    entries = jnp.stack(
        [
            jnp.where(valid[:, 2], place[:, 2] + 1, 3 * tiles),
            jnp.where(valid[:, 3], place[:, 3], 3 * tiles),
        ]
    )
    base = jnp.where(valid, 2 * block_rows * slot, -4 * block_rows)
    last = 2 * (block_rows - 1)
    west = [base[:, 4] + last] + [base[:, 0] + 2 * r for r in range(block_rows)] + [base[:, 6]]
    east = [base[:, 5] + last] + [base[:, 1] + 2 * r for r in range(block_rows)] + [base[:, 7]]
    none = [jnp.full((slot_count,), -1, jnp.int32)] * (8 - block_rows - 2)
    at = jnp.stack(west + none + [e + 1 for e in east] + none, axis=1)
    return entries, at.reshape(1, slot_count * 16)


def rims_of(place, entries, chosen, strips_prev, strips, strips_next, groups):
    count, chan_local, block_cols = strips.shape
    slot_count = entries.shape[1]
    per = slot_count // groups
    tiles = 2 * slot_count + 1
    *rims, up, down, both = pl.pallas_call(
        rim_kernel,
        out_shape=(shape((2 * per + 1, chan_local, block_cols)),) * groups
        + (shape((count - tiles, chan_local, block_cols)),) * 2
        + (shape((2 * (count - tiles), chan_local, block_cols)),),
        in_specs=[SMEM, SMEM, VMEM, VMEM, VMEM, VMEM],
        out_specs=(VMEM,) * (groups + 3),
        scratch_shapes=[
            pltpu.VMEM((3 * tiles + 1, chan_local, block_cols), bf16),
            pltpu.VMEM((chosen.shape[1] // block_cols, chan_local, block_cols), bf16),
        ],
        compiler_params=params(),
        name="rims",
    )(place, entries, chosen, strips_prev, strips, strips_next)
    return rims, up, down, both


def block_kernel(groups, place_ref, *refs):
    body_ref, refs = refs[0], refs[1:]
    rims, refs = refs[:groups], refs[groups:]
    conv_ref, in_ref, out_ref, col_ref, hid_col_ref = refs[:5]
    updates, scratch = refs[5 : 5 + groups], refs[5 + groups :]
    _, per, block_rows, chan_local, block_cols = body_ref.shape
    channels = groups * chan_local
    hidden = in_ref.shape[0]
    me = place_ref[0]
    lane = lax.broadcasted_iota(jnp.int32, (chan_local, block_cols), 1)
    bias = col_ref[:, 0:1]
    gain = col_ref[:, 1:2]
    base = (me * (16 * per)) % block_cols
    rows = [
        pl.multiple_of(jnp.bitwise_xor(me, d) * chan_local, chan_local) for d in range(groups)
    ]
    rim_v, side_v = scratch[6:]
    for d in range(groups):
        source = jnp.bitwise_xor(me, d)
        rim_v[source] = rims[d][...]
        side_v[source] = pltpu.roll(rims[d][2 * per].astype(f32), block_cols - base, 1)
    for s in range(per):
        taken, hid, upd_v = scratch[3 * (s % 2) : 3 * (s % 2) + 3]
        for d in range(groups):
            for p in range(block_rows + 2):
                if p == 0:
                    mid = rim_v[d, 2 * s]
                elif p == block_rows + 1:
                    mid = rim_v[d, 2 * s + 1]
                else:
                    mid = body_ref[d, s, p - 1]
                wide = mid.astype(f32)
                spot = 16 * s + p
                left = jnp.where(
                    lane == 0,
                    pltpu.roll(side_v[d], (block_cols - spot) % block_cols, 1),
                    pltpu.roll(wide, 1, 1),
                ).astype(bf16)
                right = jnp.where(
                    lane == block_cols - 1,
                    pltpu.roll(side_v[d], (2 * block_cols - 1 - spot - 8) % block_cols, 1),
                    pltpu.roll(wide, block_cols - 1, 1),
                ).astype(bf16)
                for a in range(3):
                    i = p - a
                    if 0 <= i < block_rows:
                        for b, piece in enumerate((left, mid, right)):
                            taken[
                                3 * a + b,
                                pl.ds(d * chan_local, chan_local),
                                pl.ds(i * block_cols, block_cols),
                            ] = piece
        columns = taken[...].reshape(9 * channels, block_rows * block_cols)
        conv = ein(conv_ref[...], columns, ((1,), (0,))) + bias
        squares = jnp.sum(conv * conv, axis=0, keepdims=True)
        normed = (conv * lax.rsqrt(squares / channels + norm_eps) * gain).astype(bf16)
        step = min(hidden, 256)
        for h in range(0, hidden, step):
            pre = ein(in_ref[pl.ds(h, step), :], normed, ((1,), (0,)))
            pre = pre + hid_col_ref[pl.ds(h, step), 2:3]
            act = pre * (0.5 * lax.erf(pre * (0.5**0.5)) + 0.5)
            hid[pl.ds(h, step), :] = act.astype(bf16)
        upd_v[...] = ein(out_ref[...], hid[...], ((1,), (0,))).astype(bf16)
        for d in range(groups):
            for i in range(block_rows):
                updates[d][s, i] = upd_v[
                    pl.ds(rows[d], chan_local), pl.ds(i * block_cols, block_cols)
                ]


def block_step(place, bodies, rims, weights):
    groups, per, block_rows, chan_local, block_cols = bodies.shape
    channels = groups * chan_local
    hidden = weights[1].shape[0]
    cells = per * block_rows * block_cols
    return pl.pallas_call(
        functools.partial(block_kernel, groups),
        out_shape=(shape(bodies.shape[1:]),) * groups,
        in_specs=[SMEM] + [VMEM] * (groups + 6),
        out_specs=(VMEM,) * groups,
        scratch_shapes=[
            pltpu.VMEM((9, channels, block_rows * block_cols), bf16),
            pltpu.VMEM((hidden, block_rows * block_cols), bf16),
            pltpu.VMEM((channels, block_rows * block_cols), bf16),
        ]
        * 2
        + [
            pltpu.VMEM((groups,) + rims[0].shape, bf16),
            pltpu.VMEM((groups, chan_local, block_cols), f32),
        ],
        compiler_params=params(24),
        cost_estimate=pl.CostEstimate(
            flops=2 * cells * (9 * channels * channels + 2 * channels * hidden),
            bytes_accessed=8 * 1024 * 1024,
            transcendentals=0,
        ),
        name="block_step",
    )(place, bodies, *rims, *weights)


def forcing_kernel(row_ref, side_ref, *refs):
    *pieces, out_ref, wide, even, odd = refs
    slot_count, block_rows, chan_local, block_cols = out_ref.shape
    lanes = wide.shape[1]
    at = 0
    for piece in pieces:
        wide[pl.ds(at, piece.shape[0]), :] = piece[...].astype(f32)
        at += piece.shape[0]
    row_at = lax.broadcasted_iota(jnp.int32, (lanes, lanes), 0)
    col_at = lax.broadcasted_iota(jnp.int32, (lanes, lanes), 1)
    eye = (row_at == col_at).astype(f32).astype(bf16)
    count = slot_count * block_rows
    batch = even.shape[0] // block_cols

    def fetch(q, got):
        for j in range(batch):
            for k in range(block_cols):
                got[pl.ds(j * block_cols + k, 1), :] = wide[pl.ds(row_ref[q + j, k], 1), :]

    def emit(q, got):
        across = ein(eye, got[...].astype(bf16), ((1,), (1,)))
        for j in range(batch):
            mine = across[:, j * block_cols : (j + 1) * block_cols]
            side = side_ref[pl.ds(q + j, 1), :]
            total = mine[:chan_local]
            for k in range(1, lanes // chan_local):
                total = jnp.where(side == k, mine[k * chan_local : (k + 1) * chan_local], total)
            out_ref[q // block_rows, j] = total.astype(bf16)

    fetch(0, even)

    def two(n, _):
        q = 2 * batch * n
        fetch(q + batch, odd)
        emit(q, even)
        fetch(jnp.minimum(q + 2 * batch, count - batch), even)
        emit(q + batch, odd)
        return 0

    lax.fori_loop(0, count // (2 * batch), two, 0)


def gather_flux(flux, below, above, both):
    count = lax.axis_size("tile")
    me = lax.axis_index("tile")
    if count == 4:
        far = lax.ppermute(both, "tile", [(i, i ^ 2) for i in range(count)])
        pieces = [piece.reshape(-1, 128) for piece in (flux, below, above, far)]

        def piece_of(tile):
            far = jnp.abs(tile - me)
            return jnp.where(far > 1, far + 1, jnp.where(tile > me, 2, far))

        return pieces, piece_of
    whole = lax.all_gather(flux, "tile", axis=0)
    return [whole.reshape(-1, 128)], lambda tile: tile


def forcing_of(pieces, piece_of, remap, rows_local, chan_local):
    slot_count, block_rows, block_cols = remap.shape
    side_by = 128 // chan_local
    part = rows_local // side_by
    target = jnp.clip(remap, 0, lax.axis_size("tile") * rows_local - 1).reshape(-1, block_cols)
    tile_of = target // rows_local
    within = target - tile_of * rows_local
    side = within // part
    row = piece_of(tile_of) * part + within - side * part
    lines = sum(piece.shape[0] for piece in pieces)
    return pl.pallas_call(
        forcing_kernel,
        out_shape=shape((slot_count, block_rows, chan_local, block_cols)),
        in_specs=[SMEM, VMEM] + [VMEM] * len(pieces),
        out_specs=VMEM,
        scratch_shapes=[pltpu.VMEM((lines, 128), f32)]
        + [pltpu.VMEM((block_rows * block_cols, 128), f32)] * 2,
        compiler_params=params(),
        cost_estimate=pl.CostEstimate(
            flops=0, bytes_accessed=32 * 1024 * 1024, transcendentals=0
        ),
        name="forcing",
    )(row, side, *pieces)


def final_kernel(groups, place_ref, *refs):
    xt_ref, updates, rest = refs[0], refs[1 : 1 + groups], refs[1 + groups :]
    forcing_ref, mask_ref, scale_ref, out_ref, piece_v, upd_v, forcing_v, out_v, sems = rest
    per = piece_v.shape[1]
    loads = []
    for d in range(groups):
        first = jnp.bitwise_xor(place_ref[0], d) * per
        loads.append(
            [
                pltpu.make_async_copy(
                    xt_ref.at[pl.ds(first, per)], piece_v.at[d], sems.at[0, d]
                ),
                pltpu.make_async_copy(updates[d], upd_v.at[d], sems.at[1, d]),
                pltpu.make_async_copy(
                    forcing_ref.at[pl.ds(first, per)], forcing_v.at[d], sems.at[2, d]
                ),
            ]
        )
        for load in loads[d]:
            load.start()
    scale = scale_ref[...]
    stores = []
    for d in range(groups):
        first = jnp.bitwise_xor(place_ref[0], d) * per
        for load in loads[d]:
            load.wait()
        for s in range(per):
            total = piece_v[d, s].astype(f32) + scale[None] * upd_v[d, s].astype(f32)
            total = total + forcing_v[d, s].astype(f32)
            total = mask_ref[first + s].astype(f32)[:, None, :] * total
            out_v[d, :, s] = jnp.swapaxes(total, 0, 1).astype(bf16)
        stores.append(
            pltpu.make_async_copy(out_v.at[d], out_ref.at[:, pl.ds(first, per)], sems.at[3, d])
        )
        stores[d].start()
    for store in stores:
        store.wait()


def final_step(place, xt, updates, forcing, cell_mask, layer_scale):
    slot_count, block_rows, chan_local, block_cols = forcing.shape
    groups = len(updates)
    per = slot_count // groups
    return pl.pallas_call(
        functools.partial(final_kernel, groups),
        out_shape=shape((chan_local, slot_count, block_rows, block_cols)),
        in_specs=[SMEM] + [ANY] * (groups + 2) + [VMEM, VMEM],
        out_specs=ANY,
        scratch_shapes=[pltpu.VMEM((groups,) + updates[0].shape, bf16)] * 3
        + [
            pltpu.VMEM((groups, chan_local, per, block_rows, block_cols), bf16),
            pltpu.SemaphoreType.DMA((4, groups)),
        ],
        compiler_params=params(),
        name="final_step",
    )(place, xt, *updates, forcing, cell_mask, layer_scale.astype(f32)[:, None])


def on_device(
    ocean_state,
    atmos,
    flux_weight,
    conv_weight,
    conv_bias,
    norm_gain,
    in_weight,
    in_bias,
    out_weight,
    layer_scale,
    cell_mask,
    neighbours,
    remap,
):
    chan_local, slot_count, block_rows, block_cols = ocean_state.shape
    groups = lax.axis_size(GROUP)
    tile_count = lax.axis_size("tile")
    hid_local = in_weight.shape[1]
    place = lax.axis_index(GROUP)[None]
    first_slot = (lax.axis_index("tile") - 1) * slot_count

    xt, strips, packed, part, flux = start_step(
        ocean_state,
        conv_weight,
        conv_bias,
        norm_gain,
        in_weight,
        in_bias,
        out_weight,
        atmos,
        flux_weight,
    )
    up = [(i, i + 1) for i in range(tile_count - 1)]
    strips_prev = lax.ppermute(strips, "tile", up)
    strips_next = lax.ppermute(strips, "tile", [(b, a) for a, b in up])
    entries, at = rim_places(neighbours, first_slot, block_rows)
    chosen = onehot_of(at, 3 * block_cols)
    picked, below, above, both = rims_of(
        place, entries, chosen, strips_prev, strips, strips_next, groups
    )
    if lax.axis_size("ens") == 2 and lax.axis_size("chan") == 2:
        near = swap(part, "chan")
        (xt,) = gate([xt], near, 60)
        (far,) = gate([swap(near, "ens")], picked[0])
        parts = [packed, swap(packed, "sec"), near, far, swap(near, "sec"), swap(far, "sec")]
        starts = weight_places()
    else:
        parts = [lax.all_gather(packed, GROUP, axis=0, tiled=True)]
        starts = jnp.zeros((1,), jnp.int32)
    bodies = lax.all_to_all(
        xt.reshape((groups, slot_count // groups) + xt.shape[1:]), GROUP, 0, 0, tiled=True
    )
    rims = trade(picked)
    table, piece_of = gather_flux(flux, below, above, both)
    weights = unpack_weights(parts, starts, groups, chan_local, hid_local, bodies)
    updates = trade(block_step(place, bodies, rims, weights))
    forcing = forcing_of(table, piece_of, remap, atmos.shape[0], chan_local)
    return final_step(place, xt, updates, forcing, cell_mask, layer_scale)


def solution(mesh):
    placed = (
        P(("chan", "sec"), ("ens", "tile"), None, None),
        P(("ens", "tile"), None),
        P(None, ("chan", "sec")),
        P(None, None, ("chan", "sec")),
        P(("chan", "sec")),
        P(("chan", "sec")),
        P(None, ("chan", "sec")),
        P(("chan", "sec")),
        P(("chan", "sec"), None),
        P(("chan", "sec")),
        P("tile", None, None),
        P("tile", None),
        P("tile", None, None),
    )
    return jax.shard_map(
        on_device,
        mesh=mesh,
        in_specs=placed,
        out_specs=P(("chan", "sec"), ("ens", "tile"), None, None),
        check_vma=False,
    )
```

```python
import functools

import jax
import jax.numpy as jnp
from jax import lax
from jax.experimental import pallas as pl
from jax.experimental.pallas import tpu as pltpu
from jax.sharding import PartitionSpec as P

norm_eps = 1e-06
bf16 = jnp.bfloat16
f32 = jnp.float32
GROUP = ("chan", "sec")
BIAS_ROWS = 32
VMEM = pl.BlockSpec(memory_space=pltpu.VMEM)
SMEM = pl.BlockSpec(memory_space=pltpu.SMEM)
ANY = pl.BlockSpec(memory_space=pl.ANY)


def shape(dims, dtype=bf16):
    return jax.ShapeDtypeStruct(dims, dtype)


def params(mib=20):
    return pltpu.CompilerParams(vmem_limit_bytes=mib * 1024 * 1024)


def ein(a, b, dims):
    return lax.dot_general(a, b, (dims, ((), ())), preferred_element_type=f32)


def start_kernel(*refs):
    state_ref, conv_ref, bias_ref, gain_ref, in_ref, in_bias_ref, out_ref, atmos_ref, flux_ref = (
        refs[:9]
    )
    xt_ref, strips_ref, pack_ref, part_ref, own_ref = refs[9:14]
    state_v, conv_v, in_v, out_v, atmos_v, half_v, strips_v, pack_v, sems = refs[14:]
    chunks, chan_local, span, block_rows, block_cols = state_v.shape
    taps, _, channels = conv_v.shape
    hid_local = out_v.shape[0]
    loads = [
        pltpu.make_async_copy(
            state_ref.at[:, pl.ds(c * span, span)], state_v.at[c], sems.at[c]
        )
        for c in range(chunks)
    ]
    copies = [
        pltpu.make_async_copy(conv_ref, conv_v, sems.at[chunks]),
        pltpu.make_async_copy(in_ref, in_v, sems.at[chunks + 1]),
        pltpu.make_async_copy(out_ref, out_v, sems.at[chunks + 2]),
    ]
    air = pltpu.make_async_copy(atmos_ref, atmos_v, sems.at[chunks + 3])
    for copy in loads + [air] + copies:
        copy.start()
    stores = []

    def store(source, target):
        stores.append(pltpu.make_async_copy(source, target, sems.at[chunks + 4 + len(stores)]))
        stores[-1].start()

    lane = lax.broadcasted_iota(jnp.int32, (chan_local, block_cols), 1)
    ends = jnp.zeros((chan_local, block_cols), f32)
    for c in range(chunks):
        loads[c].wait()
        for k in range(span):
            rows = jnp.swapaxes(state_v[c, :, k].astype(f32), 0, 1)
            packed = rows.astype(bf16)
            half_v[c, k] = packed
            slot = c * span + k
            strips_v[2 * slot] = packed[0]
            strips_v[2 * slot + 1] = packed[block_rows - 1]
            for r in range(block_rows):
                spot = 2 * (block_rows * slot + r)
                turned = pltpu.roll(rows[r], spot + 1, 1)
                ends = jnp.where((lane == spot) | (lane == spot + 1), turned, ends)
        store(half_v.at[c], xt_ref.at[pl.ds(c * span, span)])
    tiles = 2 * chunks * span + 1
    strips_v[tiles - 1] = ends.astype(bf16)
    air.wait()
    weight = flux_ref[...]
    side_by = block_cols // chan_local
    lines = atmos_v.shape[0] // side_by
    total = jnp.zeros((lines, block_cols), f32)
    for k in range(side_by):
        wide = [weight if j == k else jnp.zeros_like(weight) for j in range(side_by)]
        wide = jnp.concatenate(wide, axis=0)
        total = total + ein(atmos_v[pl.ds(k * lines, lines), :], wide, ((1,), (1,)))
    total = total.astype(bf16).reshape(lines // chan_local, chan_local, block_cols)
    strips_v[pl.ds(tiles, lines // chan_local)] = total
    store(strips_v, strips_ref)
    store(strips_v.at[pl.ds(tiles, lines // chan_local)], own_ref)

    def widen(ref):
        rows = ref[...].astype(f32)
        row = jnp.concatenate([rows[k : k + 1] for k in range(rows.shape[0])], axis=1)
        if row.shape[1] == channels:
            return row
        return jnp.concatenate([row, jnp.zeros((1, channels - row.shape[1]), f32)], axis=1)

    rest = jnp.zeros((BIAS_ROWS - 3, channels), f32)
    biases = jnp.concatenate(
        [widen(bias_ref), widen(gain_ref), widen(in_bias_ref), rest], axis=0
    )
    at = taps * chan_local
    for copy in copies:
        copy.wait()
    for t in range(taps):
        pack_v[pl.ds(t * chan_local, chan_local), :] = conv_v[t]
    pack_v[pl.ds(at, hid_local), :] = in_v[...].astype(f32).T.astype(bf16)
    pack_v[pl.ds(at + hid_local, hid_local), :] = out_v[...]
    pack_v[pl.ds(at + 2 * hid_local, BIAS_ROWS), :] = biases.astype(bf16)
    part = part_ref.shape[0]
    store(pack_v, pack_ref)
    store(pack_v.at[pl.ds(pl.multiple_of(lax.axis_index("ens") * part, 16), part)], part_ref)
    for copy in stores:
        copy.wait()


def start_step(
    state, conv_weight, conv_bias, norm_gain, in_weight, in_bias, out_weight, atmos, flux_weight
):
    chan_local, slot_count, block_rows, block_cols = state.shape
    chunks = 4
    span = slot_count // chunks
    taps, channels, _ = conv_weight.shape
    hid_local = out_weight.shape[0]
    rows = taps * chan_local + 2 * hid_local + BIAS_ROWS
    half = (span, block_rows, chan_local, block_cols)
    lines = atmos.shape[0] * chan_local // block_cols
    strips = (2 * slot_count + 1 + lines // chan_local, chan_local, block_cols)
    return pl.pallas_call(
        start_kernel,
        out_shape=(shape((slot_count,) + half[1:]),)
        + (
            shape(strips),
            shape((rows, channels)),
            shape((rows // 2, channels)),
            shape((lines // chan_local,) + strips[1:]),
        ),
        in_specs=[ANY, ANY, VMEM, VMEM, ANY, VMEM, ANY, ANY, VMEM],
        out_specs=(ANY,) * 5,
        scratch_shapes=[
            pltpu.VMEM((chunks, chan_local, span, block_rows, block_cols), bf16),
            pltpu.VMEM((taps, chan_local, channels), bf16),
            pltpu.VMEM((channels, hid_local), bf16),
            pltpu.VMEM((hid_local, channels), bf16),
            pltpu.VMEM(atmos.shape, bf16),
            pltpu.VMEM((chunks,) + half, bf16),
            pltpu.VMEM(strips, bf16),
            pltpu.VMEM((rows, channels), bf16),
            pltpu.SemaphoreType.DMA((2 * chunks + 8,)),
        ],
        compiler_params=params(60),
        name="start_step",
    )(
        state,
        conv_weight.transpose(0, 2, 1),
        conv_bias.reshape(-1, min(128, chan_local)),
        norm_gain.reshape(-1, min(128, chan_local)),
        in_weight,
        in_bias.reshape(-1, min(128, hid_local)),
        out_weight,
        atmos,
        flux_weight.T,
    )


def send(piece, d, count):
    return lax.ppermute(piece, GROUP, [(i, i ^ d) for i in range(count)])


def trade(pieces):
    count = len(pieces)
    got = list(pieces)
    for d in list(range(count // 2, count)) + list(range(1, count // 2)):
        got[d] = send(pieces[d], d, count)
    return got


def unpack_kernel(count, chan_local, hid_local, starts_ref, *refs):
    pieces = refs[:count]
    *_, conv_ref, in_ref, out_ref, col_ref, hid_col_ref, all_ref = refs
    groups, rows, channels = all_ref.shape
    unit = min(rows, *(piece.shape[0] for piece in pieces))
    for n, piece in enumerate(pieces):
        for k in range(piece.shape[0] // unit):
            at = starts_ref[n] + k
            parts = rows // unit
            start = pl.multiple_of((at % parts) * unit, 16)
            all_ref[at // parts, pl.ds(start, unit), :] = piece[pl.ds(k * unit, unit), :]
    at = 9 * chan_local
    for j in range(groups):
        for t in range(9):
            conv_ref[pl.ds(j * chan_local, chan_local), pl.ds(t * channels, channels)] = all_ref[
                j, pl.ds(t * chan_local, chan_local), :
            ]
        in_ref[pl.ds(j * hid_local, hid_local), :] = all_ref[j, pl.ds(at, hid_local), :]
        biases = all_ref[j, pl.ds(at + 2 * hid_local, BIAS_ROWS), :].astype(f32)
        across = biases.T
        col_ref[pl.ds(j * chan_local, chan_local), :] = across[:chan_local]
        hid_col_ref[pl.ds(j * hid_local, hid_local), :] = across[:hid_local]
    outs = jnp.concatenate(
        [all_ref[j, pl.ds(at + hid_local, hid_local), :] for j in range(groups)], axis=0
    )
    out_ref[...] = outs.astype(f32).T.astype(bf16)


def unpack_weights(pieces, starts, groups, chan_local, hid_local, after):
    rows = sum(piece.shape[0] for piece in pieces) // groups
    channels = groups * chan_local
    hidden = groups * hid_local
    return pl.pallas_call(
        functools.partial(unpack_kernel, len(pieces), chan_local, hid_local),
        out_shape=(
            shape((channels, 9 * channels)),
            shape((hidden, channels)),
            shape((channels, hidden)),
            shape((channels, BIAS_ROWS), f32),
            shape((hidden, BIAS_ROWS), f32),
        ),
        in_specs=[SMEM] + [VMEM] * len(pieces) + [ANY],
        out_specs=(VMEM,) * 5,
        scratch_shapes=[pltpu.VMEM((groups, rows, channels), bf16)],
        compiler_params=params(),
        name="unpack_weights",
    )(starts, *pieces, after)


def swap(value, axis):
    return lax.ppermute(value, axis, [(0, 1), (1, 0)])


def gate_kernel(*refs):
    pass


def gate(values, after, mib=20):
    count = len(values)
    return pl.pallas_call(
        gate_kernel,
        out_shape=tuple(shape(value.shape) for value in values),
        in_specs=[ANY] * (count + 1),
        out_specs=(ANY,) * count,
        input_output_aliases={k: k for k in range(count)},
        compiler_params=params(mib),
        name="gate",
    )(*values, after)


def weight_places():
    ens, chan, sec = (lax.axis_index(name) for name in ("ens", "chan", "sec"))
    own = 2 * (2 * chan + sec)
    beside = 2 * (2 * chan + 1 - sec)
    across = 2 * (2 * (1 - chan) + sec)
    corner = 2 * (2 * (1 - chan) + 1 - sec)
    return jnp.stack([own, beside, across + ens, across + 1 - ens, corner + ens, corner + 1 - ens])


def onehot_kernel(at_ref, out_ref):
    spot = lax.broadcasted_iota(jnp.int32, out_ref.shape, 0)
    out_ref[...] = (spot == at_ref[...]).astype(f32).astype(bf16)


def onehot_of(at, rows):
    return pl.pallas_call(
        onehot_kernel,
        out_shape=shape((rows, at.shape[1])),
        in_specs=[VMEM],
        out_specs=VMEM,
        compiler_params=params(),
        name="onehot",
    )(at)


def rim_kernel(place_ref, entry_ref, chosen_ref, prev_ref, own_ref, next_ref, *refs):
    *rims, up_ref, down_ref, held, cols, rim_v, sems = refs
    groups, rows, chan_local, block_cols = rim_v.shape
    per = (rows - 1) // 2
    tiles = 2 * per * groups + 1
    flux = pl.ds(tiles, up_ref.shape[0])
    stores = [
        pltpu.make_async_copy(prev_ref.at[flux], up_ref, sems.at[groups]),
        pltpu.make_async_copy(next_ref.at[flux], down_ref, sems.at[groups + 1]),
    ]
    for store in stores:
        store.start()
    ends = jnp.concatenate(
        [prev_ref[tiles - 1], own_ref[tiles - 1], next_ref[tiles - 1]], axis=1
    )
    picked = ein(ends, chosen_ref[...], ((1,), (0,))).astype(bf16)
    for k in range(cols.shape[0]):
        cols[k] = picked[:, k * block_cols : (k + 1) * block_cols]
    for k, ref in enumerate((prev_ref, own_ref, next_ref)):
        held[pl.ds(k * tiles, tiles)] = ref[pl.ds(0, tiles)]
    held[3 * tiles] = jnp.zeros((chan_local, block_cols), bf16)
    for d in list(range(groups // 2, groups)) + list(range(groups // 2)):
        group = jnp.bitwise_xor(place_ref[0], d)
        for s in range(per):
            rim_v[d, 2 * s] = held[entry_ref[0, group * per + s]]
            rim_v[d, 2 * s + 1] = held[entry_ref[1, group * per + s]]
        rim_v[d, 2 * per] = cols[group * (16 * per) // block_cols]
        stores.append(pltpu.make_async_copy(rim_v.at[d], rims[d], sems.at[d]))
        stores[-1].start()
    for store in stores:
        store.wait()


def rim_places(neighbours, first_slot, block_rows):
    slot_count = neighbours.shape[0]
    tiles = 2 * slot_count + 1
    valid = neighbours >= 0
    slot = jnp.clip(neighbours - first_slot, 0, 3 * slot_count - 1)
    tile_of = slot // slot_count
    place = tile_of * tiles + 2 * (slot - tile_of * slot_count)
    entries = jnp.stack(
        [
            jnp.where(valid[:, 2], place[:, 2] + 1, 3 * tiles),
            jnp.where(valid[:, 3], place[:, 3], 3 * tiles),
        ]
    )
    base = jnp.where(valid, 2 * block_rows * slot, -4 * block_rows)
    last = 2 * (block_rows - 1)
    west = [base[:, 4] + last] + [base[:, 0] + 2 * r for r in range(block_rows)] + [base[:, 6]]
    east = [base[:, 5] + last] + [base[:, 1] + 2 * r for r in range(block_rows)] + [base[:, 7]]
    none = [jnp.full((slot_count,), -1, jnp.int32)] * (8 - block_rows - 2)
    at = jnp.stack(west + none + [e + 1 for e in east] + none, axis=1)
    return entries, at.reshape(1, slot_count * 16)


def rims_of(place, entries, chosen, strips_prev, strips, strips_next, groups):
    count, chan_local, block_cols = strips.shape
    slot_count = entries.shape[1]
    per = slot_count // groups
    tiles = 2 * slot_count + 1
    rim = (2 * per + 1, chan_local, block_cols)
    *rims, up, down = pl.pallas_call(
        rim_kernel,
        out_shape=(shape(rim),) * groups
        + (shape((count - tiles, chan_local, block_cols)),) * 2,
        in_specs=[SMEM, SMEM, VMEM, VMEM, VMEM, VMEM],
        out_specs=(pl.BlockSpec(memory_space=pltpu.HBM),) * (groups + 2),
        scratch_shapes=[
            pltpu.VMEM((3 * tiles + 1, chan_local, block_cols), bf16),
            pltpu.VMEM((chosen.shape[1] // block_cols, chan_local, block_cols), bf16),
            pltpu.VMEM((groups,) + rim, bf16),
            pltpu.SemaphoreType.DMA((groups + 2,)),
        ],
        compiler_params=params(),
        name="rims",
    )(place, entries, chosen, strips_prev, strips, strips_next)
    return rims, up, down


def block_kernel(groups, place_ref, *refs):
    body_ref, refs = refs[0], refs[1:]
    rims, refs = refs[:groups], refs[groups:]
    conv_ref, in_ref, out_ref, col_ref, hid_col_ref = refs[:5]
    updates, scratch = refs[5 : 5 + groups], refs[5 + groups :]
    _, per, block_rows, chan_local, block_cols = body_ref.shape
    channels = groups * chan_local
    hidden = in_ref.shape[0]
    me = place_ref[0]
    lane = lax.broadcasted_iota(jnp.int32, (chan_local, block_cols), 1)
    bias = col_ref[:, 0:1]
    gain = col_ref[:, 1:2]
    base = (me * (16 * per)) % block_cols
    rows = [
        pl.multiple_of(jnp.bitwise_xor(me, d) * chan_local, chan_local) for d in range(groups)
    ]
    rim_v, side_v = scratch[6:]
    for d in range(groups):
        source = jnp.bitwise_xor(me, d)
        rim_v[source] = rims[d][...]
        side_v[source] = pltpu.roll(rims[d][2 * per].astype(f32), block_cols - base, 1)
    for s in range(per):
        taken, hid, upd_v = scratch[3 * (s % 2) : 3 * (s % 2) + 3]
        for d in range(groups):
            for p in range(block_rows + 2):
                if p == 0:
                    mid = rim_v[d, 2 * s]
                elif p == block_rows + 1:
                    mid = rim_v[d, 2 * s + 1]
                else:
                    mid = body_ref[d, s, p - 1]
                wide = mid.astype(f32)
                spot = 16 * s + p
                left = jnp.where(
                    lane == 0,
                    pltpu.roll(side_v[d], (block_cols - spot) % block_cols, 1),
                    pltpu.roll(wide, 1, 1),
                ).astype(bf16)
                right = jnp.where(
                    lane == block_cols - 1,
                    pltpu.roll(side_v[d], (2 * block_cols - 1 - spot - 8) % block_cols, 1),
                    pltpu.roll(wide, block_cols - 1, 1),
                ).astype(bf16)
                for a in range(3):
                    i = p - a
                    if 0 <= i < block_rows:
                        for b, piece in enumerate((left, mid, right)):
                            taken[
                                3 * a + b,
                                pl.ds(d * chan_local, chan_local),
                                pl.ds(i * block_cols, block_cols),
                            ] = piece
        columns = taken[...].reshape(9 * channels, block_rows * block_cols)
        conv = ein(conv_ref[...], columns, ((1,), (0,))) + bias
        squares = jnp.sum(conv * conv, axis=0, keepdims=True)
        normed = (conv * lax.rsqrt(squares / channels + norm_eps) * gain).astype(bf16)
        step = min(hidden, 256)
        for h in range(0, hidden, step):
            pre = ein(in_ref[pl.ds(h, step), :], normed, ((1,), (0,)))
            pre = pre + hid_col_ref[pl.ds(h, step), 2:3]
            act = pre * (0.5 * lax.erf(pre * (0.5**0.5)) + 0.5)
            hid[pl.ds(h, step), :] = act.astype(bf16)
        upd_v[...] = ein(out_ref[...], hid[...], ((1,), (0,))).astype(bf16)
        for d in range(groups):
            for i in range(block_rows):
                updates[d][s, i] = upd_v[
                    pl.ds(rows[d], chan_local), pl.ds(i * block_cols, block_cols)
                ]


def block_step(place, bodies, rims, weights):
    groups, per, block_rows, chan_local, block_cols = bodies.shape
    channels = groups * chan_local
    hidden = weights[1].shape[0]
    cells = per * block_rows * block_cols
    return pl.pallas_call(
        functools.partial(block_kernel, groups),
        out_shape=(shape(bodies.shape[1:]),) * groups,
        in_specs=[SMEM] + [VMEM] * (groups + 6),
        out_specs=(VMEM,) * groups,
        scratch_shapes=[
            pltpu.VMEM((9, channels, block_rows * block_cols), bf16),
            pltpu.VMEM((hidden, block_rows * block_cols), bf16),
            pltpu.VMEM((channels, block_rows * block_cols), bf16),
        ]
        * 2
        + [
            pltpu.VMEM((groups,) + rims[0].shape, bf16),
            pltpu.VMEM((groups, chan_local, block_cols), f32),
        ],
        compiler_params=params(24),
        cost_estimate=pl.CostEstimate(
            flops=2 * cells * (9 * channels * channels + 2 * channels * hidden),
            bytes_accessed=8 * 1024 * 1024,
            transcendentals=0,
        ),
        name="block_step",
    )(place, bodies, *rims, *weights)


def forcing_kernel(row_ref, side_ref, *refs):
    *pieces, out_ref, wide, even, odd = refs
    slot_count, block_rows, chan_local, block_cols = out_ref.shape
    lanes = wide.shape[1]
    at = 0
    for piece in pieces:
        wide[pl.ds(at, piece.shape[0]), :] = piece[...].astype(f32)
        at += piece.shape[0]
    row_at = lax.broadcasted_iota(jnp.int32, (lanes, lanes), 0)
    col_at = lax.broadcasted_iota(jnp.int32, (lanes, lanes), 1)
    eye = (row_at == col_at).astype(f32).astype(bf16)
    count = slot_count * block_rows
    batch = even.shape[0] // block_cols

    def fetch(q, got):
        for j in range(batch):
            for k in range(block_cols):
                got[pl.ds(j * block_cols + k, 1), :] = wide[pl.ds(row_ref[q + j, k], 1), :]

    def emit(q, got):
        across = ein(eye, got[...].astype(bf16), ((1,), (1,)))
        for j in range(batch):
            mine = across[:, j * block_cols : (j + 1) * block_cols]
            side = side_ref[pl.ds(q + j, 1), :]
            total = mine[:chan_local]
            for k in range(1, lanes // chan_local):
                total = jnp.where(side == k, mine[k * chan_local : (k + 1) * chan_local], total)
            out_ref[q // block_rows, j] = total.astype(bf16)

    fetch(0, even)

    def two(n, _):
        q = 2 * batch * n
        fetch(q + batch, odd)
        emit(q, even)
        fetch(jnp.minimum(q + 2 * batch, count - batch), even)
        emit(q + batch, odd)
        return 0

    lax.fori_loop(0, count // (2 * batch), two, 0)


def gather_flux(flux, below, above):
    count = lax.axis_size("tile")
    me = lax.axis_index("tile")
    if count == 4:
        two = lax.ppermute(flux, "tile", [(i, i ^ 2) for i in range(count)])
        three = lax.ppermute(flux, "tile", [(0, 3), (3, 0)])
        pieces = [piece.reshape(-1, 128) for piece in (flux, below, above, two, three)]

        def piece_of(tile):
            far = jnp.abs(tile - me)
            return jnp.where(far > 1, far + 1, jnp.where(tile > me, 2, far))

        return pieces, piece_of
    whole = lax.all_gather(flux, "tile", axis=0)
    return [whole.reshape(-1, 128)], lambda tile: tile


def forcing_of(pieces, piece_of, remap, rows_local, chan_local):
    slot_count, block_rows, block_cols = remap.shape
    side_by = 128 // chan_local
    part = rows_local // side_by
    target = jnp.clip(remap, 0, lax.axis_size("tile") * rows_local - 1).reshape(-1, block_cols)
    tile_of = target // rows_local
    within = target - tile_of * rows_local
    side = within // part
    row = piece_of(tile_of) * part + within - side * part
    lines = sum(piece.shape[0] for piece in pieces)
    return pl.pallas_call(
        forcing_kernel,
        out_shape=shape((slot_count, block_rows, chan_local, block_cols)),
        in_specs=[SMEM, VMEM] + [VMEM] * len(pieces),
        out_specs=VMEM,
        scratch_shapes=[pltpu.VMEM((lines, 128), f32)]
        + [pltpu.VMEM((block_rows * block_cols, 128), f32)] * 2,
        compiler_params=params(),
        cost_estimate=pl.CostEstimate(
            flops=0, bytes_accessed=32 * 1024 * 1024, transcendentals=0
        ),
        name="forcing",
    )(row, side, *pieces)


def final_kernel(groups, place_ref, *refs):
    xt_ref, updates, rest = refs[0], refs[1 : 1 + groups], refs[1 + groups :]
    forcing_ref, mask_ref, scale_ref, out_ref, piece_v, upd_v, forcing_v, out_v, sems = rest
    per = piece_v.shape[1]
    loads = []
    for d in range(groups):
        first = jnp.bitwise_xor(place_ref[0], d) * per
        loads.append(
            [
                pltpu.make_async_copy(
                    xt_ref.at[pl.ds(first, per)], piece_v.at[d], sems.at[0, d]
                ),
                pltpu.make_async_copy(updates[d], upd_v.at[d], sems.at[1, d]),
                pltpu.make_async_copy(
                    forcing_ref.at[pl.ds(first, per)], forcing_v.at[d], sems.at[2, d]
                ),
            ]
        )
        for load in loads[d]:
            load.start()
    scale = scale_ref[...]
    stores = []
    for d in range(groups):
        first = jnp.bitwise_xor(place_ref[0], d) * per
        for load in loads[d]:
            load.wait()
        for s in range(per):
            total = piece_v[d, s].astype(f32) + scale[None] * upd_v[d, s].astype(f32)
            total = total + forcing_v[d, s].astype(f32)
            total = mask_ref[first + s].astype(f32)[:, None, :] * total
            out_v[d, :, s] = jnp.swapaxes(total, 0, 1).astype(bf16)
        stores.append(
            pltpu.make_async_copy(out_v.at[d], out_ref.at[:, pl.ds(first, per)], sems.at[3, d])
        )
        stores[d].start()
    for store in stores:
        store.wait()


def final_step(place, xt, updates, forcing, cell_mask, layer_scale):
    slot_count, block_rows, chan_local, block_cols = forcing.shape
    groups = len(updates)
    per = slot_count // groups
    return pl.pallas_call(
        functools.partial(final_kernel, groups),
        out_shape=shape((chan_local, slot_count, block_rows, block_cols)),
        in_specs=[SMEM] + [ANY] * (groups + 2) + [VMEM, VMEM],
        out_specs=ANY,
        scratch_shapes=[pltpu.VMEM((groups,) + updates[0].shape, bf16)] * 3
        + [
            pltpu.VMEM((groups, chan_local, per, block_rows, block_cols), bf16),
            pltpu.SemaphoreType.DMA((4, groups)),
        ],
        compiler_params=params(),
        name="final_step",
    )(place, xt, *updates, forcing, cell_mask, layer_scale.astype(f32)[:, None])


def on_device(
    ocean_state,
    atmos,
    flux_weight,
    conv_weight,
    conv_bias,
    norm_gain,
    in_weight,
    in_bias,
    out_weight,
    layer_scale,
    cell_mask,
    neighbours,
    remap,
):
    chan_local, slot_count, block_rows, block_cols = ocean_state.shape
    groups = lax.axis_size(GROUP)
    tile_count = lax.axis_size("tile")
    hid_local = in_weight.shape[1]
    place = lax.axis_index(GROUP)[None]
    first_slot = (lax.axis_index("tile") - 1) * slot_count

    xt, strips, packed, part, flux = start_step(
        ocean_state,
        conv_weight,
        conv_bias,
        norm_gain,
        in_weight,
        in_bias,
        out_weight,
        atmos,
        flux_weight,
    )
    up = [(i, i + 1) for i in range(tile_count - 1)]
    strips_prev = lax.ppermute(strips, "tile", up)
    strips_next = lax.ppermute(strips, "tile", [(b, a) for a, b in up])
    entries, at = rim_places(neighbours, first_slot, block_rows)
    chosen = onehot_of(at, 3 * block_cols)
    picked, below, above = rims_of(
        place, entries, chosen, strips_prev, strips, strips_next, groups
    )
    if lax.axis_size("ens") == 2 and lax.axis_size("chan") == 2:
        near = swap(part, "chan")
        (xt,) = gate([xt], near, 60)
        (far,) = gate([swap(near, "ens")], picked[0])
        parts = [packed, swap(packed, "sec"), near, far, swap(near, "sec"), swap(far, "sec")]
        starts = weight_places()
    else:
        parts = [lax.all_gather(packed, GROUP, axis=0, tiled=True)]
        starts = jnp.zeros((1,), jnp.int32)
    bodies = lax.all_to_all(
        xt.reshape((groups, slot_count // groups) + xt.shape[1:]), GROUP, 0, 0, tiled=True
    )
    rims = trade(picked)
    table, piece_of = gather_flux(flux, below, above)
    weights = unpack_weights(parts, starts, groups, chan_local, hid_local, bodies)
    updates = trade(block_step(place, bodies, rims, weights))
    forcing = forcing_of(table, piece_of, remap, atmos.shape[0], chan_local)
    return final_step(place, xt, updates, forcing, cell_mask, layer_scale)


def solution(mesh):
    placed = (
        P(("chan", "sec"), ("ens", "tile"), None, None),
        P(("ens", "tile"), None),
        P(None, ("chan", "sec")),
        P(None, None, ("chan", "sec")),
        P(("chan", "sec")),
        P(("chan", "sec")),
        P(None, ("chan", "sec")),
        P(("chan", "sec")),
        P(("chan", "sec"), None),
        P(("chan", "sec")),
        P("tile", None, None),
        P("tile", None),
        P("tile", None, None),
    )
    return jax.shard_map(
        on_device,
        mesh=mesh,
        in_specs=placed,
        out_specs=P(("chan", "sec"), ("ens", "tile"), None, None),
        check_vma=False,
    )
```

```python
import functools

import jax
import jax.numpy as jnp
from jax import lax
from jax.experimental import pallas as pl
from jax.experimental.pallas import tpu as pltpu
from jax.sharding import PartitionSpec as P

norm_eps = 1e-06
bf16 = jnp.bfloat16
f32 = jnp.float32
GROUP = ("chan", "sec")
BIAS_ROWS = 32
VMEM = pl.BlockSpec(memory_space=pltpu.VMEM)
SMEM = pl.BlockSpec(memory_space=pltpu.SMEM)
ANY = pl.BlockSpec(memory_space=pl.ANY)


def shape(dims, dtype=bf16):
    return jax.ShapeDtypeStruct(dims, dtype)


def params(mib=20):
    return pltpu.CompilerParams(vmem_limit_bytes=mib * 1024 * 1024)


def ein(a, b, dims):
    return lax.dot_general(a, b, (dims, ((), ())), preferred_element_type=f32)


def start_kernel(*refs):
    state_ref, conv_ref, bias_ref, gain_ref, in_ref, in_bias_ref, out_ref, atmos_ref, flux_ref = (
        refs[:9]
    )
    xt_ref, strips_ref, pack_ref, part_ref, own_ref = refs[9:14]
    state_v, conv_v, in_v, out_v, atmos_v, half_v, strips_v, pack_v, sems = refs[14:]
    chunks, chan_local, span, block_rows, block_cols = state_v.shape
    taps, _, channels = conv_v.shape
    hid_local = out_v.shape[0]
    loads = [
        pltpu.make_async_copy(
            state_ref.at[:, pl.ds(c * span, span)], state_v.at[c], sems.at[c]
        )
        for c in range(chunks)
    ]
    copies = [
        pltpu.make_async_copy(conv_ref, conv_v, sems.at[chunks]),
        pltpu.make_async_copy(in_ref, in_v, sems.at[chunks + 1]),
        pltpu.make_async_copy(out_ref, out_v, sems.at[chunks + 2]),
    ]
    air = pltpu.make_async_copy(atmos_ref, atmos_v, sems.at[chunks + 3])
    for copy in loads + [air] + copies:
        copy.start()
    stores = []

    def store(source, target):
        stores.append(pltpu.make_async_copy(source, target, sems.at[chunks + 4 + len(stores)]))
        stores[-1].start()

    lane = lax.broadcasted_iota(jnp.int32, (chan_local, block_cols), 1)
    ends = jnp.zeros((chan_local, block_cols), f32)
    for c in range(chunks):
        loads[c].wait()
        for k in range(span):
            rows = jnp.swapaxes(state_v[c, :, k].astype(f32), 0, 1)
            packed = rows.astype(bf16)
            half_v[c, k] = packed
            slot = c * span + k
            strips_v[2 * slot] = packed[0]
            strips_v[2 * slot + 1] = packed[block_rows - 1]
            for r in range(block_rows):
                spot = 2 * (block_rows * slot + r)
                turned = pltpu.roll(rows[r], spot + 1, 1)
                ends = jnp.where((lane == spot) | (lane == spot + 1), turned, ends)
        store(half_v.at[c], xt_ref.at[pl.ds(c * span, span)])
    tiles = 2 * chunks * span + 1
    strips_v[tiles - 1] = ends.astype(bf16)
    air.wait()
    weight = flux_ref[...]
    side_by = block_cols // chan_local
    lines = atmos_v.shape[0] // side_by
    total = jnp.zeros((lines, block_cols), f32)
    for k in range(side_by):
        wide = [weight if j == k else jnp.zeros_like(weight) for j in range(side_by)]
        wide = jnp.concatenate(wide, axis=0)
        total = total + ein(atmos_v[pl.ds(k * lines, lines), :], wide, ((1,), (1,)))
    total = total.astype(bf16).reshape(lines // chan_local, chan_local, block_cols)
    strips_v[pl.ds(tiles, lines // chan_local)] = total
    store(strips_v, strips_ref)
    store(strips_v.at[pl.ds(tiles, lines // chan_local)], own_ref)

    def widen(ref):
        rows = ref[...].astype(f32)
        row = jnp.concatenate([rows[k : k + 1] for k in range(rows.shape[0])], axis=1)
        if row.shape[1] == channels:
            return row
        return jnp.concatenate([row, jnp.zeros((1, channels - row.shape[1]), f32)], axis=1)

    rest = jnp.zeros((BIAS_ROWS - 3, channels), f32)
    biases = jnp.concatenate(
        [widen(bias_ref), widen(gain_ref), widen(in_bias_ref), rest], axis=0
    )
    at = taps * chan_local
    for copy in copies:
        copy.wait()
    for t in range(taps):
        pack_v[pl.ds(t * chan_local, chan_local), :] = conv_v[t]
    pack_v[pl.ds(at, hid_local), :] = in_v[...].astype(f32).T.astype(bf16)
    pack_v[pl.ds(at + hid_local, hid_local), :] = out_v[...]
    pack_v[pl.ds(at + 2 * hid_local, BIAS_ROWS), :] = biases.astype(bf16)
    part = part_ref.shape[0]
    store(pack_v, pack_ref)
    store(pack_v.at[pl.ds(pl.multiple_of(lax.axis_index("ens") * part, 16), part)], part_ref)
    for copy in stores:
        copy.wait()


def start_step(
    state, conv_weight, conv_bias, norm_gain, in_weight, in_bias, out_weight, atmos, flux_weight
):
    chan_local, slot_count, block_rows, block_cols = state.shape
    chunks = 4
    span = slot_count // chunks
    taps, channels, _ = conv_weight.shape
    hid_local = out_weight.shape[0]
    rows = taps * chan_local + 2 * hid_local + BIAS_ROWS
    half = (span, block_rows, chan_local, block_cols)
    lines = atmos.shape[0] * chan_local // block_cols
    strips = (2 * slot_count + 1 + lines // chan_local, chan_local, block_cols)
    return pl.pallas_call(
        start_kernel,
        out_shape=(shape((slot_count,) + half[1:]),)
        + (
            shape(strips),
            shape((rows, channels)),
            shape((rows // 2, channels)),
            shape((lines // chan_local,) + strips[1:]),
        ),
        in_specs=[ANY, ANY, VMEM, VMEM, ANY, VMEM, ANY, ANY, VMEM],
        out_specs=(ANY,) * 5,
        scratch_shapes=[
            pltpu.VMEM((chunks, chan_local, span, block_rows, block_cols), bf16),
            pltpu.VMEM((taps, chan_local, channels), bf16),
            pltpu.VMEM((channels, hid_local), bf16),
            pltpu.VMEM((hid_local, channels), bf16),
            pltpu.VMEM(atmos.shape, bf16),
            pltpu.VMEM((chunks,) + half, bf16),
            pltpu.VMEM(strips, bf16),
            pltpu.VMEM((rows, channels), bf16),
            pltpu.SemaphoreType.DMA((2 * chunks + 8,)),
        ],
        compiler_params=params(60),
        name="start_step",
    )(
        state,
        conv_weight.transpose(0, 2, 1),
        conv_bias.reshape(-1, min(128, chan_local)),
        norm_gain.reshape(-1, min(128, chan_local)),
        in_weight,
        in_bias.reshape(-1, min(128, hid_local)),
        out_weight,
        atmos,
        flux_weight.T,
    )


def send(piece, d, count):
    return lax.ppermute(piece, GROUP, [(i, i ^ d) for i in range(count)])


def trade(pieces):
    count = len(pieces)
    got = list(pieces)
    for d in list(range(count // 2, count)) + list(range(1, count // 2)):
        got[d] = send(pieces[d], d, count)
    return got


def unpack_kernel(count, chan_local, hid_local, starts_ref, *refs):
    pieces = refs[:count]
    *_, conv_ref, in_ref, out_ref, col_ref, hid_col_ref, all_ref = refs
    groups, rows, channels = all_ref.shape
    unit = min(rows, *(piece.shape[0] for piece in pieces))
    for n, piece in enumerate(pieces):
        for k in range(piece.shape[0] // unit):
            at = starts_ref[n] + k
            parts = rows // unit
            start = pl.multiple_of((at % parts) * unit, 16)
            all_ref[at // parts, pl.ds(start, unit), :] = piece[pl.ds(k * unit, unit), :]
    at = 9 * chan_local
    for j in range(groups):
        for t in range(9):
            conv_ref[pl.ds(j * chan_local, chan_local), pl.ds(t * channels, channels)] = all_ref[
                j, pl.ds(t * chan_local, chan_local), :
            ]
        in_ref[pl.ds(j * hid_local, hid_local), :] = all_ref[j, pl.ds(at, hid_local), :]
        biases = all_ref[j, pl.ds(at + 2 * hid_local, BIAS_ROWS), :].astype(f32)
        across = biases.T
        col_ref[pl.ds(j * chan_local, chan_local), :] = across[:chan_local]
        hid_col_ref[pl.ds(j * hid_local, hid_local), :] = across[:hid_local]
    outs = jnp.concatenate(
        [all_ref[j, pl.ds(at + hid_local, hid_local), :] for j in range(groups)], axis=0
    )
    out_ref[...] = outs.astype(f32).T.astype(bf16)


def unpack_weights(pieces, starts, groups, chan_local, hid_local, after):
    rows = sum(piece.shape[0] for piece in pieces) // groups
    channels = groups * chan_local
    hidden = groups * hid_local
    return pl.pallas_call(
        functools.partial(unpack_kernel, len(pieces), chan_local, hid_local),
        out_shape=(
            shape((channels, 9 * channels)),
            shape((hidden, channels)),
            shape((channels, hidden)),
            shape((channels, BIAS_ROWS), f32),
            shape((hidden, BIAS_ROWS), f32),
        ),
        in_specs=[SMEM] + [VMEM] * len(pieces) + [ANY],
        out_specs=(VMEM,) * 5,
        scratch_shapes=[pltpu.VMEM((groups, rows, channels), bf16)],
        compiler_params=params(),
        name="unpack_weights",
    )(starts, *pieces, after)


def swap(value, axis):
    return lax.ppermute(value, axis, [(0, 1), (1, 0)])


def gate_kernel(*refs):
    pass


def gate(values, after, mib=20):
    count = len(values)
    return pl.pallas_call(
        gate_kernel,
        out_shape=tuple(shape(value.shape) for value in values),
        in_specs=[ANY] * (count + 1),
        out_specs=(ANY,) * count,
        input_output_aliases={k: k for k in range(count)},
        compiler_params=params(mib),
        name="gate",
    )(*values, after)


def weight_places():
    ens, chan, sec = (lax.axis_index(name) for name in ("ens", "chan", "sec"))
    own = 2 * (2 * chan + sec)
    beside = 2 * (2 * chan + 1 - sec)
    across = 2 * (2 * (1 - chan) + sec)
    corner = 2 * (2 * (1 - chan) + 1 - sec)
    return jnp.stack([own, beside, across + ens, across + 1 - ens, corner + ens, corner + 1 - ens])


def onehot_kernel(at_ref, out_ref):
    spot = lax.broadcasted_iota(jnp.int32, out_ref.shape, 0)
    out_ref[...] = (spot == at_ref[...]).astype(f32).astype(bf16)


def onehot_of(at, rows):
    return pl.pallas_call(
        onehot_kernel,
        out_shape=shape((rows, at.shape[1])),
        in_specs=[VMEM],
        out_specs=VMEM,
        compiler_params=params(),
        name="onehot",
    )(at)


def rim_kernel(place_ref, entry_ref, chosen_ref, prev_ref, own_ref, next_ref, *refs):
    *rims, up_ref, down_ref, held, cols, rim_v, sems = refs
    groups, rows, chan_local, block_cols = rim_v.shape
    per = (rows - 1) // 2
    tiles = 2 * per * groups + 1
    flux = pl.ds(tiles, up_ref.shape[0])
    stores = [
        pltpu.make_async_copy(prev_ref.at[flux], up_ref, sems.at[groups]),
        pltpu.make_async_copy(next_ref.at[flux], down_ref, sems.at[groups + 1]),
    ]
    for store in stores:
        store.start()
    ends = jnp.concatenate(
        [prev_ref[tiles - 1], own_ref[tiles - 1], next_ref[tiles - 1]], axis=1
    )
    picked = ein(ends, chosen_ref[...], ((1,), (0,))).astype(bf16)
    for k in range(cols.shape[0]):
        cols[k] = picked[:, k * block_cols : (k + 1) * block_cols]
    for k, ref in enumerate((prev_ref, own_ref, next_ref)):
        held[pl.ds(k * tiles, tiles)] = ref[pl.ds(0, tiles)]
    held[3 * tiles] = jnp.zeros((chan_local, block_cols), bf16)
    for d in list(range(groups // 2, groups)) + list(range(groups // 2)):
        group = jnp.bitwise_xor(place_ref[0], d)
        for s in range(per):
            rim_v[d, 2 * s] = held[entry_ref[0, group * per + s]]
            rim_v[d, 2 * s + 1] = held[entry_ref[1, group * per + s]]
        rim_v[d, 2 * per] = cols[group * (16 * per) // block_cols]
        stores.append(pltpu.make_async_copy(rim_v.at[d], rims[d], sems.at[d]))
        stores[-1].start()
    for store in stores:
        store.wait()


def rim_places(neighbours, first_slot, block_rows):
    slot_count = neighbours.shape[0]
    tiles = 2 * slot_count + 1
    valid = neighbours >= 0
    slot = jnp.clip(neighbours - first_slot, 0, 3 * slot_count - 1)
    tile_of = slot // slot_count
    place = tile_of * tiles + 2 * (slot - tile_of * slot_count)
    entries = jnp.stack(
        [
            jnp.where(valid[:, 2], place[:, 2] + 1, 3 * tiles),
            jnp.where(valid[:, 3], place[:, 3], 3 * tiles),
        ]
    )
    base = jnp.where(valid, 2 * block_rows * slot, -4 * block_rows)
    last = 2 * (block_rows - 1)
    west = [base[:, 4] + last] + [base[:, 0] + 2 * r for r in range(block_rows)] + [base[:, 6]]
    east = [base[:, 5] + last] + [base[:, 1] + 2 * r for r in range(block_rows)] + [base[:, 7]]
    none = [jnp.full((slot_count,), -1, jnp.int32)] * (8 - block_rows - 2)
    at = jnp.stack(west + none + [e + 1 for e in east] + none, axis=1)
    return entries, at.reshape(1, slot_count * 16)


def rims_of(place, entries, chosen, strips_prev, strips, strips_next, groups):
    count, chan_local, block_cols = strips.shape
    slot_count = entries.shape[1]
    per = slot_count // groups
    tiles = 2 * slot_count + 1
    rim = (2 * per + 1, chan_local, block_cols)
    *rims, up, down = pl.pallas_call(
        rim_kernel,
        out_shape=(shape(rim),) * groups
        + (shape((count - tiles, chan_local, block_cols)),) * 2,
        in_specs=[SMEM, SMEM, VMEM, VMEM, VMEM, VMEM],
        out_specs=(pl.BlockSpec(memory_space=pltpu.HBM),) * (groups + 2),
        scratch_shapes=[
            pltpu.VMEM((3 * tiles + 1, chan_local, block_cols), bf16),
            pltpu.VMEM((chosen.shape[1] // block_cols, chan_local, block_cols), bf16),
            pltpu.VMEM((groups,) + rim, bf16),
            pltpu.SemaphoreType.DMA((groups + 2,)),
        ],
        compiler_params=params(60),
        name="rims",
    )(place, entries, chosen, strips_prev, strips, strips_next)
    return rims, up, down


def block_kernel(groups, place_ref, *refs):
    body_ref, refs = refs[0], refs[1:]
    rims, refs = refs[:groups], refs[groups:]
    conv_ref, in_ref, out_ref, col_ref, hid_col_ref = refs[:5]
    updates, scratch = refs[5 : 5 + groups], refs[5 + groups :]
    _, per, block_rows, chan_local, block_cols = body_ref.shape
    channels = groups * chan_local
    hidden = in_ref.shape[0]
    me = place_ref[0]
    lane = lax.broadcasted_iota(jnp.int32, (chan_local, block_cols), 1)
    bias = col_ref[:, 0:1]
    gain = col_ref[:, 1:2]
    base = (me * (16 * per)) % block_cols
    rows = [
        pl.multiple_of(jnp.bitwise_xor(me, d) * chan_local, chan_local) for d in range(groups)
    ]
    rim_v, side_v = scratch[6:]
    for d in range(groups):
        source = jnp.bitwise_xor(me, d)
        rim_v[source] = rims[d][...]
        side_v[source] = pltpu.roll(rims[d][2 * per].astype(f32), block_cols - base, 1)
    for s in range(per):
        taken, hid, upd_v = scratch[3 * (s % 2) : 3 * (s % 2) + 3]
        for d in range(groups):
            for p in range(block_rows + 2):
                if p == 0:
                    mid = rim_v[d, 2 * s]
                elif p == block_rows + 1:
                    mid = rim_v[d, 2 * s + 1]
                else:
                    mid = body_ref[d, s, p - 1]
                wide = mid.astype(f32)
                spot = 16 * s + p
                left = jnp.where(
                    lane == 0,
                    pltpu.roll(side_v[d], (block_cols - spot) % block_cols, 1),
                    pltpu.roll(wide, 1, 1),
                ).astype(bf16)
                right = jnp.where(
                    lane == block_cols - 1,
                    pltpu.roll(side_v[d], (2 * block_cols - 1 - spot - 8) % block_cols, 1),
                    pltpu.roll(wide, block_cols - 1, 1),
                ).astype(bf16)
                for a in range(3):
                    i = p - a
                    if 0 <= i < block_rows:
                        for b, piece in enumerate((left, mid, right)):
                            taken[
                                3 * a + b,
                                pl.ds(d * chan_local, chan_local),
                                pl.ds(i * block_cols, block_cols),
                            ] = piece
        columns = taken[...].reshape(9 * channels, block_rows * block_cols)
        conv = ein(conv_ref[...], columns, ((1,), (0,))) + bias
        squares = jnp.sum(conv * conv, axis=0, keepdims=True)
        normed = (conv * lax.rsqrt(squares / channels + norm_eps) * gain).astype(bf16)
        step = min(hidden, 256)
        for h in range(0, hidden, step):
            pre = ein(in_ref[pl.ds(h, step), :], normed, ((1,), (0,)))
            pre = pre + hid_col_ref[pl.ds(h, step), 2:3]
            act = pre * (0.5 * lax.erf(pre * (0.5**0.5)) + 0.5)
            hid[pl.ds(h, step), :] = act.astype(bf16)
        upd_v[...] = ein(out_ref[...], hid[...], ((1,), (0,))).astype(bf16)
        for d in range(groups):
            for i in range(block_rows):
                updates[d][s, i] = upd_v[
                    pl.ds(rows[d], chan_local), pl.ds(i * block_cols, block_cols)
                ]


def block_step(place, bodies, rims, weights):
    groups, per, block_rows, chan_local, block_cols = bodies.shape
    channels = groups * chan_local
    hidden = weights[1].shape[0]
    cells = per * block_rows * block_cols
    return pl.pallas_call(
        functools.partial(block_kernel, groups),
        out_shape=(shape(bodies.shape[1:]),) * groups,
        in_specs=[SMEM] + [VMEM] * (groups + 6),
        out_specs=(VMEM,) * groups,
        scratch_shapes=[
            pltpu.VMEM((9, channels, block_rows * block_cols), bf16),
            pltpu.VMEM((hidden, block_rows * block_cols), bf16),
            pltpu.VMEM((channels, block_rows * block_cols), bf16),
        ]
        * 2
        + [
            pltpu.VMEM((groups,) + rims[0].shape, bf16),
            pltpu.VMEM((groups, chan_local, block_cols), f32),
        ],
        compiler_params=params(24),
        cost_estimate=pl.CostEstimate(
            flops=2 * cells * (9 * channels * channels + 2 * channels * hidden),
            bytes_accessed=8 * 1024 * 1024,
            transcendentals=0,
        ),
        name="block_step",
    )(place, bodies, *rims, *weights)


def forcing_kernel(row_ref, side_ref, *refs):
    *pieces, out_ref, wide, even, odd = refs
    slot_count, block_rows, chan_local, block_cols = out_ref.shape
    lanes = wide.shape[1]
    at = 0
    for piece in pieces:
        wide[pl.ds(at, piece.shape[0]), :] = piece[...].astype(f32)
        at += piece.shape[0]
    row_at = lax.broadcasted_iota(jnp.int32, (lanes, lanes), 0)
    col_at = lax.broadcasted_iota(jnp.int32, (lanes, lanes), 1)
    eye = (row_at == col_at).astype(f32).astype(bf16)
    count = slot_count * block_rows
    batch = even.shape[0] // block_cols

    def fetch(q, got):
        for j in range(batch):
            for k in range(block_cols):
                got[pl.ds(j * block_cols + k, 1), :] = wide[pl.ds(row_ref[q + j, k], 1), :]

    def emit(q, got):
        across = ein(eye, got[...].astype(bf16), ((1,), (1,)))
        for j in range(batch):
            mine = across[:, j * block_cols : (j + 1) * block_cols]
            side = side_ref[pl.ds(q + j, 1), :]
            total = mine[:chan_local]
            for k in range(1, lanes // chan_local):
                total = jnp.where(side == k, mine[k * chan_local : (k + 1) * chan_local], total)
            out_ref[q // block_rows, j] = total.astype(bf16)

    fetch(0, even)

    def two(n, _):
        q = 2 * batch * n
        fetch(q + batch, odd)
        emit(q, even)
        fetch(jnp.minimum(q + 2 * batch, count - batch), even)
        emit(q + batch, odd)
        return 0

    lax.fori_loop(0, count // (2 * batch), two, 0)


def gather_flux(flux, below, above):
    count = lax.axis_size("tile")
    me = lax.axis_index("tile")
    if count == 4:
        two = lax.ppermute(flux, "tile", [(i, i ^ 2) for i in range(count)])
        three = lax.ppermute(flux, "tile", [(0, 3), (3, 0)])
        pieces = [piece.reshape(-1, 128) for piece in (flux, below, above, two, three)]

        def piece_of(tile):
            far = jnp.abs(tile - me)
            return jnp.where(far > 1, far + 1, jnp.where(tile > me, 2, far))

        return pieces, piece_of
    whole = lax.all_gather(flux, "tile", axis=0)
    return [whole.reshape(-1, 128)], lambda tile: tile


def forcing_of(pieces, piece_of, remap, rows_local, chan_local):
    slot_count, block_rows, block_cols = remap.shape
    side_by = 128 // chan_local
    part = rows_local // side_by
    target = jnp.clip(remap, 0, lax.axis_size("tile") * rows_local - 1).reshape(-1, block_cols)
    tile_of = target // rows_local
    within = target - tile_of * rows_local
    side = within // part
    row = piece_of(tile_of) * part + within - side * part
    lines = sum(piece.shape[0] for piece in pieces)
    return pl.pallas_call(
        forcing_kernel,
        out_shape=shape((slot_count, block_rows, chan_local, block_cols)),
        in_specs=[SMEM, VMEM] + [VMEM] * len(pieces),
        out_specs=VMEM,
        scratch_shapes=[pltpu.VMEM((lines, 128), f32)]
        + [pltpu.VMEM((block_rows * block_cols, 128), f32)] * 2,
        compiler_params=params(),
        cost_estimate=pl.CostEstimate(
            flops=0, bytes_accessed=32 * 1024 * 1024, transcendentals=0
        ),
        name="forcing",
    )(row, side, *pieces)


def final_kernel(groups, place_ref, *refs):
    xt_ref, updates, rest = refs[0], refs[1 : 1 + groups], refs[1 + groups :]
    forcing_ref, mask_ref, scale_ref, out_ref, piece_v, upd_v, forcing_v, out_v, sems = rest
    per = piece_v.shape[1]
    loads = []
    for d in range(groups):
        first = jnp.bitwise_xor(place_ref[0], d) * per
        loads.append(
            [
                pltpu.make_async_copy(
                    xt_ref.at[pl.ds(first, per)], piece_v.at[d], sems.at[0, d]
                ),
                pltpu.make_async_copy(updates[d], upd_v.at[d], sems.at[1, d]),
                pltpu.make_async_copy(
                    forcing_ref.at[pl.ds(first, per)], forcing_v.at[d], sems.at[2, d]
                ),
            ]
        )
        for load in loads[d]:
            load.start()
    scale = scale_ref[...]
    stores = []
    for d in range(groups):
        first = jnp.bitwise_xor(place_ref[0], d) * per
        for load in loads[d]:
            load.wait()
        for s in range(per):
            total = piece_v[d, s].astype(f32) + scale[None] * upd_v[d, s].astype(f32)
            total = total + forcing_v[d, s].astype(f32)
            total = mask_ref[first + s].astype(f32)[:, None, :] * total
            out_v[d, :, s] = jnp.swapaxes(total, 0, 1).astype(bf16)
        stores.append(
            pltpu.make_async_copy(out_v.at[d], out_ref.at[:, pl.ds(first, per)], sems.at[3, d])
        )
        stores[d].start()
    for store in stores:
        store.wait()


def final_step(place, xt, updates, forcing, cell_mask, layer_scale):
    slot_count, block_rows, chan_local, block_cols = forcing.shape
    groups = len(updates)
    per = slot_count // groups
    return pl.pallas_call(
        functools.partial(final_kernel, groups),
        out_shape=shape((chan_local, slot_count, block_rows, block_cols)),
        in_specs=[SMEM] + [ANY] * (groups + 2) + [VMEM, VMEM],
        out_specs=ANY,
        scratch_shapes=[pltpu.VMEM((groups,) + updates[0].shape, bf16)] * 3
        + [
            pltpu.VMEM((groups, chan_local, per, block_rows, block_cols), bf16),
            pltpu.SemaphoreType.DMA((4, groups)),
        ],
        compiler_params=params(),
        name="final_step",
    )(place, xt, *updates, forcing, cell_mask, layer_scale.astype(f32)[:, None])


def on_device(
    ocean_state,
    atmos,
    flux_weight,
    conv_weight,
    conv_bias,
    norm_gain,
    in_weight,
    in_bias,
    out_weight,
    layer_scale,
    cell_mask,
    neighbours,
    remap,
):
    chan_local, slot_count, block_rows, block_cols = ocean_state.shape
    groups = lax.axis_size(GROUP)
    tile_count = lax.axis_size("tile")
    hid_local = in_weight.shape[1]
    place = lax.axis_index(GROUP)[None]
    first_slot = (lax.axis_index("tile") - 1) * slot_count

    xt, strips, packed, part, flux = start_step(
        ocean_state,
        conv_weight,
        conv_bias,
        norm_gain,
        in_weight,
        in_bias,
        out_weight,
        atmos,
        flux_weight,
    )
    up = [(i, i + 1) for i in range(tile_count - 1)]
    strips_prev = lax.ppermute(strips, "tile", up)
    strips_next = lax.ppermute(strips, "tile", [(b, a) for a, b in up])
    entries, at = rim_places(neighbours, first_slot, block_rows)
    chosen = onehot_of(at, 3 * block_cols)
    picked, below, above = rims_of(
        place, entries, chosen, strips_prev, strips, strips_next, groups
    )
    if lax.axis_size("ens") == 2 and lax.axis_size("chan") == 2:
        near = swap(part, "chan")
        (xt,) = gate([xt], near, 60)
        (far,) = gate([swap(near, "ens")], picked[0])
        parts = [packed, swap(packed, "sec"), near, far, swap(near, "sec"), swap(far, "sec")]
        starts = weight_places()
    else:
        parts = [lax.all_gather(packed, GROUP, axis=0, tiled=True)]
        starts = jnp.zeros((1,), jnp.int32)
    bodies = lax.all_to_all(
        xt.reshape((groups, slot_count // groups) + xt.shape[1:]), GROUP, 0, 0, tiled=True
    )
    rims = trade(picked)
    table, piece_of = gather_flux(flux, below, above)
    weights = unpack_weights(parts, starts, groups, chan_local, hid_local, bodies)
    updates = trade(block_step(place, bodies, rims, weights))
    forcing = forcing_of(table, piece_of, remap, atmos.shape[0], chan_local)
    return final_step(place, xt, updates, forcing, cell_mask, layer_scale)


def solution(mesh):
    placed = (
        P(("chan", "sec"), ("ens", "tile"), None, None),
        P(("ens", "tile"), None),
        P(None, ("chan", "sec")),
        P(None, None, ("chan", "sec")),
        P(("chan", "sec")),
        P(("chan", "sec")),
        P(None, ("chan", "sec")),
        P(("chan", "sec")),
        P(("chan", "sec"), None),
        P(("chan", "sec")),
        P("tile", None, None),
        P("tile", None),
        P("tile", None, None),
    )
    return jax.shard_map(
        on_device,
        mesh=mesh,
        in_specs=placed,
        out_specs=P(("chan", "sec"), ("ens", "tile"), None, None),
        check_vma=False,
    )
```
